32 devices in a mesh: fsdp: 8 (over y, x, core), head: 4 (over z).
Axes of the slice: x: 2, y: 2, z: 4, core: 2. Of those that a mesh axis runs over, the one named last changes fastest.
Arguments:
- images: bfloat16 [16, 577, 1024], P('fsdp'), may hold values from -6 to 6
- cotangent: bfloat16 [16, 577, 1024], P('fsdp'), may hold values from -6 to 6
- w_qkv: bfloat16 [2, 3, 1024, 1024], P(None, None, 'fsdp', 'head'), may hold values from -0.1875 to 0.1875
- w_out: bfloat16 [2, 1024, 1024], P(None, 'head', 'fsdp'), may hold values from -0.75 to 0.75
- w_in: bfloat16 [2, 1024, 4096], P(None, 'fsdp', 'head'), may hold values from -0.1875 to 0.1875
- w_down: bfloat16 [2, 4096, 1024], P(None, 'head', 'fsdp'), may hold values from -0.09375 to 0.09375
- qv_bias: bfloat16 [2, 2, 128, 8], P(None, None, 'head', 'fsdp'), may hold values from -3 to 3
- in_bias: bfloat16 [2, 512, 8], P(None, 'head', 'fsdp'), may hold values from -3 to 3
- gains: bfloat16 [2, 2, 1024], P(None, None, 'fsdp'), may hold values from 0.25 to 1.75
- shifts: bfloat16 [2, 4, 1024], P(None, None, 'fsdp'), may hold values from -2 to 2
Outputs:
- block_out: float32 [16, 577, 1024], P('fsdp')
- input_grad: float32 [16, 577, 1024], P('fsdp')
- grad_qkv: float32 [2, 3, 1024, 1024], P(None, None, 'fsdp', 'head')
- grad_out_proj: float32 [2, 1024, 1024], P(None, 'head', 'fsdp')
- grad_in_proj: float32 [2, 1024, 4096], P(None, 'fsdp', 'head')
- grad_down_proj: float32 [2, 4096, 1024], P(None, 'head', 'fsdp')
- grad_qv_bias: float32 [2, 2, 128, 8], P(None, None, 'head', 'fsdp')
- grad_in_bias: float32 [2, 512, 8], P(None, 'head', 'fsdp')
- grad_gains: float32 [2, 2, 1024], P(None, None, 'fsdp')
- grad_shifts: float32 [2, 4, 1024], P(None, None, 'fsdp')
The draws below stay inside these ranges and needn't reach their ends.
All inputs are finite; a program needn't handle non-finite values.
Results may differ from the reference program's by a relative error of at most 0.019.
Values may be sent and summed in bfloat16 or wider, within the bound.
A program may use at most 256 MiB of HBM per device.

```python
import jax
import jax.numpy as jnp
from jax import lax

D = 1024
HEADS = 16
HD = 64
FF = 4096
SEQ = 577
LAYERS = 2
IMAGES = 16
N_FSDP = 8


def block_scale(stream_key, dims, cuts, low, top_value):
    def one(dim, parts):
        draws = jax.random.uniform(jax.random.fold_in(jax.random.fold_in(stream_key, 6), dim), (parts,), jnp.float32, low / len(cuts), top_value / len(cuts))
        return jnp.repeat(jnp.exp(draws), dims[dim] // parts).reshape((-1,) + (1,) * (len(dims) - dim - 1))

    level = one(*cuts[0])
    for cut in cuts[1:]:
        level = level * one(*cut)
    return level


def normal_values(own_key, dims, spread, most, cuts=(), held_as=jnp.bfloat16):
    factor_of = block_scale(own_key, dims, cuts, -0.22, 0.18) if cuts else 1.0
    array = jax.random.normal(own_key, dims, jnp.float32) * spread * factor_of
    return jnp.minimum(jnp.maximum(array, -most), most).astype(held_as)


def setup_inputs(seed: int = 0) -> dict:
    key_list = jax.random.split(jax.random.key(seed), 11)
    images = normal_values(key_list[0], (IMAGES, SEQ, D), 1.0, 6.0, ((0, 8),))
    cotangent = normal_values(key_list[1], (IMAGES, SEQ, D), 1.0, 6.0, ((0, 8),))
    w_qkv = normal_values(key_list[2], (LAYERS, 3, D, D), D ** -0.5, 0.1875, ((2, 8), (3, 4)))
    w_out = normal_values(key_list[3], (LAYERS, D, D), (D // 16) ** -0.5, 0.75, ((1, 4), (2, 8)))
    w_in = normal_values(key_list[4], (LAYERS, D, FF), D ** -0.5, 0.1875, ((1, 8), (2, 4)))
    w_down = normal_values(key_list[5], (LAYERS, FF, D), FF ** -0.5, 0.09375, ((1, 4), (2, 8)))
    qv_bias = normal_values(key_list[6], (LAYERS, 2, D // N_FSDP, N_FSDP), 0.5, 3.0, ((2, 4), (3, 8)))
    in_bias = normal_values(key_list[7], (LAYERS, FF // N_FSDP, N_FSDP), 0.5, 3.0, ((1, 4), (2, 8)))
    gains = jnp.clip(1.0 + 0.15 * jax.random.normal(key_list[8], (LAYERS, 2, D), jnp.float32), 0.25, 1.75).astype(jnp.bfloat16)
    shifts = normal_values(key_list[9], (LAYERS, 4, D), 0.3, 2.0, ((2, 8),))
    return {"images": images, "cotangent": cotangent, "w_qkv": w_qkv, "w_out": w_out, "w_in": w_in, "w_down": w_down, "qv_bias": qv_bias, "in_bias": in_bias, "gains": gains, "shifts": shifts}


epsilon = 1e-06
highest = lax.Precision.HIGHEST

@jax.custom_vjp
def low(v):
    return lax.optimization_barrier(v.astype(jnp.bfloat16)).astype(jnp.float32)

@jax.custom_vjp
def low_back(v):
    return v

def low_keep(v):
    return (low(v), None)

def low_pass(kept, grad):
    return (grad,)

def back_keep(v):
    return (v, None)

def back_low(kept, grad):
    return (low(grad),)
low.defvjp(low_keep, low_pass)
low_back.defvjp(back_keep, back_low)

def layer_norm(stream, gain, shift):
    average = lax.optimization_barrier(jnp.mean(stream, axis=-1, keepdims=True))
    centred = stream - average
    variance = lax.optimization_barrier(jnp.mean(centred * centred, axis=-1, keepdims=True))
    return centred * lax.rsqrt(variance + epsilon) * gain + shift

def matmul(left, right):
    return jnp.dot(left, right, precision=highest)

def layer_slice(params, layer_index):
    w_qkv, w_out, w_in, w_down, qv_bias, in_bias, gains, shifts = params
    return (w_qkv[layer_index], w_out[layer_index], w_in[layer_index], w_down[layer_index], qv_bias[layer_index].reshape(2, D), in_bias[layer_index].reshape(FF), gains[layer_index], shifts[layer_index])

def one_layer(stream, weights):
    w_qkv, w_out, w_in, w_down, qv_bias, in_bias, gains, shifts = weights
    length = stream.shape[0]
    normed = low(layer_norm(stream, gains[0], shifts[0]))
    queries = low_back(low(matmul(normed, w_qkv[0]) + qv_bias[0])).reshape(length, HEADS, HD)
    key_rows = low_back(low(matmul(normed, w_qkv[1]))).reshape(length, HEADS, HD)
    value_rows = low_back(low(matmul(normed, w_qkv[2]) + qv_bias[1])).reshape(length, HEADS, HD)
    scores = low_back(jnp.einsum('qhd,khd->hqk', queries, key_rows, precision=highest) * HD ** (-0.5))
    soft = jax.nn.softmax(scores, axis=-1)
    attended = jnp.einsum('hqk,khd->qhd', low(soft), value_rows, precision=highest).reshape(length, D)
    attended = low_back(low(attended))
    stream = stream + low_back(matmul(attended, w_out)) + shifts[2]
    normed_second = low(layer_norm(stream, gains[1], shifts[1]))
    hidden = low_back(matmul(normed_second, w_in) + in_bias)
    active = low(jax.nn.gelu(hidden, approximate=False))
    return stream + low_back(matmul(active, w_down)) + shifts[3]

def forward(params, inputs):

    def per_image(carry, one_image):
        stream = one_image
        for layer_index in range(LAYERS):
            stream = one_layer(stream, layer_slice(params, layer_index))
        return (carry, stream)
    carry, results = lax.scan(jax.checkpoint(per_image), jnp.float32(0.0), inputs)
    return results

def reference(images, cotangent, w_qkv, w_out, w_in, w_down, qv_bias, in_bias, gains, shifts):
    params = (w_qkv.astype(jnp.float32), w_out.astype(jnp.float32), w_in.astype(jnp.float32), w_down.astype(jnp.float32), qv_bias.astype(jnp.float32), in_bias.astype(jnp.float32), gains.astype(jnp.float32), shifts.astype(jnp.float32))
    results, pullback = jax.vjp(forward, params, images.astype(jnp.float32))
    grad_params, grad_inputs = pullback(cotangent.astype(jnp.float32))
    return (results, grad_inputs, grad_params[0], grad_params[1], grad_params[2], grad_params[3], grad_params[4], grad_params[5], grad_params[6], grad_params[7])
```

```python
import functools

import jax
import jax.numpy as jnp
from jax import lax
from jax.sharding import PartitionSpec as P

HD = 64
LAYERS = 2
TP = 4
AXES = ("fsdp", "head")
epsilon = 1e-06


def product(left, right, form):
    return jnp.einsum(form, left, right, preferred_element_type=jnp.float32)


def low(v):
    return v.astype(jnp.bfloat16)


def wide(v):
    return v.astype(jnp.float32)


class Places:
    def __init__(self, fsdp, head):
        self.fsdp, self.head = fsdp, head
        self.blocks = fsdp // TP
        index, plane = lax.axis_index("fsdp"), lax.axis_index("head")
        self.block, self.role, self.plane = index // TP, index % TP, plane

    def pairs(self, move, sends=None):
        found = []
        for block in range(self.blocks):
            for role in range(TP):
                for plane in range(self.head):
                    if sends is not None and not sends(block, role, plane):
                        continue
                    to_block, to_role, to_plane = move(block, role, plane)
                    found.append(
                        (
                            (block * TP + role) * self.head + plane,
                            (to_block * TP + to_role) * self.head + to_plane,
                        )
                    )
        return found

    def role_xor(self, v, bits, sends=None):
        return lax.ppermute(v, AXES, self.pairs(lambda b, r, p: (b, r ^ bits, p), sends))

    def plane_xor(self, v, bits, sends=None):
        return lax.ppermute(v, AXES, self.pairs(lambda b, r, p: (b, r, p ^ bits), sends))

    def block_shift(self, v, step):
        return lax.ppermute(v, AXES, self.pairs(lambda b, r, p: ((b + step) % self.blocks, r, p)))


def pick(parts, index):
    return lax.dynamic_index_in_dim(jnp.stack(parts), index, 0, keepdims=False)


def by_xor(parts, index):
    a, b, c, d = parts
    odd = (index & 1) == 1
    a, b = jnp.where(odd, b, a), jnp.where(odd, a, b)
    c, d = jnp.where(odd, d, c), jnp.where(odd, c, d)
    top = (index & 2) == 2
    return [jnp.where(top, c, a), jnp.where(top, d, b), jnp.where(top, a, c), jnp.where(top, b, d)]


def gather_group(pl, pack):
    exchanged = [lax.dynamic_index_in_dim(pack, pl.role, 0, False)]
    for bits in (1, 2, 3):
        exchanged.append(pl.role_xor(lax.dynamic_index_in_dim(pack, pl.role ^ bits, 0, False), bits))
    piece = jnp.concatenate(by_xor(exchanged, pl.role), axis=-1)
    planes = [piece] + [pl.plane_xor(piece, bits) for bits in (1, 2, 3)]
    planes = jnp.stack(planes, axis=1)
    if pl.blocks == 2:
        other = pl.block_shift(planes, 1)
        first = pl.block == 0
        both = [jnp.where(first, planes, other), jnp.where(first, other, planes)]
    else:
        shifted = jnp.stack([planes] + [pl.block_shift(planes, s) for s in range(1, pl.blocks)])
        both = [
            lax.dynamic_index_in_dim(shifted, (pl.block - b) % pl.blocks, 0, False)
            for b in range(pl.blocks)
        ]
    whole = jnp.concatenate(both, axis=-1)
    return whole.reshape(whole.shape[0], whole.shape[1] * whole.shape[2], whole.shape[3])


def scatter_group(pl, grads):
    mats, rows, width = grads.shape
    grads = grads.reshape(mats, pl.head, rows // pl.head, pl.blocks, width // pl.blocks)
    total = lax.dynamic_index_in_dim(grads, pl.block, 3, False)
    for step in range(1, pl.blocks):
        sent = lax.dynamic_index_in_dim(grads, (pl.block + step) % pl.blocks, 3, False)
        total = total + wide(pl.block_shift(low(sent), step))
    mine = total[:, 0]
    for bits in (1, 2, 3):
        mine = mine + wide(pl.plane_xor(low(total[:, bits]), bits))
    mine = low(mine).reshape(mats, rows // pl.head, TP, -1)
    exchanged = [lax.dynamic_index_in_dim(mine, pl.role, 2, False)]
    for bits in (1, 2, 3):
        exchanged.append(pl.role_xor(lax.dynamic_index_in_dim(mine, pl.role ^ bits, 2, False), bits))
    return wide(jnp.stack(by_xor(exchanged, pl.role)))


def sum_roles(pl, rows):
    half = rows.shape[1] // 2
    core = pl.role & 1
    rows = low(rows)
    kept = jnp.where(core == 0, rows[:, :half], rows[:, half:])
    sent = jnp.where(core == 0, rows[:, half:], rows[:, :half])
    chip = low(wide(kept) + wide(pl.role_xor(sent, 1)))
    total = low(wide(chip) + wide(pl.role_xor(chip, 2)))
    other = pl.role_xor(total, 1)
    return wide(
        jnp.concatenate(
            [jnp.where(core == 0, total, other), jnp.where(core == 0, other, total)], axis=1
        )
    )


def share_images(pl, held):
    own = lax.dynamic_index_in_dim(held, pl.plane // 2, 0, False)
    owner = lambda b, r, p: (r & 1) == (p & 1)
    other = pl.role_xor(own, 2, owner)
    top = pl.role >= 2
    pair = jnp.stack([jnp.where(top, other, own), jnp.where(top, own, other)])
    passed = pl.role_xor(pair, 1, owner)
    return jnp.where((pl.role & 1) == (pl.plane & 1), pair, passed)


def return_images(pl, pair):
    mine = low(jnp.where(pl.role >= 2, pair[1], pair[0]))
    owner = lambda b, r, p: (r & 1) == (p & 1)
    one, two, three = [pl.plane_xor(mine, bits, owner) for bits in (1, 2, 3)]
    odd = (pl.role & 1) != (pl.plane & 1)
    near = jnp.where(odd, one, mine)
    far = jnp.where(odd, three, two)
    first = pl.plane < 2
    return wide(jnp.stack([jnp.where(first, near, far), jnp.where(first, far, near)]))


def norm_rows(stream, gain, shift):
    average = jnp.mean(stream, axis=-1, keepdims=True)
    centred = stream - average
    inverse = lax.rsqrt(jnp.mean(centred * centred, axis=-1, keepdims=True) + epsilon)
    unit = centred * inverse
    return low(unit * gain + shift), unit, inverse


def norm_back(upstream, unit, inverse, gain):
    scaled = upstream * gain
    return inverse * (
        scaled
        - jnp.mean(scaled, axis=-1, keepdims=True)
        - unit * jnp.mean(scaled * unit, axis=-1, keepdims=True)
    )


def split_heads(rows):
    return rows.reshape(rows.shape[0], rows.shape[1] // HD, HD)


def layer_forward(pl, stream, weights):
    (w_qkv, w_out), (w_in, w_down), qv_bias, in_bias, gains, shifts = weights
    normed, unit_first, inverse_first = norm_rows(stream, gains[0], shifts[0])
    queries = low(product(normed, w_qkv[0], "sd,ad->sa") + qv_bias[0])
    key_rows = low(product(normed, w_qkv[1], "sd,ad->sa"))
    value_rows = low(product(normed, w_qkv[2], "sd,ad->sa") + qv_bias[1])
    scores = product(split_heads(queries), split_heads(key_rows), "qhd,khd->hqk") * HD ** (-0.5)
    largest = jnp.max(scores, axis=-1, keepdims=True)
    logsum = largest + jnp.log(jnp.sum(jnp.exp(scores - largest), axis=-1, keepdims=True))
    soft_low = low(jnp.exp(scores - logsum))
    attended = product(soft_low, split_heads(value_rows), "hqk,khd->qhd")
    attended = low(attended.reshape(queries.shape))
    branch = sum_roles(pl, product(attended, w_out, "sa,ad->sd"))
    stream = stream + branch + shifts[2]
    normed_second, unit_second, inverse_second = norm_rows(stream, gains[1], shifts[1])
    hidden = product(normed_second, w_in, "sd,fd->sf") + in_bias
    active = low(jax.nn.gelu(hidden, approximate=False))
    branch = sum_roles(pl, product(active, w_down, "sf,fd->sd"))
    stream = stream + branch + shifts[3]
    stored = (
        unit_first, inverse_first, normed, queries, key_rows, value_rows, logsum, attended,
        unit_second, inverse_second, normed_second, hidden, active,
    )
    return stream, stored


def layer_backward(pl, upstream, weights, stored):
    (w_qkv, w_out), (w_in, w_down), qv_bias, in_bias, gains, shifts = weights
    (
        unit_first, inverse_first, normed, queries, key_rows, value_rows, logsum, attended,
        unit_second, inverse_second, normed_second, hidden, active,
    ) = stored
    shift_down = jnp.sum(upstream, axis=0)
    upstream_low = low(upstream)
    grad_down = product(active, upstream_low, "sf,sd->fd")
    grad_active = product(upstream_low, w_down, "sd,fd->sf")
    unused, gelu_back = jax.vjp(functools.partial(jax.nn.gelu, approximate=False), hidden)
    grad_hidden = low(gelu_back(grad_active)[0])
    grad_in_bias = jnp.sum(wide(grad_hidden), axis=0)
    grad_in = product(grad_hidden, normed_second, "sf,sd->fd")
    grad_normed_second = sum_roles(pl, product(grad_hidden, w_in, "sf,fd->sd"))
    gain_second = jnp.sum(grad_normed_second * unit_second, axis=0)
    shift_second = jnp.sum(grad_normed_second, axis=0)
    grad_mid = upstream + norm_back(grad_normed_second, unit_second, inverse_second, gains[1])
    shift_out = jnp.sum(grad_mid, axis=0)
    mid_low = low(grad_mid)
    grad_out = product(attended, mid_low, "sa,sd->ad")
    grad_attended = low(product(mid_low, w_out, "sd,ad->sa"))
    query_heads, key_heads, value_heads = map(split_heads, (queries, key_rows, value_rows))
    factor = HD ** (-0.5)
    soft = jnp.exp(product(query_heads, key_heads, "qhd,khd->hqk") * factor - logsum)
    attended_heads = split_heads(grad_attended)
    flat = queries.shape
    grad_values = low(product(low(soft), attended_heads, "hqk,qhd->khd").reshape(flat))
    grad_soft = product(attended_heads, value_heads, "qhd,khd->hqk")
    grad_scores = low(soft * (grad_soft - jnp.sum(grad_soft * soft, axis=-1, keepdims=True)))
    grad_queries = low((product(grad_scores, key_heads, "hqk,khd->qhd") * factor).reshape(flat))
    grad_keys = low((product(grad_scores, query_heads, "hqk,qhd->khd") * factor).reshape(flat))
    grad_qv = jnp.stack([jnp.sum(wide(grad_queries), axis=0), jnp.sum(wide(grad_values), axis=0)])
    grad_qkv = [product(g, normed, "sa,sd->ad") for g in (grad_queries, grad_keys, grad_values)]
    partial_sum = (
        product(grad_queries, w_qkv[0], "sa,ad->sd")
        + product(grad_keys, w_qkv[1], "sa,ad->sd")
        + product(grad_values, w_qkv[2], "sa,ad->sd")
    )
    grad_normed_first = sum_roles(pl, partial_sum)
    gain_first = jnp.sum(grad_normed_first * unit_first, axis=0)
    shift_first = jnp.sum(grad_normed_first, axis=0)
    upstream = grad_mid + norm_back(grad_normed_first, unit_first, inverse_first, gains[0])
    attn_grads = jnp.stack(grad_qkv + [grad_out])
    mlp_grads = jnp.stack([grad_in, grad_down])
    by_feature = jnp.stack(
        [gain_first, gain_second, shift_first, shift_second, shift_out, shift_down]
    )
    return upstream, (attn_grads, mlp_grads, grad_qv, grad_in_bias, by_feature)


def body(images, cotangent, w_qkv, w_out, w_in, w_down, qv_bias, in_bias, gains, shifts):
    fsdp, head = lax.axis_size("fsdp"), lax.axis_size("head")
    pl = Places(fsdp, head)
    cols = w_qkv.shape[2]
    width, units = w_qkv.shape[3] // TP, w_in.shape[2] // TP

    first = share_images(pl, images)
    small = jnp.concatenate(
        [qv_bias.reshape(-1), in_bias.reshape(-1), gains.reshape(-1), shifts.reshape(-1)]
    )
    small = wide(lax.all_gather(small, AXES, axis=0, tiled=False)).reshape(fsdp, head, -1)
    sizes = [qv_bias.size, in_bias.size, gains.size, shifts.size]
    marks = [0]
    for s in sizes:
        marks.append(marks[-1] + s)
    qv_all, in_all, gain_all, shift_all = [small[:, :, a:b] for a, b in zip(marks, marks[1:])]
    gain_all = gain_all[:, 0].reshape(fsdp, LAYERS, 2, cols).transpose(1, 2, 0, 3).reshape(LAYERS, 2, -1)
    shift_all = shift_all[:, 0].reshape(fsdp, LAYERS, 4, cols).transpose(1, 2, 0, 3).reshape(LAYERS, 4, -1)
    xor_planes = pl.plane ^ jnp.arange(head)
    qv_all = qv_all.reshape(fsdp, head, LAYERS, 2, -1).transpose(2, 3, 1, 4, 0).reshape(LAYERS, 2, head, TP, width)
    qv_mine = lax.dynamic_index_in_dim(qv_all, pl.role, 3, False)[:, :, xor_planes].reshape(LAYERS, 2, -1)
    in_all = in_all.reshape(fsdp, head, LAYERS, -1).transpose(2, 1, 3, 0).reshape(LAYERS, head, TP, units)
    in_mine = lax.dynamic_index_in_dim(in_all, pl.role, 2, False)[:, xor_planes].reshape(LAYERS, -1)

    weights = []
    for l in range(LAYERS):
        attn = jnp.concatenate([w_qkv[l].transpose(0, 2, 1), w_out[l][None]]).reshape(4, TP, width, cols)
        mlp = jnp.stack([w_in[l].T, w_down[l]]).reshape(2, TP, units, cols)
        attn = gather_group(pl, attn.transpose(1, 0, 2, 3))
        mlp = gather_group(pl, mlp.transpose(1, 0, 2, 3))
        weights.append(((attn[:3], attn[3]), (mlp[0], mlp[1]), qv_mine[l], in_mine[l], gain_all[l], shift_all[l]))

    streams = [wide(first[0]), wide(first[1])]
    stored = [[], []]
    for l in range(LAYERS):
        for i in range(2):
            streams[i], kept = layer_forward(pl, streams[i], weights[l])
            stored[i].append(kept)
    block_out = return_images(pl, streams)
    second = share_images(pl, cotangent)
    upstreams = [wide(second[0]), wide(second[1])]
    parts = {}
    for l in reversed(range(LAYERS)):
        sums = None
        for i in range(2):
            upstreams[i], grads = layer_backward(pl, upstreams[i], weights[l], stored[i][l])
            sums = grads if sums is None else tuple(a + b for a, b in zip(sums, grads))
        mlp = scatter_group(pl, sums[1])
        attn = scatter_group(pl, sums[0])
        parts[l] = (attn, mlp, *sums[2:])
    input_grad = return_images(pl, upstreams)

    attn = jnp.stack([parts[l][0] for l in range(LAYERS)])
    mlp = jnp.stack([parts[l][1] for l in range(LAYERS)])
    attn = attn.transpose(0, 2, 1, 3, 4).reshape(LAYERS, 4, TP * width, cols)
    mlp = mlp.transpose(0, 2, 1, 3, 4).reshape(LAYERS, 2, TP * units, cols)
    grad_qkv = attn[:, :3].transpose(0, 1, 3, 2)
    grad_out = attn[:, 3]
    grad_in = mlp[:, 0].transpose(0, 2, 1)
    grad_down = mlp[:, 1]

    by_feature = jnp.stack([parts[l][4] for l in range(LAYERS)])
    qv = jnp.stack([parts[l][2] for l in range(LAYERS)]).reshape(LAYERS, 2, head, width)[:, :, xor_planes]
    inner = jnp.stack([parts[l][3] for l in range(LAYERS)]).reshape(LAYERS, head, units)[:, xor_planes]
    qv_full = lax.dynamic_update_index_in_dim(
        jnp.zeros((LAYERS, 2, head, TP, width), jnp.float32), qv, pl.role, 3
    )
    inner_full = lax.dynamic_update_index_in_dim(
        jnp.zeros((LAYERS, head, TP, units), jnp.float32), inner, pl.role, 2
    )
    vector = jnp.concatenate([by_feature.reshape(-1) / TP, qv_full.reshape(-1), inner_full.reshape(-1)])
    vector = lax.psum(vector, AXES)
    f, h = lax.axis_index("fsdp"), lax.axis_index("head")
    a, b = by_feature.size, by_feature.size + qv_full.size
    by_feature = vector[:a].reshape(LAYERS, 6, fsdp, cols)
    by_feature = lax.dynamic_index_in_dim(by_feature, f, 2, False)
    qv = vector[a:b].reshape(LAYERS, 2, head, -1, fsdp)
    qv = lax.dynamic_index_in_dim(lax.dynamic_index_in_dim(qv, h, 2, False), f, 3, True)
    inner = vector[b:].reshape(LAYERS, head, -1, fsdp)
    inner = lax.dynamic_index_in_dim(lax.dynamic_index_in_dim(inner, h, 1, False), f, 2, True)
    return (
        block_out, input_grad, grad_qkv, grad_out, grad_in, grad_down,
        qv, inner, by_feature[:, :2], by_feature[:, 2:],
    )


def solution(mesh):
    placed = (
        P("fsdp", None, None),
        P("fsdp", None, None),
        P(None, None, "fsdp", "head"),
        P(None, "head", "fsdp"),
        P(None, "fsdp", "head"),
        P(None, "head", "fsdp"),
        P(None, None, "head", "fsdp"),
        P(None, "head", "fsdp"),
        P(None, None, "fsdp"),
        P(None, None, "fsdp"),
    )
    return jax.shard_map(
        body, mesh=mesh, in_specs=placed, out_specs=placed, check_vma=False
    )
```

```python
import functools
import math

import jax
import jax.numpy as jnp
from jax import lax
from jax.experimental import pallas as pl
from jax.experimental.pallas import tpu as pltpu
from jax.sharding import PartitionSpec as P

D = 1024
HD = 64
LAYERS = 2
TP = 4
HALF = D // 2
AXES = ("fsdp", "head")
MESH = pl.DeviceIdType.MESH
epsilon = 1e-06
f32, bf16 = jnp.float32, jnp.bfloat16


def dot(left, right, left_dim, right_dim):
    return lax.dot_general(
        left, right, (((left_dim,), (right_dim,)), ((), ())), preferred_element_type=f32
    )


def flip1(n):
    return n + 1 - 2 * (n % 2)


def flip2(n):
    return n + 2 - 4 * ((n // 2) % 2)


def flip(n, bits):
    if bits & 1:
        n = flip1(n)
    if bits & 2:
        n = flip2(n)
    return n


class Spot:
    def __init__(self, fsdp, head):
        self.blocks = fsdp // TP
        self.planes = head
        index = lax.axis_index("fsdp")
        self.index = index
        self.block, self.role, self.plane = index // TP, index % TP, lax.axis_index("head")
        self.core, self.side = self.role % 2, self.role // 2

    def at(self, block=None, role=None, plane=None):
        block = self.block if block is None else block
        role = self.role if role is None else role
        plane = self.plane if plane is None else plane
        return (block * TP + role, plane)

    def partners(self):
        found = [self.at(role=flip(self.role, o)) for o in (1, 2, 3)]
        found += [self.at(plane=flip(self.plane, o)) for o in (1, 2, 3)]
        found += [self.at(block=(self.block + s) % self.blocks) for s in range(1, self.blocks)]
        return found


def greet(partners):
    barrier = pltpu.get_barrier_semaphore()
    for partner in partners:
        pl.semaphore_signal(barrier, inc=1, device_id=partner, device_id_type=MESH)
    pl.semaphore_wait(barrier, len(partners))


def send(source, target, sems, where, device):
    return pltpu.make_async_remote_copy(
        src_ref=source,
        dst_ref=target,
        send_sem=sems[0].at[where],
        recv_sem=sems[1].at[where],
        device_id=device,
        device_id_type=MESH,
    )


def lanes(start, size):
    return pl.ds(pl.multiple_of(start, 128), size)


class Gather:
    def __init__(self, spot, packed, whole, role_sems, plane_sems, block_sems, base, local_sem, direct):
        self.spot, self.packed, self.whole, self.direct = spot, packed, whole, direct
        self.role_sems, self.plane_sems, self.block_sems = role_sems, plane_sems, block_sems
        self.base, self.local_sem = base, local_sem
        self.cols = D // spot.blocks // TP
        self.span = D // spot.blocks

    def piece(self, g, plane, block):
        return self.whole.at[g, plane, :, lanes(block * self.span, self.span)]

    def own(self, g):
        spot = self.spot
        if self.direct:
            return pltpu.make_async_copy(
                self.packed.at[g, spot.role],
                self.whole.at[g, spot.plane, :, lanes(spot.index * self.cols, self.cols)],
                self.local_sem.at[self.base + g],
            )
        return pltpu.make_async_copy(
            self.packed.at[g], self.piece(g, spot.plane, spot.block), self.local_sem.at[self.base + g]
        )

    def to_role(self, g, o):
        spot = self.spot
        other = flip(spot.role, o)
        return send(
            self.packed.at[g, other],
            self.whole.at[g, spot.plane, :, lanes(spot.index * self.cols, self.cols)],
            self.role_sems,
            (self.base + g, o),
            spot.at(role=other),
        )

    def from_role(self, g, o):
        spot = self.spot
        other = flip(spot.role, o)
        place = self.whole.at[
            g, spot.plane, :, lanes((spot.block * TP + other) * self.cols, self.cols)
        ]
        return send(place, place, self.role_sems, (self.base + g, o), spot.at(role=other))

    def to_plane(self, g, o):
        spot = self.spot
        place = self.piece(g, spot.plane, spot.block)
        return send(
            place, place, self.plane_sems, (self.base + g, o), spot.at(plane=flip(spot.plane, o))
        )

    def from_plane(self, g, o):
        spot = self.spot
        other = flip(spot.plane, o)
        place = self.piece(g, other, spot.block)
        return send(place, place, self.plane_sems, (self.base + g, o), spot.at(plane=other))

    def to_block(self, g, s, o):
        spot = self.spot
        place = self.piece(g, flip(spot.plane, o), spot.block)
        block = (spot.block + s) % spot.blocks
        return send(
            place, place, self.block_sems, (self.base + g, s, o), spot.at(block=block)
        )

    def from_block(self, g, s, o):
        spot = self.spot
        block = (spot.block + spot.blocks - s) % spot.blocks
        place = self.piece(g, flip(spot.plane, o), block)
        return send(
            place, place, self.block_sems, (self.base + g, s, o), spot.at(block=block)
        )

    def begin(self, g):
        self.own(g).start()
        if self.direct:
            for o in (1, 2, 3):
                self.to_role(g, o).start()

    def spread(self, g):
        self.own(g).wait()
        if self.direct:
            for o in (1, 2, 3):
                self.from_role(g, o).wait_recv()
        for o in (1, 2, 3):
            self.to_plane(g, o).start()
        for s in range(1, self.spot.blocks):
            self.to_block(g, s, 0).start()

    def relay(self, g, o):
        self.from_plane(g, o).wait_recv()
        for s in range(1, self.spot.blocks):
            self.to_block(g, s, o).start()

    def complete(self, g):
        for s in range(1, self.spot.blocks):
            for o in range(4):
                self.from_block(g, s, o).wait_recv()

    def drain(self, g):
        for o in (1, 2, 3):
            if self.direct:
                self.to_role(g, o).wait_send()
            self.to_plane(g, o).wait_send()
        for s in range(1, self.spot.blocks):
            for o in range(4):
                self.to_block(g, s, o).wait_send()


class Exchange:
    def __init__(self, spot, sent, core_in, chip, side_in, full, core_sems, side_sems, back_sems):
        self.spot = spot
        self.sent, self.core_in, self.chip, self.side_in, self.full = sent, core_in, chip, side_in, full
        self.core_sems, self.side_sems, self.back_sems = core_sems, side_sems, back_sems
        self.mine = lanes(spot.core * HALF, HALF)
        self.theirs = lanes((1 - spot.core) * HALF, HALF)

    def core_copy(self, i):
        return send(
            self.sent.at[i], self.core_in.at[i], self.core_sems, (i,),
            self.spot.at(role=flip1(self.spot.role)),
        )

    def side_copy(self, i, slot):
        return send(
            self.chip.at[i], self.side_in.at[i, slot], self.side_sems, (i, slot),
            self.spot.at(role=flip2(self.spot.role)),
        )

    def back_copy(self, i):
        place = self.full.at[i, :, self.mine]
        return send(place, place, self.back_sems, (i,), self.spot.at(role=flip1(self.spot.role)))

    def back_in(self, i):
        place = self.full.at[i, :, self.theirs]
        return send(place, place, self.back_sems, (i,), self.spot.at(role=flip1(self.spot.role)))

    def reduce(self, i, product, kept):
        rows = kept.shape[0]
        self.sent[i] = product(self.theirs).astype(bf16)
        self.core_copy(i).start()
        kept[...] = product(self.mine)
        copy = self.core_copy(i)
        copy.wait_recv()

        def add(c, carry):
            r = pl.ds(pl.multiple_of(c * 16, 16), 16)
            self.chip[i, r] = (kept[r] + self.core_in[i, r].astype(f32)).astype(bf16)
            return carry

        lax.fori_loop(0, rows // 16, add, 0, unroll=2)
        copy.wait_send()

    def finish(self, i, slot):
        copy = self.side_copy(i, slot)
        copy.wait_recv()
        rows = self.chip.shape[1]

        def add(c, carry):
            r = pl.ds(pl.multiple_of(c * 16, 16), 16)
            total = self.chip[i, r].astype(f32) + self.side_in[i, slot, r].astype(f32)
            self.full[i, r, self.mine] = total.astype(bf16)
            return carry

        lax.fori_loop(0, rows // 16, add, 0, unroll=2)
        self.back_copy(i).start()
        copy.wait_send()
        self.back_in(i).wait_recv()
        self.back_copy(i).wait_send()


def each_rows(rows, size, step, unroll=1):
    def one(c, carry):
        step(pl.ds(pl.multiple_of(c * size, size), size))
        return carry

    lax.fori_loop(0, rows // size, one, 0, unroll=unroll)


def forward_kernel(cfg, *refs):
    fsdp, head, tokens, rows, direct = cfg
    (
        own_image, own_cot, packed, extras,
        weights_out, vec_out, normed_out, unit_out, inverse_out, qkv_out, att_out, lse_out, hidden_out,
        stream_out, chip_out, cot_out,
        whole, extra, vec, pair, cots, stream, normed, unit, inverse, qkv, scores, soft, att_sum, att,
        row_scale, lse, lse_rows, hidden, low_hidden, active, kept,
        sent, core_in, chip, side_in, full,
        role_s, role_r, plane_s, plane_r, block_s, block_r, local_sem,
        core_s, core_r, side_s, side_r, back_s, back_r,
        share_s, share_r, store_sem,
    ) = refs
    spot = Spot(fsdp, head)
    groups = 3 * LAYERS
    greet(spot.partners())
    sems = ((role_s, role_r), (plane_s, plane_r), (block_s, block_r))
    small = Gather(spot, extras, extra, *sems, groups, local_sem, direct)
    large = Gather(spot, packed, whole, *sems, 0, local_sem, direct)
    exchange = Exchange(
        spot, sent, core_in, chip, side_in, full, (core_s, core_r), (side_s, side_r), (back_s, back_r)
    )
    owner = spot.core == spot.plane % 2
    x, other_x = spot.side, 1 - spot.side

    small.begin(0)
    large.begin(0)

    def share(source, held, n):
        across = send(
            source, held.at[x], (share_s, share_r), (n, 0), spot.at(role=flip2(spot.role))
        )
        across_in = send(
            held.at[other_x], held.at[other_x], (share_s, share_r), (n, 0), spot.at(role=flip2(spot.role))
        )
        down = [
            send(src, held.at[at], (share_s, share_r), (n, 1 + k), spot.at(role=flip1(spot.role)))
            for k, (src, at) in enumerate(((source, x), (held.at[other_x], other_x)))
        ]
        mine = pltpu.make_async_copy(source, held.at[x], store_sem.at[30 + n])
        return across, across_in, down, mine

    def share_begin(source, held, n):
        across, across_in, down, mine = share(source, held, n)

        @pl.when(owner)
        def _():
            across.start()
            mine.start()
            down[0].start()

    def share_end(source, held, n):
        across, across_in, down, mine = share(source, held, n)

        @pl.when(owner)
        def _():
            across_in.wait_recv()
            down[1].start()
            across.wait_send()
            mine.wait()
            down[0].wait_send()
            down[1].wait_send()

        @pl.when(jnp.logical_not(owner))
        def _():
            down[0].wait_recv()
            down[1].wait_recv()

    share_begin(own_image, pair, 0)
    for g in range(1, groups):
        large.begin(g)
    small.spread(0)
    large.spread(0)
    large.spread(1)
    for o in (1, 2, 3):
        small.relay(0, o)
    for o in (1, 2, 3):
        large.relay(0, o)
    large.spread(2)
    share_end(own_image, pair, 0)
    small.complete(0)

    cols = D // fsdp
    quarter = 64
    for l in range(LAYERS):
        vec[l, 0:6] = extra[0, 0, 16 * l : 16 * l + 16].astype(f32)[0:6]

        def selector(width, offset):
            c = lax.broadcasted_iota(jnp.int32, (D, width), 0)
            j = lax.broadcasted_iota(jnp.int32, (D, width), 1)
            return jnp.where((c // cols == j % fsdp) & (c % cols == offset + j // fsdp), 1.0, 0.0).astype(bf16)

        per = quarter // fsdp
        for plane in range(4):
            block = extra[0, plane, 16 * l : 16 * l + 16]
            vec[l, 6:7, plane * 256 : plane * 256 + 256] = dot(block, selector(256, 2 * per), 1, 0)[6:7]
            if plane % 2 == 0:
                following = extra[0, plane + 1, 16 * l : 16 * l + 16]
                for k in range(2):
                    pick = selector(quarter, k * per)
                    two = jnp.concatenate([dot(block, pick, 1, 0), dot(following, pick, 1, 0)], axis=1)
                    at = k * 256 + plane * quarter
                    vec[l, 7:8, at : at + 128] = two[6:7]
    store_vec = pltpu.make_async_copy(vec, vec_out, store_sem.at[28])
    store_vec.start()
    large.complete(0)

    lane_head = lax.broadcasted_iota(jnp.int32, (1, 256), 1) // HD
    key_bias = jnp.where(lax.broadcasted_iota(jnp.int32, (1, rows), 1) < tokens, 0.0, -1e30)

    def stores(l, n, i):
        return [
            pltpu.make_async_copy(normed.at[i], normed_out.at[l, n, i], store_sem.at[0 + i]),
            pltpu.make_async_copy(unit.at[i], unit_out.at[l, n, i], store_sem.at[2 + i]),
            pltpu.make_async_copy(inverse.at[i], inverse_out.at[l, n, i], store_sem.at[4 + i]),
        ]

    def norm(l, n, i, read):
        def step(r):
            v = read(r)
            stream[i, r] = v
            average = jnp.mean(v, axis=-1, keepdims=True)
            centred = v - average
            scale = lax.rsqrt(jnp.mean(centred * centred, axis=-1, keepdims=True) + epsilon)
            u = centred * scale
            unit[i, r] = u.astype(bf16)
            inverse[i, r] = jnp.broadcast_to(scale, (16, 128))
            normed[i, r] = (u * vec[l, n : n + 1] + vec[l, 2 + n : 3 + n]).astype(bf16)

        each_rows(rows, 16, step, unroll=2)
        for copy in stores(l, n, i):
            copy.start()

    def attn_stage(l, i):
        g = 3 * l

        @pl.when(l > 0)
        def _():
            exchange.finish(i, 1)
            for copy in stores(l - 1, 1, i):
                copy.wait()
            before = jnp.maximum(l - 1, 0)
            norm(l, 0, i, lambda r: stream[i, r] + full[i, r].astype(f32) + vec[before, 5:6])

        @pl.when(l == 0)
        def _():
            norm(l, 0, i, lambda r: pair[i, r].astype(f32))

        store_qkv = pltpu.make_async_copy(qkv, qkv_out.at[l, i], store_sem.at[6])
        store_att = pltpu.make_async_copy(att.at[i], att_out.at[l, i], store_sem.at[8 + i])
        store_lse = pltpu.make_async_copy(lse_rows.at[i], lse_out.at[l, i], store_sem.at[10 + i])

        @pl.when(l + i > 0)
        def _():
            store_qkv.wait()

        @pl.when(l > 0)
        def _():
            store_att.wait()
            store_lse.wait()

        for k in range(3):
            w = whole[g, :, k * HD : k * HD + HD].reshape(256, D)
            part = dot(normed[i], w, 1, 1)
            if k == 0:
                part = part + vec[l, 7:8, 0:256]
            if k == 2:
                part = part + vec[l, 7:8, 256:512]
            qkv[:, k * 256 : k * 256 + 256] = part.astype(bf16)
        store_qkv.start()

        att_sum[...] = jnp.zeros_like(att_sum)
        lse[...] = jnp.zeros_like(lse)

        def one_head(h, carry):
            mask = jnp.where(lane_head == h, 1.0, 0.0)
            q = qkv[:, 0:256] * (mask * HD ** (-0.5)).astype(bf16)
            scores[...] = dot(q, qkv[:, 256:512], 1, 1)
            here = lax.broadcasted_iota(jnp.int32, (1, 128), 1) == h

            def step(r):
                s = scores[r] + key_bias
                largest = jnp.max(s, axis=-1, keepdims=True)
                e = jnp.exp(s - largest)
                total = jnp.sum(e, axis=-1, keepdims=True)
                soft[r] = e.astype(bf16)
                row_scale[r] = jnp.broadcast_to(1.0 / total, (16, 128))
                lse[r] = jnp.where(here, largest + jnp.log(total), lse[r])

            each_rows(rows, 16, step, unroll=2)
            o = dot(soft[...], qkv[:, 512:768], 1, 0)
            scale = row_scale[...]
            att_sum[...] += o * jnp.concatenate([scale, scale], axis=1) * mask
            return carry

        lax.fori_loop(0, 4, one_head, 0)
        att[i] = att_sum[...].astype(bf16)
        lse_rows[i] = jnp.transpose(lse[...])[0:8]
        store_att.start()
        store_lse.start()
        exchange.reduce(
            i, lambda at: dot(att[i], whole[g, :, 192:256, at].reshape(256, HALF), 1, 0), kept
        )
        exchange.side_copy(i, 0).start()

    def mlp_stage(l, i):
        g = 3 * l
        exchange.finish(i, 0)
        for copy in stores(l, 0, i):
            copy.wait()
        norm(l, 1, i, lambda r: stream[i, r] + full[i, r].astype(f32) + vec[l, 4:5])
        store_hidden = pltpu.make_async_copy(low_hidden.at[i], hidden_out.at[l, i], store_sem.at[12 + i])

        @pl.when(l > 0)
        def _():
            store_hidden.wait()

        hidden[...] = dot(normed[i], whole[g + 1].reshape(D, D), 1, 1)

        def step(r):
            v = hidden[r] + vec[l, 6:7]
            low_hidden[i, r] = v.astype(bf16)
            active[r] = (v * (0.5 + 0.5 * lax.erf(v * (0.5**0.5)))).astype(bf16)

        each_rows(rows, 16, step, unroll=2)
        store_hidden.start()

        @pl.when(i == 0)
        def _():
            large.complete(g + 2)

        exchange.reduce(i, lambda at: dot(active[...], whole[g + 2, :, :, at].reshape(D, HALF), 1, 0), kept)

        @pl.when(l < LAYERS - 1)
        def _():
            exchange.side_copy(i, 1).start()

        @pl.when(l == LAYERS - 1)
        def _():
            pltpu.make_async_copy(chip.at[i], chip_out.at[i], store_sem.at[14 + i]).start()
            pltpu.make_async_copy(stream.at[i], stream_out.at[i], store_sem.at[16 + i]).start()

    def store_weights(g):
        return pltpu.make_async_copy(whole.at[g], weights_out.at[g], store_sem.at[18 + g])

    def one_layer(l, carry):
        g = 3 * l

        @pl.when(l > 0)
        def _():
            large.complete(g)

        attn_stage(l, 0)

        @pl.when(l == 0)
        def _():
            share_begin(own_cot, cots, 1)
            large.spread(3)

        for o in (1, 2, 3):
            large.relay(g + 1, o)
        attn_stage(l, 1)

        for o in (1, 2, 3):
            large.relay(g + 2, o)

        @pl.when(l == 0)
        def _():
            large.spread(4)

        large.complete(g + 1)
        mlp_stage(l, 0)

        @pl.when(l == 0)
        def _():
            for o in (1, 2, 3):
                large.relay(3, o)
            large.spread(5)

        mlp_stage(l, 1)
        for k in range(3):
            store_weights(g + k).start()
        return carry

    lax.fori_loop(0, LAYERS, one_layer, 0)
    share_end(own_cot, cots, 1)
    store_cots = pltpu.make_async_copy(cots, cot_out, store_sem.at[29])
    store_cots.start()
    last = LAYERS - 1
    for i in range(2):
        for copy in stores(last, 1, i):
            copy.wait()
        pltpu.make_async_copy(att.at[i], att_out.at[last, i], store_sem.at[8 + i]).wait()
        pltpu.make_async_copy(lse_rows.at[i], lse_out.at[last, i], store_sem.at[10 + i]).wait()
        pltpu.make_async_copy(low_hidden.at[i], hidden_out.at[last, i], store_sem.at[12 + i]).wait()
        pltpu.make_async_copy(chip.at[i], chip_out.at[i], store_sem.at[14 + i]).wait()
        pltpu.make_async_copy(stream.at[i], stream_out.at[i], store_sem.at[16 + i]).wait()
    pltpu.make_async_copy(qkv, qkv_out.at[last, 1], store_sem.at[6]).wait()
    store_vec.wait()
    store_cots.wait()

    def finish_group(g, carry):
        store_weights(g).wait()
        large.drain(g)
        return carry

    lax.fori_loop(0, groups, finish_group, 0)
    small.drain(0)


def forward_call(fsdp, head, tokens, rows, direct, own_image, own_cot, packed, extras):
    groups = 3 * LAYERS
    blocks = fsdp // TP
    anyspace = pl.BlockSpec(memory_space=pl.ANY)
    shape = jax.ShapeDtypeStruct
    dma = pltpu.SemaphoreType.DMA
    out_shape = (
        shape((groups, 4, 256, D), bf16),
        shape((LAYERS, 8, D), f32),
        shape((LAYERS, 2, 2, rows, D), bf16),
        shape((LAYERS, 2, 2, rows, D), bf16),
        shape((LAYERS, 2, 2, rows, 128), f32),
        shape((LAYERS, 2, rows, 768), bf16),
        shape((LAYERS, 2, rows, 256), bf16),
        shape((LAYERS, 2, 8, rows), f32),
        shape((LAYERS, 2, rows, D), bf16),
        shape((2, rows, D), f32),
        shape((2, rows, HALF), bf16),
        shape((2, rows, D), bf16),
    )
    scratch = [
        pltpu.VMEM((groups, 4, 256, D), bf16),
        pltpu.VMEM((1, 4, 32, D), bf16),
        pltpu.VMEM((LAYERS, 8, D), f32),
        pltpu.VMEM((2, rows, D), bf16),
        pltpu.VMEM((2, rows, D), bf16),
        pltpu.VMEM((2, rows, D), f32),
        pltpu.VMEM((2, rows, D), bf16),
        pltpu.VMEM((2, rows, D), bf16),
        pltpu.VMEM((2, rows, 128), f32),
        pltpu.VMEM((rows, 768), bf16),
        pltpu.VMEM((rows, rows), f32),
        pltpu.VMEM((rows, rows), bf16),
        pltpu.VMEM((rows, 256), f32),
        pltpu.VMEM((2, rows, 256), bf16),
        pltpu.VMEM((rows, 128), f32),
        pltpu.VMEM((rows, 128), f32),
        pltpu.VMEM((2, 8, rows), f32),
        pltpu.VMEM((rows, D), f32),
        pltpu.VMEM((2, rows, D), bf16),
        pltpu.VMEM((rows, D), bf16),
        pltpu.VMEM((rows, HALF), f32),
        pltpu.VMEM((2, rows, HALF), bf16),
        pltpu.VMEM((2, rows, HALF), bf16),
        pltpu.VMEM((2, rows, HALF), bf16),
        pltpu.VMEM((2, 2, rows, HALF), bf16),
        pltpu.VMEM((2, rows, D), bf16),
        dma((groups + 1, 4)), dma((groups + 1, 4)),
        dma((groups + 1, 4)), dma((groups + 1, 4)),
        dma((groups + 1, blocks, 4)), dma((groups + 1, blocks, 4)),
        dma((groups + 1,)),
        dma((2,)), dma((2,)),
        dma((2, 2)), dma((2, 2)),
        dma((2,)), dma((2,)),
        dma((2, 3)), dma((2, 3)),
        dma((32,)),
    ]
    return pl.pallas_call(
        functools.partial(forward_kernel, (fsdp, head, tokens, rows, direct)),
        out_shape=out_shape,
        in_specs=[anyspace] * 4,
        out_specs=tuple(anyspace for _ in out_shape),
        scratch_shapes=scratch,
        compiler_params=pltpu.CompilerParams(
            collective_id=0, has_side_effects=True, vmem_limit_bytes=60 << 20
        ),
        name="forward_layers",
    )(own_image, own_cot, packed, extras)


def product(left, right, form):
    return jnp.einsum(form, left, right, preferred_element_type=jnp.float32)


def low(v):
    return v.astype(jnp.bfloat16)


def wide(v):
    return v.astype(jnp.float32)


class Places:
    def __init__(self, fsdp, head):
        self.fsdp, self.head = fsdp, head
        self.blocks = fsdp // TP
        index, plane = lax.axis_index("fsdp"), lax.axis_index("head")
        self.block, self.role, self.plane = index // TP, index % TP, plane

    def pairs(self, move, sends=None):
        found = []
        for block in range(self.blocks):
            for role in range(TP):
                for plane in range(self.head):
                    if sends is not None and not sends(block, role, plane):
                        continue
                    to_block, to_role, to_plane = move(block, role, plane)
                    found.append(
                        (
                            (block * TP + role) * self.head + plane,
                            (to_block * TP + to_role) * self.head + to_plane,
                        )
                    )
        return found

    def role_xor(self, v, bits, sends=None):
        return lax.ppermute(v, AXES, self.pairs(lambda b, r, p: (b, r ^ bits, p), sends))

    def plane_xor(self, v, bits, sends=None):
        return lax.ppermute(v, AXES, self.pairs(lambda b, r, p: (b, r, p ^ bits), sends))

    def block_shift(self, v, step):
        return lax.ppermute(v, AXES, self.pairs(lambda b, r, p: ((b + step) % self.blocks, r, p)))


def pick(parts, index):
    return lax.dynamic_index_in_dim(jnp.stack(parts), index, 0, keepdims=False)


def by_xor(parts, index):
    a, b, c, d = parts
    odd = (index & 1) == 1
    a, b = jnp.where(odd, b, a), jnp.where(odd, a, b)
    c, d = jnp.where(odd, d, c), jnp.where(odd, c, d)
    top = (index & 2) == 2
    return [jnp.where(top, c, a), jnp.where(top, d, b), jnp.where(top, a, c), jnp.where(top, b, d)]


def sum_roles(pl, rows):
    half = rows.shape[1] // 2
    core = pl.role & 1
    rows = low(rows)
    kept = jnp.where(core == 0, rows[:, :half], rows[:, half:])
    sent = jnp.where(core == 0, rows[:, half:], rows[:, :half])
    chip = low(wide(kept) + wide(pl.role_xor(sent, 1)))
    total = low(wide(chip) + wide(pl.role_xor(chip, 2)))
    other = pl.role_xor(total, 1)
    return wide(
        jnp.concatenate(
            [jnp.where(core == 0, total, other), jnp.where(core == 0, other, total)], axis=1
        )
    )


def scatter_group(pl, grads):
    mats, head, units, width = grads.shape
    grads = grads.reshape(mats, head, units, pl.blocks, width // pl.blocks)
    total = lax.dynamic_index_in_dim(grads, pl.block, 3, False)
    for step in range(1, pl.blocks):
        sent = lax.dynamic_index_in_dim(grads, (pl.block + step) % pl.blocks, 3, False)
        total = total + wide(pl.block_shift(low(sent), step))
    mine = lax.dynamic_index_in_dim(total, pl.plane, 1, False)
    for bits in (1, 2, 3):
        sent = lax.dynamic_index_in_dim(total, pl.plane ^ bits, 1, False)
        mine = mine + wide(pl.plane_xor(low(sent), bits))
    mine = low(mine).reshape(mats, units, TP, -1)
    exchanged = [lax.dynamic_index_in_dim(mine, pl.role, 2, False)]
    for bits in (1, 2, 3):
        exchanged.append(pl.role_xor(lax.dynamic_index_in_dim(mine, pl.role ^ bits, 2, False), bits))
    return wide(jnp.stack(by_xor(exchanged, pl.role)))

def return_images(pl, pair):
    mine = low(jnp.where(pl.role >= 2, pair[1], pair[0]))
    owner = lambda b, r, p: (r & 1) == (p & 1)
    one, two, three = [pl.plane_xor(mine, bits, owner) for bits in (1, 2, 3)]
    odd = (pl.role & 1) != (pl.plane & 1)
    near = jnp.where(odd, one, mine)
    far = jnp.where(odd, three, two)
    first = pl.plane < 2
    return wide(jnp.stack([jnp.where(first, near, far), jnp.where(first, far, near)]))


def norm_rows(stream, gain, shift):
    average = jnp.mean(stream, axis=-1, keepdims=True)
    centred = stream - average
    inverse = lax.rsqrt(jnp.mean(centred * centred, axis=-1, keepdims=True) + epsilon)
    unit = centred * inverse
    return low(unit * gain + shift), unit, inverse


def norm_back(upstream, unit, inverse, gain):
    scaled = upstream * gain
    return inverse * (
        scaled
        - jnp.mean(scaled, axis=-1, keepdims=True)
        - unit * jnp.mean(scaled * unit, axis=-1, keepdims=True)
    )


def split_heads(rows):
    return rows.reshape(rows.shape[0], rows.shape[1] // HD, HD)


def layer_backward(pl, upstream, weights, stored):
    (w_qkv, w_out), (w_in, w_down), qv_bias, in_bias, gains, shifts = weights
    (
        unit_first, inverse_first, normed, queries, key_rows, value_rows, logsum, attended,
        unit_second, inverse_second, normed_second, hidden, active,
    ) = stored
    shift_down = jnp.sum(upstream, axis=0)
    upstream_low = low(upstream)
    grad_down = product(active, upstream_low, "sf,sd->fd")
    grad_active = product(upstream_low, w_down, "sd,fd->sf")
    unused, gelu_back = jax.vjp(functools.partial(jax.nn.gelu, approximate=False), hidden)
    grad_hidden = low(gelu_back(grad_active)[0])
    grad_in_bias = jnp.sum(wide(grad_hidden), axis=0)
    grad_in = product(grad_hidden, normed_second, "sf,sd->fd")
    grad_normed_second = sum_roles(pl, product(grad_hidden, w_in, "sf,fd->sd"))
    gain_second = jnp.sum(grad_normed_second * unit_second, axis=0)
    shift_second = jnp.sum(grad_normed_second, axis=0)
    grad_mid = upstream + norm_back(grad_normed_second, unit_second, inverse_second, gains[1])
    shift_out = jnp.sum(grad_mid, axis=0)
    mid_low = low(grad_mid)
    grad_out = product(attended, mid_low, "sa,sd->ad")
    grad_attended = low(product(mid_low, w_out, "sd,ad->sa"))
    query_heads, key_heads, value_heads = map(split_heads, (queries, key_rows, value_rows))
    factor = HD ** (-0.5)
    soft = jnp.exp(product(query_heads, key_heads, "qhd,khd->hqk") * factor - logsum)
    attended_heads = split_heads(grad_attended)
    flat = queries.shape
    grad_values = low(product(low(soft), attended_heads, "hqk,qhd->khd").reshape(flat))
    grad_soft = product(attended_heads, value_heads, "qhd,khd->hqk")
    grad_scores = low(soft * (grad_soft - jnp.sum(grad_soft * soft, axis=-1, keepdims=True)))
    grad_queries = low((product(grad_scores, key_heads, "hqk,khd->qhd") * factor).reshape(flat))
    grad_keys = low((product(grad_scores, query_heads, "hqk,qhd->khd") * factor).reshape(flat))
    grad_qv = jnp.stack([jnp.sum(wide(grad_queries), axis=0), jnp.sum(wide(grad_values), axis=0)])
    grad_qkv = [product(g, normed, "sa,sd->ad") for g in (grad_queries, grad_keys, grad_values)]
    partial_sum = (
        product(grad_queries, w_qkv[0], "sa,ad->sd")
        + product(grad_keys, w_qkv[1], "sa,ad->sd")
        + product(grad_values, w_qkv[2], "sa,ad->sd")
    )
    grad_normed_first = sum_roles(pl, partial_sum)
    gain_first = jnp.sum(grad_normed_first * unit_first, axis=0)
    shift_first = jnp.sum(grad_normed_first, axis=0)
    upstream = grad_mid + norm_back(grad_normed_first, unit_first, inverse_first, gains[0])
    attn_grads = jnp.stack(grad_qkv + [grad_out])
    mlp_grads = jnp.stack([grad_in, grad_down])
    by_feature = jnp.stack(
        [gain_first, gain_second, shift_first, shift_second, shift_out, shift_down]
    )
    return upstream, (attn_grads, mlp_grads, grad_qv, grad_in_bias, by_feature)


def pack_inputs(pl, w_qkv, w_out, w_in, w_down, qv_bias, in_bias, gains, shifts):
    fsdp = lax.axis_size("fsdp")
    cols = w_qkv.shape[2]
    groups = []
    small = []
    for l in range(LAYERS):
        attn = jnp.concatenate([w_qkv[l].transpose(0, 2, 1), w_out[l][None]]).reshape(4, TP, HD, cols)
        groups.append(attn.transpose(1, 0, 2, 3).reshape(TP, 256, cols))
        groups.append(w_in[l].T.reshape(TP, 256, cols))
        groups.append(w_down[l].reshape(TP, 256, cols))
        features = jnp.concatenate([gains[l], shifts[l]])
        features = jnp.broadcast_to(features[None], (TP, 6, cols))
        qv = qv_bias[l].reshape(2, TP, -1).transpose(1, 0, 2).reshape(TP, -1)
        units = jnp.concatenate([qv, in_bias[l].reshape(TP, -1)], axis=1)
        units = jnp.pad(units, ((0, 0), (0, cols - units.shape[1])))[:, None]
        small.append(jnp.pad(jnp.concatenate([features, units], axis=1), ((0, 0), (0, 9), (0, 0))))
    packed, extras = jnp.stack(groups), jnp.concatenate(small, axis=1)[None]
    if cols % 128 == 0:
        return packed, extras, True
    return gather_roles(pl, packed), gather_roles(pl, extras), False


def gather_roles(pl, pack):
    exchanged = [lax.dynamic_index_in_dim(pack, pl.role, 1, False)]
    for bits in (1, 2, 3):
        exchanged.append(pl.role_xor(lax.dynamic_index_in_dim(pack, pl.role ^ bits, 1, False), bits))
    return jnp.concatenate(by_xor(exchanged, pl.role), axis=-1)


def body(images, cotangent, w_qkv, w_out, w_in, w_down, qv_bias, in_bias, gains, shifts):
    fsdp, head = lax.axis_size("fsdp"), lax.axis_size("head")
    places = Places(fsdp, head)
    cols = w_qkv.shape[2]
    width, units = w_qkv.shape[3] // TP, w_in.shape[2] // TP
    tokens = images.shape[1]
    rows = -(-tokens // 32) * 32
    packed, extras, direct = pack_inputs(places, w_qkv, w_out, w_in, w_down, qv_bias, in_bias, gains, shifts)
    pad = ((0, rows - tokens), (0, 0))
    own_image = jnp.pad(lax.dynamic_index_in_dim(images, places.plane // 2, 0, False), pad)
    own_cot = jnp.pad(lax.dynamic_index_in_dim(cotangent, places.plane // 2, 0, False), pad)
    (
        whole, vec, normed, unit, inverse, qkv, att, lse, hidden, stream, chip, cots
    ) = forward_call(fsdp, head, tokens, rows, direct, own_image, own_cot, packed, extras)
    streams = []
    core = places.role & 1
    for i in range(2):
        total = low(wide(chip[i]) + wide(places.role_xor(chip[i], 2)))
        other = places.role_xor(total, 1)
        both = jnp.concatenate([jnp.where(core == 0, total, other), jnp.where(core == 0, other, total)], axis=1)
        streams.append((stream[i] + wide(both) + vec[1, 5])[:tokens])
    block_out = return_images(places, streams)
    upstreams = [wide(cots[i, :tokens]) for i in range(2)]
    parts = {}
    for l in reversed(range(LAYERS)):
        sums = None
        attn_w = whole[3 * l].reshape(4, 4, HD, D).transpose(1, 0, 2, 3).reshape(4, 256, D)
        weights = (
            (attn_w[:3], attn_w[3]),
            (whole[3 * l + 1].reshape(D, D), whole[3 * l + 2].reshape(D, D)),
            None, None, vec[l, 0:2], None,
        )
        for i in range(2):
            kept = (
                wide(unit[l, 0, i, :tokens]), inverse[l, 0, i, :tokens, 0:1], normed[l, 0, i, :tokens],
                qkv[l, i, :tokens, 0:256], qkv[l, i, :tokens, 256:512], qkv[l, i, :tokens, 512:768],
                lse[l, i, 0:4, :tokens][:, :, None], att[l, i, :tokens],
                wide(unit[l, 1, i, :tokens]), inverse[l, 1, i, :tokens, 0:1], normed[l, 1, i, :tokens],
                wide(hidden[l, i, :tokens]), low(jax.nn.gelu(wide(hidden[l, i, :tokens]), approximate=False)),
            )
            upstreams[i], grads = layer_backward(places, upstreams[i], weights, kept)
            sums = grads if sums is None else tuple(a + b for a, b in zip(sums, grads))
        mlp = scatter_group(places, sums[1].reshape(2, 4, 256, D))
        attn = scatter_group(places, sums[0].reshape(4, 4, HD, D))
        parts[l] = (attn, mlp, *sums[2:])
    input_grad = return_images(places, upstreams)

    attn = jnp.stack([parts[l][0] for l in range(LAYERS)])
    mlp = jnp.stack([parts[l][1] for l in range(LAYERS)])
    attn = attn.transpose(0, 2, 1, 3, 4).reshape(LAYERS, 4, TP * width, cols)
    mlp = mlp.transpose(0, 2, 1, 3, 4).reshape(LAYERS, 2, TP * units, cols)
    grad_qkv = attn[:, :3].transpose(0, 1, 3, 2)
    grad_out = attn[:, 3]
    grad_in = mlp[:, 0].transpose(0, 2, 1)
    grad_down = mlp[:, 1]

    by_feature = jnp.stack([parts[l][4] for l in range(LAYERS)])
    qv = jnp.stack([parts[l][2] for l in range(LAYERS)]).reshape(LAYERS, 2, head, width)
    inner = jnp.stack([parts[l][3] for l in range(LAYERS)]).reshape(LAYERS, head, units)
    qv_full = lax.dynamic_update_index_in_dim(
        jnp.zeros((LAYERS, 2, head, TP, width), jnp.float32), qv, places.role, 3
    )
    inner_full = lax.dynamic_update_index_in_dim(
        jnp.zeros((LAYERS, head, TP, units), jnp.float32), inner, places.role, 2
    )
    vector = jnp.concatenate([by_feature.reshape(-1) / TP, qv_full.reshape(-1), inner_full.reshape(-1)])
    vector = lax.psum(vector, AXES)
    f, h = lax.axis_index("fsdp"), lax.axis_index("head")
    a, b = by_feature.size, by_feature.size + qv_full.size
    by_feature = vector[:a].reshape(LAYERS, 6, fsdp, cols)
    by_feature = lax.dynamic_index_in_dim(by_feature, f, 2, False)
    qv = vector[a:b].reshape(LAYERS, 2, head, -1, fsdp)
    qv = lax.dynamic_index_in_dim(lax.dynamic_index_in_dim(qv, h, 2, False), f, 3, True)
    inner = vector[b:].reshape(LAYERS, head, -1, fsdp)
    inner = lax.dynamic_index_in_dim(lax.dynamic_index_in_dim(inner, h, 1, False), f, 2, True)
    return (
        block_out, input_grad, grad_qkv, grad_out, grad_in, grad_down,
        qv, inner, by_feature[:, :2], by_feature[:, 2:],
    )


def solution(mesh):
    placed = (
        P("fsdp", None, None),
        P("fsdp", None, None),
        P(None, None, "fsdp", "head"),
        P(None, "head", "fsdp"),
        P(None, "fsdp", "head"),
        P(None, "head", "fsdp"),
        P(None, None, "head", "fsdp"),
        P(None, "head", "fsdp"),
        P(None, None, "fsdp"),
        P(None, None, "fsdp"),
    )
    return jax.shard_map(
        body, mesh=mesh, in_specs=placed, out_specs=placed, check_vma=False
    )
```

```python
import functools
import math

import jax
import jax.numpy as jnp
from jax import lax
from jax.experimental import pallas as pl
from jax.experimental.pallas import tpu as pltpu
from jax.sharding import PartitionSpec as P

D = 1024
HD = 64
LAYERS = 2
TP = 4
HALF = D // 2
AXES = ("fsdp", "head")
MESH = pl.DeviceIdType.MESH
epsilon = 1e-06
f32, bf16 = jnp.float32, jnp.bfloat16


def dot(left, right, left_dim, right_dim):
    return lax.dot_general(
        left, right, (((left_dim,), (right_dim,)), ((), ())), preferred_element_type=f32
    )


def flip1(n):
    return n + 1 - 2 * (n % 2)


def flip2(n):
    return n + 2 - 4 * ((n // 2) % 2)


def flip(n, bits):
    if bits & 1:
        n = flip1(n)
    if bits & 2:
        n = flip2(n)
    return n


class Spot:
    def __init__(self, fsdp, head):
        self.blocks = fsdp // TP
        self.planes = head
        index = lax.axis_index("fsdp")
        self.index = index
        self.block, self.role, self.plane = index // TP, index % TP, lax.axis_index("head")
        self.core, self.side = self.role % 2, self.role // 2

    def at(self, block=None, role=None, plane=None):
        block = self.block if block is None else block
        role = self.role if role is None else role
        plane = self.plane if plane is None else plane
        return (block * TP + role, plane)

    def partners(self):
        found = [self.at(role=flip(self.role, o)) for o in (1, 2, 3)]
        found += [self.at(plane=flip(self.plane, o)) for o in (1, 2, 3)]
        found += [self.at(block=(self.block + s) % self.blocks) for s in range(1, self.blocks)]
        return found


def greet(partners):
    barrier = pltpu.get_barrier_semaphore()
    for partner in partners:
        pl.semaphore_signal(barrier, inc=1, device_id=partner, device_id_type=MESH)
    pl.semaphore_wait(barrier, len(partners))


def send(source, target, sems, where, device):
    return pltpu.make_async_remote_copy(
        src_ref=source,
        dst_ref=target,
        send_sem=sems[0].at[where],
        recv_sem=sems[1].at[where],
        device_id=device,
        device_id_type=MESH,
    )


def lanes(start, size):
    return pl.ds(pl.multiple_of(start, 128), size)


class Gather:
    def __init__(self, spot, packed, whole, role_sems, plane_sems, block_sems, base, local_sem, direct):
        self.spot, self.packed, self.whole, self.direct = spot, packed, whole, direct
        self.role_sems, self.plane_sems, self.block_sems = role_sems, plane_sems, block_sems
        self.base, self.local_sem = base, local_sem
        self.cols = D // spot.blocks // TP
        self.span = D // spot.blocks

    def piece(self, g, plane, block):
        return self.whole.at[g, plane, :, lanes(block * self.span, self.span)]

    def own(self, g):
        spot = self.spot
        if self.direct:
            return pltpu.make_async_copy(
                self.packed.at[g, spot.role],
                self.whole.at[g, spot.plane, :, lanes(spot.index * self.cols, self.cols)],
                self.local_sem.at[self.base + g],
            )
        return pltpu.make_async_copy(
            self.packed.at[g], self.piece(g, spot.plane, spot.block), self.local_sem.at[self.base + g]
        )

    def to_role(self, g, o):
        spot = self.spot
        other = flip(spot.role, o)
        return send(
            self.packed.at[g, other],
            self.whole.at[g, spot.plane, :, lanes(spot.index * self.cols, self.cols)],
            self.role_sems,
            (self.base + g, o),
            spot.at(role=other),
        )

    def from_role(self, g, o):
        spot = self.spot
        other = flip(spot.role, o)
        place = self.whole.at[
            g, spot.plane, :, lanes((spot.block * TP + other) * self.cols, self.cols)
        ]
        return send(place, place, self.role_sems, (self.base + g, o), spot.at(role=other))

    def to_plane(self, g, o):
        spot = self.spot
        place = self.piece(g, spot.plane, spot.block)
        return send(
            place, place, self.plane_sems, (self.base + g, o), spot.at(plane=flip(spot.plane, o))
        )

    def from_plane(self, g, o):
        spot = self.spot
        other = flip(spot.plane, o)
        place = self.piece(g, other, spot.block)
        return send(place, place, self.plane_sems, (self.base + g, o), spot.at(plane=other))

    def to_block(self, g, s, o):
        spot = self.spot
        place = self.piece(g, flip(spot.plane, o), spot.block)
        block = (spot.block + s) % spot.blocks
        return send(
            place, place, self.block_sems, (self.base + g, s, o), spot.at(block=block)
        )

    def from_block(self, g, s, o):
        spot = self.spot
        block = (spot.block + spot.blocks - s) % spot.blocks
        place = self.piece(g, flip(spot.plane, o), block)
        return send(
            place, place, self.block_sems, (self.base + g, s, o), spot.at(block=block)
        )

    def begin(self, g):
        self.own(g).start()
        if self.direct:
            for o in (1, 2, 3):
                self.to_role(g, o).start()

    def spread(self, g):
        self.own(g).wait()
        if self.direct:
            for o in (1, 2, 3):
                self.from_role(g, o).wait_recv()
        for o in (1, 2, 3):
            self.to_plane(g, o).start()
        for s in range(1, self.spot.blocks):
            self.to_block(g, s, 0).start()

    def relay(self, g, o):
        self.from_plane(g, o).wait_recv()
        for s in range(1, self.spot.blocks):
            self.to_block(g, s, o).start()

    def complete(self, g):
        for s in range(1, self.spot.blocks):
            for o in range(4):
                self.from_block(g, s, o).wait_recv()

    def drain(self, g):
        for o in (1, 2, 3):
            if self.direct:
                self.to_role(g, o).wait_send()
            self.to_plane(g, o).wait_send()
        for s in range(1, self.spot.blocks):
            for o in range(4):
                self.to_block(g, s, o).wait_send()


class Exchange:
    def __init__(self, spot, sent, core_in, chip, side_in, full, core_sems, side_sems, back_sems):
        self.spot = spot
        self.sent, self.core_in, self.chip, self.side_in, self.full = sent, core_in, chip, side_in, full
        self.core_sems, self.side_sems, self.back_sems = core_sems, side_sems, back_sems
        self.mine = lanes(spot.core * HALF, HALF)
        self.theirs = lanes((1 - spot.core) * HALF, HALF)

    def core_copy(self, i):
        return send(
            self.sent.at[i], self.core_in.at[i], self.core_sems, (i,),
            self.spot.at(role=flip1(self.spot.role)),
        )

    def side_copy(self, i, slot):
        return send(
            self.chip.at[i], self.side_in.at[i, slot], self.side_sems, (i, slot),
            self.spot.at(role=flip2(self.spot.role)),
        )

    def back_copy(self, i):
        place = self.full.at[i, :, self.mine]
        return send(place, place, self.back_sems, (i,), self.spot.at(role=flip1(self.spot.role)))

    def back_in(self, i):
        place = self.full.at[i, :, self.theirs]
        return send(place, place, self.back_sems, (i,), self.spot.at(role=flip1(self.spot.role)))

    def reduce(self, i, product, kept):
        rows = kept.shape[0]
        self.sent[i] = product(self.theirs).astype(bf16)
        self.core_copy(i).start()
        kept[...] = product(self.mine)
        copy = self.core_copy(i)
        copy.wait_recv()

        def add(c, carry):
            r = pl.ds(pl.multiple_of(c * 16, 16), 16)
            self.chip[i, r] = (kept[r] + self.core_in[i, r].astype(f32)).astype(bf16)
            return carry

        lax.fori_loop(0, rows // 16, add, 0, unroll=2)
        copy.wait_send()

    def finish(self, i, slot):
        copy = self.side_copy(i, slot)
        copy.wait_recv()
        rows = self.chip.shape[1]

        def add(c, carry):
            r = pl.ds(pl.multiple_of(c * 16, 16), 16)
            total = self.chip[i, r].astype(f32) + self.side_in[i, slot, r].astype(f32)
            self.full[i, r, self.mine] = total.astype(bf16)
            return carry

        lax.fori_loop(0, rows // 16, add, 0, unroll=2)
        self.back_copy(i).start()
        copy.wait_send()
        self.back_in(i).wait_recv()
        self.back_copy(i).wait_send()


def each_rows(rows, size, step, unroll=1):
    def one(c, carry):
        step(pl.ds(pl.multiple_of(c * size, size), size))
        return carry

    lax.fori_loop(0, rows // size, one, 0, unroll=unroll)


def forward_kernel(cfg, *refs):
    fsdp, head, tokens, rows, direct = cfg
    (
        own_image, own_cot, packed, extras,
        weights_out, vec_out, normed_out, unit_out, inverse_out, qkv_out, att_out, lse_out, hidden_out,
        stream_out, chip_out, cot_out,
        whole, extra, vec, pair, cots, stream, normed, unit, inverse, qkv, scores, soft, att_sum, att,
        row_scale, lse, lse_rows, hidden, low_hidden, active, kept,
        sent, core_in, chip, side_in, full,
        role_s, role_r, plane_s, plane_r, block_s, block_r, local_sem,
        core_s, core_r, side_s, side_r, back_s, back_r,
        share_s, share_r, store_sem,
    ) = refs
    spot = Spot(fsdp, head)
    groups = 3 * LAYERS
    greet(spot.partners())
    sems = ((role_s, role_r), (plane_s, plane_r), (block_s, block_r))
    small = Gather(spot, extras, extra, *sems, groups, local_sem, direct)
    large = Gather(spot, packed, whole, *sems, 0, local_sem, direct)
    exchange = Exchange(
        spot, sent, core_in, chip, side_in, full, (core_s, core_r), (side_s, side_r), (back_s, back_r)
    )
    owner = spot.core == spot.plane % 2
    x, other_x = spot.side, 1 - spot.side

    small.begin(0)
    large.begin(0)

    def share(source, held, n):
        across = send(
            source, held.at[x], (share_s, share_r), (n, 0), spot.at(role=flip2(spot.role))
        )
        across_in = send(
            held.at[other_x], held.at[other_x], (share_s, share_r), (n, 0), spot.at(role=flip2(spot.role))
        )
        down = [
            send(src, held.at[at], (share_s, share_r), (n, 1 + k), spot.at(role=flip1(spot.role)))
            for k, (src, at) in enumerate(((source, x), (held.at[other_x], other_x)))
        ]
        mine = pltpu.make_async_copy(source, held.at[x], store_sem.at[30 + n])
        return across, across_in, down, mine

    def share_begin(source, held, n):
        across, across_in, down, mine = share(source, held, n)

        @pl.when(owner)
        def _():
            across.start()
            mine.start()
            down[0].start()

    def share_end(source, held, n):
        across, across_in, down, mine = share(source, held, n)

        @pl.when(owner)
        def _():
            across_in.wait_recv()
            down[1].start()
            across.wait_send()
            mine.wait()
            down[0].wait_send()
            down[1].wait_send()

        @pl.when(jnp.logical_not(owner))
        def _():
            down[0].wait_recv()
            down[1].wait_recv()

    share_begin(own_image, pair, 0)
    for g in range(1, groups):
        large.begin(g)
    small.spread(0)
    large.spread(0)
    large.spread(1)
    for o in (1, 2, 3):
        small.relay(0, o)
    for o in (1, 2, 3):
        large.relay(0, o)
    large.spread(2)
    share_end(own_image, pair, 0)
    small.complete(0)

    cols = D // fsdp
    quarter = 64
    for l in range(LAYERS):
        vec[l, 0:6] = extra[0, 0, 16 * l : 16 * l + 16].astype(f32)[0:6]

        def selector(width, offset):
            c = lax.broadcasted_iota(jnp.int32, (D, width), 0)
            j = lax.broadcasted_iota(jnp.int32, (D, width), 1)
            return jnp.where((c // cols == j % fsdp) & (c % cols == offset + j // fsdp), 1.0, 0.0).astype(bf16)

        per = quarter // fsdp
        for plane in range(4):
            block = extra[0, plane, 16 * l : 16 * l + 16]
            vec[l, 6:7, plane * 256 : plane * 256 + 256] = dot(block, selector(256, 2 * per), 1, 0)[6:7]
            if plane % 2 == 0:
                following = extra[0, plane + 1, 16 * l : 16 * l + 16]
                for k in range(2):
                    pick = selector(quarter, k * per)
                    two = jnp.concatenate([dot(block, pick, 1, 0), dot(following, pick, 1, 0)], axis=1)
                    at = k * 256 + plane * quarter
                    vec[l, 7:8, at : at + 128] = two[6:7]
    store_vec = pltpu.make_async_copy(vec, vec_out, store_sem.at[28])
    store_vec.start()
    large.complete(0)

    lane_head = lax.broadcasted_iota(jnp.int32, (1, 256), 1) // HD
    key_bias = jnp.where(lax.broadcasted_iota(jnp.int32, (1, rows), 1) < tokens, 0.0, -1e30)

    def stores(l, n, i):
        return [
            pltpu.make_async_copy(normed.at[i], normed_out.at[l, n, i], store_sem.at[0 + i]),
            pltpu.make_async_copy(unit.at[i], unit_out.at[l, n, i], store_sem.at[2 + i]),
            pltpu.make_async_copy(inverse.at[i], inverse_out.at[l, n, i], store_sem.at[4 + i]),
        ]

    def norm(l, n, i, read):
        def step(r):
            v = read(r)
            stream[i, r] = v
            average = jnp.mean(v, axis=-1, keepdims=True)
            centred = v - average
            scale = lax.rsqrt(jnp.mean(centred * centred, axis=-1, keepdims=True) + epsilon)
            u = centred * scale
            unit[i, r] = u.astype(bf16)
            inverse[i, r] = jnp.broadcast_to(scale, (16, 128))
            normed[i, r] = (u * vec[l, n : n + 1] + vec[l, 2 + n : 3 + n]).astype(bf16)

        each_rows(rows, 16, step, unroll=2)
        for copy in stores(l, n, i):
            copy.start()

    def attn_stage(l, i):
        g = 3 * l

        @pl.when(l > 0)
        def _():
            exchange.finish(i, 1)
            for copy in stores(l - 1, 1, i):
                copy.wait()
            before = jnp.maximum(l - 1, 0)
            norm(l, 0, i, lambda r: stream[i, r] + full[i, r].astype(f32) + vec[before, 5:6])

        @pl.when(l == 0)
        def _():
            norm(l, 0, i, lambda r: pair[i, r].astype(f32))

        store_qkv = pltpu.make_async_copy(qkv, qkv_out.at[l, i], store_sem.at[6])
        store_att = pltpu.make_async_copy(att.at[i], att_out.at[l, i], store_sem.at[8 + i])
        store_lse = pltpu.make_async_copy(lse_rows.at[i], lse_out.at[l, i], store_sem.at[10 + i])

        @pl.when(l + i > 0)
        def _():
            store_qkv.wait()

        @pl.when(l > 0)
        def _():
            store_att.wait()
            store_lse.wait()

        for k in range(3):
            w = whole[g, :, k * HD : k * HD + HD].reshape(256, D)
            part = dot(normed[i], w, 1, 1)
            if k == 0:
                part = part + vec[l, 7:8, 0:256]
            if k == 2:
                part = part + vec[l, 7:8, 256:512]
            qkv[:, k * 256 : k * 256 + 256] = part.astype(bf16)
        store_qkv.start()

        att_sum[...] = jnp.zeros_like(att_sum)
        lse[...] = jnp.zeros_like(lse)

        def one_head(h, carry):
            mask = jnp.where(lane_head == h, 1.0, 0.0)
            q = qkv[:, 0:256] * (mask * HD ** (-0.5)).astype(bf16)
            scores[...] = dot(q, qkv[:, 256:512], 1, 1)
            here = lax.broadcasted_iota(jnp.int32, (1, 128), 1) == h

            def step(r):
                s = scores[r] + key_bias
                largest = jnp.max(s, axis=-1, keepdims=True)
                e = jnp.exp(s - largest)
                total = jnp.sum(e, axis=-1, keepdims=True)
                soft[r] = e.astype(bf16)
                row_scale[r] = jnp.broadcast_to(1.0 / total, (16, 128))
                lse[r] = jnp.where(here, largest + jnp.log(total), lse[r])

            each_rows(rows, 16, step, unroll=2)
            o = dot(soft[...], qkv[:, 512:768], 1, 0)
            scale = row_scale[...]
            att_sum[...] += o * jnp.concatenate([scale, scale], axis=1) * mask
            return carry

        lax.fori_loop(0, 4, one_head, 0)
        att[i] = att_sum[...].astype(bf16)
        lse_rows[i] = jnp.transpose(lse[...])[0:8]
        store_att.start()
        store_lse.start()
        exchange.reduce(
            i, lambda at: dot(att[i], whole[g, :, 192:256, at].reshape(256, HALF), 1, 0), kept
        )
        exchange.side_copy(i, 0).start()

    def mlp_stage(l, i):
        g = 3 * l
        exchange.finish(i, 0)
        for copy in stores(l, 0, i):
            copy.wait()
        norm(l, 1, i, lambda r: stream[i, r] + full[i, r].astype(f32) + vec[l, 4:5])
        store_hidden = pltpu.make_async_copy(low_hidden.at[i], hidden_out.at[l, i], store_sem.at[12 + i])

        @pl.when(l > 0)
        def _():
            store_hidden.wait()

        hidden[...] = dot(normed[i], whole[g + 1].reshape(D, D), 1, 1)

        def step(r):
            v = hidden[r] + vec[l, 6:7]
            low_hidden[i, r] = v.astype(bf16)
            active[r] = (v * (0.5 + 0.5 * lax.erf(v * (0.5**0.5)))).astype(bf16)

        each_rows(rows, 16, step, unroll=2)
        store_hidden.start()

        @pl.when(i == 0)
        def _():
            large.complete(g + 2)

        exchange.reduce(i, lambda at: dot(active[...], whole[g + 2, :, :, at].reshape(D, HALF), 1, 0), kept)

        @pl.when(l < LAYERS - 1)
        def _():
            exchange.side_copy(i, 1).start()

        @pl.when(l == LAYERS - 1)
        def _():
            pltpu.make_async_copy(chip.at[i], chip_out.at[i], store_sem.at[14 + i]).start()
            pltpu.make_async_copy(stream.at[i], stream_out.at[i], store_sem.at[16 + i]).start()

    def store_weights(g):
        return pltpu.make_async_copy(whole.at[g], weights_out.at[g], store_sem.at[18 + g])

    def one_layer(l, carry):
        g = 3 * l

        @pl.when(l > 0)
        def _():
            large.complete(g)

        attn_stage(l, 0)

        @pl.when(l == 0)
        def _():
            share_begin(own_cot, cots, 1)
            large.spread(3)

        for o in (1, 2, 3):
            large.relay(g + 1, o)
        attn_stage(l, 1)

        for o in (1, 2, 3):
            large.relay(g + 2, o)

        @pl.when(l == 0)
        def _():
            large.spread(4)

        large.complete(g + 1)
        mlp_stage(l, 0)

        @pl.when(l == 0)
        def _():
            for o in (1, 2, 3):
                large.relay(3, o)
            large.spread(5)

        mlp_stage(l, 1)
        for k in range(3):
            store_weights(g + k).start()
        return carry

    lax.fori_loop(0, LAYERS, one_layer, 0)
    share_end(own_cot, cots, 1)
    store_cots = pltpu.make_async_copy(cots, cot_out, store_sem.at[29])
    store_cots.start()
    last = LAYERS - 1
    for i in range(2):
        for copy in stores(last, 1, i):
            copy.wait()
        pltpu.make_async_copy(att.at[i], att_out.at[last, i], store_sem.at[8 + i]).wait()
        pltpu.make_async_copy(lse_rows.at[i], lse_out.at[last, i], store_sem.at[10 + i]).wait()
        pltpu.make_async_copy(low_hidden.at[i], hidden_out.at[last, i], store_sem.at[12 + i]).wait()
        pltpu.make_async_copy(chip.at[i], chip_out.at[i], store_sem.at[14 + i]).wait()
        pltpu.make_async_copy(stream.at[i], stream_out.at[i], store_sem.at[16 + i]).wait()
    pltpu.make_async_copy(qkv, qkv_out.at[last, 1], store_sem.at[6]).wait()
    store_vec.wait()
    store_cots.wait()

    def finish_group(g, carry):
        store_weights(g).wait()
        large.drain(g)
        return carry

    lax.fori_loop(0, groups, finish_group, 0)
    small.drain(0)


def forward_call(fsdp, head, tokens, rows, direct, own_image, own_cot, packed, extras):
    groups = 3 * LAYERS
    blocks = fsdp // TP
    anyspace = pl.BlockSpec(memory_space=pl.ANY)
    shape = jax.ShapeDtypeStruct
    dma = pltpu.SemaphoreType.DMA
    out_shape = (
        shape((groups, 4, 256, D), bf16),
        shape((LAYERS, 8, D), f32),
        shape((LAYERS, 2, 2, rows, D), bf16),
        shape((LAYERS, 2, 2, rows, D), bf16),
        shape((LAYERS, 2, 2, rows, 128), f32),
        shape((LAYERS, 2, rows, 768), bf16),
        shape((LAYERS, 2, rows, 256), bf16),
        shape((LAYERS, 2, 8, rows), f32),
        shape((LAYERS, 2, rows, D), bf16),
        shape((2, rows, D), f32),
        shape((2, rows, HALF), bf16),
        shape((2, rows, D), bf16),
    )
    scratch = [
        pltpu.VMEM((groups, 4, 256, D), bf16),
        pltpu.VMEM((1, 4, 32, D), bf16),
        pltpu.VMEM((LAYERS, 8, D), f32),
        pltpu.VMEM((2, rows, D), bf16),
        pltpu.VMEM((2, rows, D), bf16),
        pltpu.VMEM((2, rows, D), f32),
        pltpu.VMEM((2, rows, D), bf16),
        pltpu.VMEM((2, rows, D), bf16),
        pltpu.VMEM((2, rows, 128), f32),
        pltpu.VMEM((rows, 768), bf16),
        pltpu.VMEM((rows, rows), f32),
        pltpu.VMEM((rows, rows), bf16),
        pltpu.VMEM((rows, 256), f32),
        pltpu.VMEM((2, rows, 256), bf16),
        pltpu.VMEM((rows, 128), f32),
        pltpu.VMEM((rows, 128), f32),
        pltpu.VMEM((2, 8, rows), f32),
        pltpu.VMEM((rows, D), f32),
        pltpu.VMEM((2, rows, D), bf16),
        pltpu.VMEM((rows, D), bf16),
        pltpu.VMEM((rows, HALF), f32),
        pltpu.VMEM((2, rows, HALF), bf16),
        pltpu.VMEM((2, rows, HALF), bf16),
        pltpu.VMEM((2, rows, HALF), bf16),
        pltpu.VMEM((2, 2, rows, HALF), bf16),
        pltpu.VMEM((2, rows, D), bf16),
        dma((groups + 1, 4)), dma((groups + 1, 4)),
        dma((groups + 1, 4)), dma((groups + 1, 4)),
        dma((groups + 1, blocks, 4)), dma((groups + 1, blocks, 4)),
        dma((groups + 1,)),
        dma((2,)), dma((2,)),
        dma((2, 2)), dma((2, 2)),
        dma((2,)), dma((2,)),
        dma((2, 3)), dma((2, 3)),
        dma((32,)),
    ]
    return pl.pallas_call(
        functools.partial(forward_kernel, (fsdp, head, tokens, rows, direct)),
        out_shape=out_shape,
        in_specs=[anyspace] * 4,
        out_specs=tuple(anyspace for _ in out_shape),
        scratch_shapes=scratch,
        compiler_params=pltpu.CompilerParams(
            collective_id=0, has_side_effects=True, vmem_limit_bytes=60 << 20
        ),
        name="forward_layers",
    )(own_image, own_cot, packed, extras)


class Scatter:
    def __init__(self, spot, term, block_in, total, plane_in, mine, out, block_sems, plane_sems, role_sems, local_sem, block_free, plane_free, direct):
        self.spot, self.direct = spot, direct
        self.term, self.block_in, self.total = term, block_in, total
        self.plane_in, self.mine, self.out = plane_in, mine, out
        self.block_sems, self.plane_sems, self.role_sems, self.local_sem = block_sems, plane_sems, role_sems, local_sem
        self.block_free, self.plane_free = block_free, plane_free
        self.span = D // spot.blocks
        self.cols = self.span // TP

    def to_block(self, k, s):
        block = (self.spot.block + s) % self.spot.blocks
        return send(
            self.term.at[k, :, :, lanes(block * self.span, self.span)],
            self.block_in.at[k, s - 1],
            self.block_sems, (k, s - 1), self.spot.at(block=block),
        )

    def to_plane(self, k, o):
        other = flip(self.spot.plane, o)
        return send(
            self.total.at[k, other], self.plane_in.at[k, o - 1],
            self.plane_sems, (k, o - 1), self.spot.at(plane=other),
        )

    def to_role(self, g, k, o):
        other = flip(self.spot.role, o)
        return send(
            self.mine.at[k, :, lanes(other * self.cols, self.cols)], self.out.at[g, self.spot.role],
            self.role_sems, (g, o), self.spot.at(role=other),
        )

    def from_role(self, g, k, o):
        other = flip(self.spot.role, o)
        place = self.out.at[g, other]
        return send(place, place, self.role_sems, (g, o), self.spot.at(role=other))

    def keep(self, g, k):
        if self.direct:
            return pltpu.make_async_copy(
                self.mine.at[k, :, lanes(self.spot.role * self.cols, self.cols)],
                self.out.at[g, self.spot.role], self.local_sem.at[g],
            )
        return pltpu.make_async_copy(self.mine.at[k], self.out.at[g], self.local_sem.at[g])

    def send_terms(self, k, again):
        for s in range(1, self.spot.blocks):
            @pl.when(again)
            def _():
                pl.semaphore_wait(self.block_free.at[k, s - 1], 1)

            self.to_block(k, s).start()

    def before_terms(self, k, again):
        @pl.when(again)
        def _():
            for s in range(1, self.spot.blocks):
                self.to_block(k, s).wait_send()

    def sum_blocks(self, k, again, more):
        for s in range(1, self.spot.blocks):
            self.to_block(k, s).wait_recv()

        @pl.when(again)
        def _():
            for o in (1, 2, 3):
                self.to_plane(k, o).wait_send()

        units = self.term.shape[2]
        own = lanes(self.spot.block * self.span, self.span)
        for plane in range(4):
            def step(r):
                value = self.term[k, plane, r, own].astype(f32)
                for s in range(1, self.spot.blocks):
                    value = value + self.block_in[k, s - 1, plane, r].astype(f32)
                self.total[k, plane, r] = value.astype(bf16)

            each_rows(units, 16, step, unroll=2)

        @pl.when(more)
        def _():
            for s in range(1, self.spot.blocks):
                source = (self.spot.block + self.spot.blocks - s) % self.spot.blocks
                pl.semaphore_signal(
                    self.block_free.at[k, s - 1], inc=1, device_id=self.spot.at(block=source), device_id_type=MESH
                )

        for o in (1, 2, 3):
            @pl.when(again)
            def _():
                pl.semaphore_wait(self.plane_free.at[k, o - 1], 1)

            self.to_plane(k, o).start()

    def sum_planes(self, g, k, again, more):
        for o in (1, 2, 3):
            self.to_plane(k, o).wait_recv()
        units = self.term.shape[2]

        @pl.when(again)
        def _():
            before = jnp.minimum(g + 3, self.out.shape[0] - 1)
            self.keep(before, k).wait()
            if self.direct:
                for o in (1, 2, 3):
                    self.to_role(before, k, o).wait_send()

        def step(r):
            value = self.total[k, self.spot.plane, r].astype(f32)
            for o in (1, 2, 3):
                value = value + self.plane_in[k, o - 1, r].astype(f32)
            self.mine[k, r] = value.astype(bf16)

        each_rows(units, 16, step, unroll=2)

        @pl.when(more)
        def _():
            for o in (1, 2, 3):
                pl.semaphore_signal(
                    self.plane_free.at[k, o - 1], inc=1,
                    device_id=self.spot.at(plane=flip(self.spot.plane, o)), device_id_type=MESH,
                )

        self.keep(g, k).start()
        if self.direct:
            for o in (1, 2, 3):
                self.to_role(g, k, o).start()

    def finish(self, g, k):
        self.keep(g, k).wait()
        for s in range(1, self.spot.blocks):
            self.to_block(k, s).wait_send()
        for o in (1, 2, 3):
            self.to_plane(k, o).wait_send()
            if self.direct:
                self.to_role(g, k, o).wait_send()

    def arrive(self, g, k):
        if self.direct:
            for o in (1, 2, 3):
                self.from_role(g, k, o).wait_recv()


def backward_kernel(cfg, *refs):
    fsdp, head, tokens, rows, direct = cfg
    (
        weights_in, vec_in, normed_in, unit_in, inverse_in, qkv_in, att_in, lse_in, hidden_in,
        stream_in, chip_in, cot_in,
        out_pair, in_pair, grads, small_grads,
        weight, vec, up, up_low, hid, gh, normed, unit, inverse, qkv, att, lse, big, soft, low_scores, gab, along,
        kept, sent, core_in, chip, side_in, full, last_in, result, sums, unit_sums,
        term, block_in, total, plane_in, mine,
        small_term, small_block_in, small_total, small_plane_in, small_mine,
        core_s, core_r, side_s, side_r, back_s, back_r,
        block_s, block_r, plane_s, plane_r, role_s, role_r, local_sem, block_free, plane_free,
        small_block_s, small_block_r, small_plane_s, small_plane_r, small_role_s, small_role_r, small_local,
        small_block_free, small_plane_free,
        last_s, last_r, out_s, out_r, load_sem, weight_sem,
    ) = refs
    spot = Spot(fsdp, head)
    greet(spot.partners())
    exchange = Exchange(
        spot, sent, core_in, chip, side_in, full, (core_s, core_r), (side_s, side_r), (back_s, back_r)
    )
    scatter = Scatter(
        spot, term, block_in, total, plane_in, mine, grads, (block_s, block_r), (plane_s, plane_r),
        (role_s, role_r), local_sem, block_free, plane_free, direct,
    )
    small = Scatter(
        spot, small_term, small_block_in, small_total, small_plane_in, small_mine, small_grads,
        (small_block_s, small_block_r), (small_plane_s, small_plane_r), (small_role_s, small_role_r),
        small_local, small_block_free, small_plane_free, direct,
    )
    owner = spot.core == spot.plane % 2
    top = LAYERS - 1

    def load(source, target, n):
        return pltpu.make_async_copy(source, target, load_sem.at[n])

    def load_weight(l, k):
        return pltpu.make_async_copy(weights_in.at[3 * l + k], weight.at[k], weight_sem.at[k])

    load_vec = load(vec_in, vec, 0)
    load_cot = load(cot_in, up_low, 1)
    last_chip = qkv.at[:, :, 0:HALF]
    load_chip = load(chip_in, last_chip, 2)

    def load_hidden(l):
        return load(hidden_in.at[l], hid, 4)

    def load_normed(l, n):
        return load(normed_in.at[l, n], normed, 5)

    def load_unit(l, n):
        return [load(unit_in.at[l, n], unit, 6), load(inverse_in.at[l, n], inverse, 7)]

    def load_attn(l):
        return [load(qkv_in.at[l], qkv, 8), load(att_in.at[l], att, 9), load(lse_in.at[l], lse, 10)]

    load_chip.start()
    load_cot.start()
    load_weight(top, 2).start()
    load_hidden(top).start()
    load_vec.start()
    load_weight(top, 1).start()
    load_weight(top, 0).start()
    load_normed(top, 1).start()
    for copy in load_unit(top, 1):
        copy.start()

    last_copy = send(
        last_chip.at[1 - spot.side], last_in, (last_s, last_r), (0,), spot.at(role=flip2(spot.role))
    )
    half_copy = send(
        result.at[:, exchange.mine], result.at[:, exchange.mine], (last_s, last_r), (1,),
        spot.at(role=flip1(spot.role)),
    )
    half_in = send(
        result.at[:, exchange.theirs], result.at[:, exchange.theirs], (last_s, last_r), (1,),
        spot.at(role=flip1(spot.role)),
    )
    load_chip.wait()
    last_copy.start()

    sums[...] = jnp.zeros_like(sums)
    unit_sums[...] = jnp.zeros_like(unit_sums)
    load_cot.wait()

    def eights(v):
        return v[0:8] + v[8:16]

    for i in range(2):
        def widen(r):
            v = up_low[i, r].astype(f32)
            up[i, r] = v
            sums[(top + 1) * 6 + 5] += eights(v)

        each_rows(rows, 16, widen, unroll=2)
    load_vec.wait()

    def return_copies(n, pair_out):
        slot = spot.plane // 2
        source = result if n == 0 else up_low.at[spot.side]
        mine_copy = pltpu.make_async_copy(source, pair_out.at[slot], load_sem.at[12 + n])
        outs = [
            send(
                source, pair_out.at[slot], (out_s, out_r), (n, o), spot.at(plane=flip(spot.plane, o))
            )
            for o in (1, 2, 3)
        ]
        return mine_copy, outs

    def return_begin(n, pair_out):
        @pl.when(owner)
        def _():
            mine_copy, outs = return_copies(n, pair_out)
            mine_copy.start()
            for copy in outs:
                copy.start()

    def return_end(n, pair_out):
        for o in (1, 2, 3):
            other = flip(spot.plane, o)

            @pl.when(spot.core == other % 2)
            def _():
                place = pair_out.at[other // 2]
                send(place, place, (out_s, out_r), (n, o), spot.at(plane=other)).wait_recv()

        @pl.when(owner)
        def _():
            mine_copy, outs = return_copies(n, pair_out)
            mine_copy.wait()
            for copy in outs:
                copy.wait_send()

    def norm_back(l, n, i):
        def step(r):
            g = full[i, r].astype(f32)
            u = unit[i, r].astype(f32)
            scaled = g * vec[l, n : n + 1]
            first = jnp.mean(scaled, axis=-1, keepdims=True)
            second = jnp.mean(scaled * u, axis=-1, keepdims=True)
            scale = inverse[i, r, 0:1]
            v = up[i, r] + scale * (scaled - first - u * second)
            up[i, r] = v
            up_low[i, r] = v.astype(bf16)
            base = (l + 1) * 6
            sums[base + n] += eights(g * u)
            sums[base + 2 + n] += eights(g)
            sums[base + 4 if n == 1 else base - 1] += eights(v)

        each_rows(rows, 16, step, unroll=2)

    def mlp_stage(l, i):
        @pl.when(l < top)
        def _():
            exchange.finish(i, 1)
            norm_back(jnp.minimum(l + 1, top), 0, i)

        @pl.when(i == 0)
        def _():
            load_hidden(l).wait()
            load_weight(l, 2).wait()

        big[:, 0:D] = dot(up_low[i], weight[2].reshape(D, D), 1, 1)

        def step(r):
            v = hid[i, r].astype(f32)
            below = 0.5 + 0.5 * lax.erf(v * (0.5**0.5))
            slope = below + v * jnp.exp(-0.5 * v * v) * (1.0 / math.sqrt(2.0 * math.pi))
            hid[i, r] = (v * below).astype(bf16)
            low_grad = (big[r, 0:D] * slope).astype(bf16)
            gh[i, r] = low_grad
            unit_sums[l, 0] += eights(low_grad.astype(f32))

        each_rows(rows, 16, step, unroll=2)

        @pl.when(i == 0)
        def _():
            load_weight(l, 1).wait()

        exchange.reduce(i, lambda at: dot(gh[i], weight[1, :, :, at].reshape(D, HALF), 1, 0), kept)
        exchange.side_copy(i, 0).start()

    lane_head = lax.broadcasted_iota(jnp.int32, (1, 256), 1) // HD
    head_rows = jnp.where(
        lax.broadcasted_iota(jnp.int32, (16, 256), 1) // HD == lax.broadcasted_iota(jnp.int32, (16, 256), 0), 1.0, 0.0
    ).astype(bf16)

    def attn_stage(l, i):
        exchange.finish(i, 0)

        @pl.when(i == 0)
        def _():
            for copy in load_unit(l, 1):
                copy.wait()

        norm_back(l, 1, i)

        @pl.when(i == 0)
        def _():
            load_weight(l, 0).wait()
            for copy in load_attn(l):
                copy.wait()

        gab[...] = dot(up_low[i], weight[0, :, 192:256].reshape(256, D), 1, 1).astype(bf16)
        product = gab[...].astype(f32) * att[i].astype(f32)
        high = product.astype(bf16)
        rest = (product - high.astype(f32)).astype(bf16)
        along[...] = dot(head_rows, high, 1, 1) + dot(head_rows, rest, 1, 1)

        def one_head(h, carry):
            mask = jnp.where(lane_head == h, 1.0, 0.0)
            low_mask = mask.astype(bf16)
            q = qkv[i, :, 0:256] * low_mask
            big[:, 0:rows] = dot(qkv[i, :, 256:512], q * (HD ** (-0.5)), 1, 1)
            big[:, 640 : 640 + rows] = dot(qkv[i, :, 512:768], gab[...] * low_mask, 1, 1)
            lse_row = lse[i, pl.ds(h, 1)]
            along_row = along[pl.ds(h, 1)]

            def step(r):
                keys = lax.broadcasted_iota(jnp.int32, (16, 1), 0) + r.start
                p = jnp.exp(big[r, 0:rows] - lse_row)
                p = jnp.where(keys < tokens, p, 0.0)
                soft[r] = p.astype(bf16)
                low_scores[r] = (p * (big[r, 640 : 640 + rows] - along_row)).astype(bf16)

            each_rows(rows, 16, step, unroll=2)
            scale = HD ** (-0.5)
            grad_q = dot(low_scores[...], qkv[i, :, 256:512], 0, 0) * (mask * scale)
            grad_k = dot(low_scores[...], q, 1, 0) * (mask * scale)
            grad_v = dot(soft[...], gab[...], 1, 0) * mask
            for m, part in enumerate((grad_q, grad_k, grad_v)):
                part = part.astype(bf16)
                at = slice(m * 256, m * 256 + 256)

                @pl.when(h == 0)
                def _():
                    gh[i, :, at] = part

                @pl.when(h > 0)
                def _():
                    gh[i, :, at] = gh[i, :, at] + part

            return carry

        lax.fori_loop(0, 4, one_head, 0)

        def step(r):
            unit_sums[l, 1, :, 0:768] += eights(gh[i, r, 0:768].astype(f32))

        each_rows(rows, 16, step, unroll=2)

        def partial(at):
            terms = [
                dot(gh[i, :, m * 256 : m * 256 + 256], weight[0, :, m * HD : m * HD + HD, at].reshape(256, HALF), 1, 0)
                for m in range(3)
            ]
            return terms[0] + terms[1] + terms[2]

        exchange.reduce(i, partial, kept)
        exchange.side_copy(i, 1).start()

    span = D // spot.blocks

    def unit_term(k, left, right):
        def one(plane, carry):
            at = lanes(plane * 256, 256)
            for b in range(spot.blocks):
                to = slice(b * span, b * span + span)
                part = dot(left[0, :, at], right[0, :, to], 0, 0) + dot(left[1, :, at], right[1, :, to], 0, 0)
                term[k, plane, :, to] = part.astype(bf16)
            return carry

        lax.fori_loop(0, 4, one, 0)

    def attn_term():
        for m in range(4):
            left = gh if m < 3 else att
            right = normed if m < 3 else up_low
            at = slice(m * 256, m * 256 + 256) if m < 3 else slice(0, 256)
            for b in range(spot.blocks):
                to = slice(b * span, b * span + span)
                part = dot(left[0, :, at], right[0, :, to], 0, 0) + dot(left[1, :, at], right[1, :, to], 0, 0)
                term[0, :, m * HD : m * HD + HD, to] = part.astype(bf16).reshape(4, HD, span)

    def one_layer(step_index, carry):
        l = top - step_index
        again = l < top
        more = l > 0
        above = jnp.minimum(l + 1, top)
        mlp_stage(l, 0)

        @pl.when(again)
        def _():
            scatter.sum_blocks(1, above < top, above > 0)
            scatter.sum_planes(3 * above + 2, 2, above < top, above > 0)

        mlp_stage(l, 1)

        @pl.when(l == top)
        def _():
            last_copy.wait_recv()
            load_stream = load(stream_in.at[spot.side], big.at[:, 0:D], 11)
            load_stream.start()

            def add(r):
                v = last_chip[spot.side, r].astype(f32) + last_in[r].astype(f32)
                result[r, exchange.mine] = v.astype(bf16)

            each_rows(rows, 16, add, unroll=2)
            load_stream.wait()

            @pl.when(jnp.logical_not(owner))
            def _():
                half_copy.start()
                half_copy.wait_send()

            @pl.when(owner)
            def _():
                half_in.wait_recv()

                def whole_row(r):
                    v = big[r, 0:D] + result[r].astype(f32) + vec[top, 5:6]
                    result[r] = v.astype(bf16)

                each_rows(rows, 16, whole_row, unroll=2)

            last_copy.wait_send()
            for copy in load_attn(top):
                copy.start()
            return_begin(0, out_pair)

        @pl.when(again)
        def _():
            for copy in load_unit(l, 1):
                copy.start()

        scatter.before_terms(2, again)
        unit_term(2, hid, up_low)
        scatter.send_terms(2, again)
        load_normed(l, 1).wait()
        scatter.before_terms(1, again)
        unit_term(1, gh, normed)
        scatter.send_terms(1, again)

        @pl.when(more)
        def _():
            below = jnp.maximum(l - 1, 0)
            load_hidden(below).start()
            load_weight(below, 1).start()
            load_weight(below, 2).start()

        load_normed(l, 0).start()

        @pl.when(again)
        def _():
            scatter.sum_blocks(0, above < top, above > 0)
            scatter.sum_planes(3 * above + 1, 1, above < top, above > 0)

        attn_stage(l, 0)
        attn_stage(l, 1)
        for copy in load_unit(l, 0):
            copy.start()
        load_normed(l, 0).wait()
        scatter.before_terms(0, again)
        attn_term()
        scatter.send_terms(0, again)

        @pl.when(more)
        def _():
            below = jnp.maximum(l - 1, 0)
            load_weight(below, 0).start()
            load_normed(below, 1).start()
            for copy in load_attn(below):
                copy.start()

        @pl.when(again)
        def _():
            scatter.sum_planes(3 * above, 0, above < top, above > 0)

        scatter.sum_blocks(2, again, more)
        for copy in load_unit(l, 0):
            copy.wait()
        return carry

    lax.fori_loop(0, LAYERS, one_layer, 0)

    for i in range(2):
        exchange.finish(i, 1)
        norm_back(0, 0, i)

    return_begin(1, in_pair)

    cols = D // fsdp
    per = HD // fsdp
    for l in range(LAYERS):
        features = [jnp.sum(sums[(l + 1) * 6 + n], axis=0, keepdims=True) for n in range(6)]

        def placed(values, width, offset):
            c = lax.broadcasted_iota(jnp.int32, (D, width), 0)
            j = lax.broadcasted_iota(jnp.int32, (D, width), 1)
            pick = jnp.where((c // cols == j % fsdp) & (c % cols == offset + j // fsdp), 1.0, 0.0).astype(bf16)
            return dot(jnp.broadcast_to(values, (16, width)).astype(bf16), pick, 1, 1)[0:1]

        inner = jnp.sum(unit_sums[l, 0], axis=0, keepdims=True)
        qkv_sums = jnp.sum(unit_sums[l, 1], axis=0, keepdims=True)
        for plane in range(4):
            row = placed(inner[:, plane * 256 : plane * 256 + 256], 256, 2 * per)
            row = row + placed(qkv_sums[:, plane * HD : plane * HD + HD], HD, 0)
            row = row + placed(qkv_sums[:, 512 + plane * HD : 512 + plane * HD + HD], HD, per)
            block = jnp.concatenate(features + [row, jnp.zeros((9, D), f32)], axis=0)
            small_term[0, plane, 16 * l : 16 * l + 16] = block.astype(bf16)
    never = spot.plane < 0
    small.send_terms(0, never)
    scatter.sum_blocks(1, LAYERS > 1, False)
    scatter.sum_planes(2, 2, LAYERS > 1, False)
    scatter.sum_blocks(0, LAYERS > 1, False)
    small.sum_blocks(0, never, never)
    scatter.sum_planes(1, 1, LAYERS > 1, False)
    scatter.sum_planes(0, 0, LAYERS > 1, False)
    small.sum_planes(0, 0, never, never)
    for k in range(3):
        scatter.finish(k, k)
    small.finish(0, 0)
    for g in range(3 * LAYERS):
        scatter.arrive(g, g % 3)
    small.arrive(0, 0)
    return_end(0, out_pair)
    return_end(1, in_pair)


def backward_call(fsdp, head, tokens, rows, direct, kept):
    groups = 3 * LAYERS
    blocks = fsdp // TP
    span = D // blocks
    cols = span // TP
    anyspace = pl.BlockSpec(memory_space=pl.ANY)
    shape = jax.ShapeDtypeStruct
    dma, plain = pltpu.SemaphoreType.DMA, pltpu.SemaphoreType.REGULAR
    out_shape = (
        shape((2, rows, D), bf16),
        shape((2, rows, D), bf16),
        shape((groups, TP, 256, cols) if direct else (groups, 256, span), bf16),
        shape((1, TP, 32, cols) if direct else (1, 32, span), bf16),
    )
    scratch = [
        pltpu.VMEM((3, 4, 256, D), bf16),
        pltpu.VMEM((LAYERS, 8, D), f32),
        pltpu.VMEM((2, rows, D), f32),
        pltpu.VMEM((2, rows, D), bf16),
        pltpu.VMEM((2, rows, D), bf16),
        pltpu.VMEM((2, rows, D), bf16),
        pltpu.VMEM((2, rows, D), bf16),
        pltpu.VMEM((2, rows, D), bf16),
        pltpu.VMEM((2, rows, 128), f32),
        pltpu.VMEM((2, rows, 768), bf16),
        pltpu.VMEM((2, rows, 256), bf16),
        pltpu.VMEM((2, 8, rows), f32),
        pltpu.VMEM((rows, 640 + -(-rows // 128) * 128), f32),
        pltpu.VMEM((rows, rows), bf16),
        pltpu.VMEM((rows, rows), bf16),
        pltpu.VMEM((rows, 256), bf16),
        pltpu.VMEM((16, rows), f32),
        pltpu.VMEM((rows, HALF), f32),
        pltpu.VMEM((2, rows, HALF), bf16),
        pltpu.VMEM((2, rows, HALF), bf16),
        pltpu.VMEM((2, rows, HALF), bf16),
        pltpu.VMEM((2, 2, rows, HALF), bf16),
        pltpu.VMEM((2, rows, D), bf16),
        pltpu.VMEM((rows, HALF), bf16),
        pltpu.VMEM((rows, D), bf16),
        pltpu.VMEM((6 * (LAYERS + 1), 8, D), f32),
        pltpu.VMEM((LAYERS, 2, 8, D), f32),
    ]
    for slots, units in ((3, 256), (1, 32)):
        scratch += [
            pltpu.VMEM((slots, 4, units, D), bf16),
            pltpu.VMEM((slots, blocks - 1, 4, units, span), bf16),
            pltpu.VMEM((slots, 4, units, span), bf16),
            pltpu.VMEM((slots, 3, units, span), bf16),
            pltpu.VMEM((slots, units, span), bf16),
        ]
    scratch += [dma((2,)), dma((2,)), dma((2, 2)), dma((2, 2)), dma((2,)), dma((2,))]
    for slots, count in ((3, groups), (1, 1)):
        scratch += [
            dma((slots, blocks - 1)), dma((slots, blocks - 1)),
            dma((slots, 3)), dma((slots, 3)),
            dma((count, 4)), dma((count, 4)),
            dma((count,)),
            plain((slots, blocks - 1)), plain((slots, 3)),
        ]
    scratch += [dma((2,)), dma((2,)), dma((2, 4)), dma((2, 4)), dma((16,)), dma((3,))]
    return pl.pallas_call(
        functools.partial(backward_kernel, (fsdp, head, tokens, rows, direct)),
        out_shape=out_shape,
        in_specs=[anyspace] * len(kept),
        out_specs=tuple(anyspace for _ in out_shape),
        scratch_shapes=scratch,
        compiler_params=pltpu.CompilerParams(
            collective_id=1, has_side_effects=True, vmem_limit_bytes=63 << 20
        ),
        name="backward_layers",
    )(*kept)


class Places:
    def __init__(self, fsdp, head):
        self.fsdp, self.head = fsdp, head
        self.blocks = fsdp // TP
        index, plane = lax.axis_index("fsdp"), lax.axis_index("head")
        self.block, self.role, self.plane = index // TP, index % TP, plane

    def pairs(self, move, sends=None):
        found = []
        for block in range(self.blocks):
            for role in range(TP):
                for plane in range(self.head):
                    if sends is not None and not sends(block, role, plane):
                        continue
                    to_block, to_role, to_plane = move(block, role, plane)
                    found.append(
                        (
                            (block * TP + role) * self.head + plane,
                            (to_block * TP + to_role) * self.head + to_plane,
                        )
                    )
        return found

    def role_xor(self, v, bits, sends=None):
        return lax.ppermute(v, AXES, self.pairs(lambda b, r, p: (b, r ^ bits, p), sends))


def by_xor(parts, index):
    a, b, c, d = parts
    odd = (index & 1) == 1
    a, b = jnp.where(odd, b, a), jnp.where(odd, a, b)
    c, d = jnp.where(odd, d, c), jnp.where(odd, c, d)
    top = (index & 2) == 2
    return [jnp.where(top, c, a), jnp.where(top, d, b), jnp.where(top, a, c), jnp.where(top, b, d)]


def pack_inputs(pl, w_qkv, w_out, w_in, w_down, qv_bias, in_bias, gains, shifts):
    fsdp = lax.axis_size("fsdp")
    cols = w_qkv.shape[2]
    groups = []
    small = []
    for l in range(LAYERS):
        attn = jnp.concatenate([w_qkv[l].transpose(0, 2, 1), w_out[l][None]]).reshape(4, TP, HD, cols)
        groups.append(attn.transpose(1, 0, 2, 3).reshape(TP, 256, cols))
        groups.append(w_in[l].T.reshape(TP, 256, cols))
        groups.append(w_down[l].reshape(TP, 256, cols))
        features = jnp.concatenate([gains[l], shifts[l]])
        features = jnp.broadcast_to(features[None], (TP, 6, cols))
        qv = qv_bias[l].reshape(2, TP, -1).transpose(1, 0, 2).reshape(TP, -1)
        units = jnp.concatenate([qv, in_bias[l].reshape(TP, -1)], axis=1)
        units = jnp.pad(units, ((0, 0), (0, cols - units.shape[1])))[:, None]
        small.append(jnp.pad(jnp.concatenate([features, units], axis=1), ((0, 0), (0, 9), (0, 0))))
    packed, extras = jnp.stack(groups), jnp.concatenate(small, axis=1)[None]
    if cols % 128 == 0:
        return packed, extras, True
    return gather_roles(pl, packed), gather_roles(pl, extras), False


def gather_roles(pl, pack):
    exchanged = [lax.dynamic_index_in_dim(pack, pl.role, 1, False)]
    for bits in (1, 2, 3):
        exchanged.append(pl.role_xor(lax.dynamic_index_in_dim(pack, pl.role ^ bits, 1, False), bits))
    return jnp.concatenate(by_xor(exchanged, pl.role), axis=-1)


def scatter_roles(pl, mine):
    groups, units, width = mine.shape
    mine = mine.reshape(groups, units, TP, width // TP)
    exchanged = [lax.dynamic_index_in_dim(mine, pl.role, 2, False)]
    for bits in (1, 2, 3):
        exchanged.append(pl.role_xor(lax.dynamic_index_in_dim(mine, pl.role ^ bits, 2, False), bits))
    return jnp.stack(by_xor(exchanged, pl.role), axis=1)


def body(images, cotangent, w_qkv, w_out, w_in, w_down, qv_bias, in_bias, gains, shifts):
    fsdp, head = lax.axis_size("fsdp"), lax.axis_size("head")
    places = Places(fsdp, head)
    cols = w_qkv.shape[2]
    per = HD // fsdp
    tokens = images.shape[1]
    rows = -(-tokens // 32) * 32
    packed, extras, direct = pack_inputs(
        places, w_qkv, w_out, w_in, w_down, qv_bias, in_bias, gains, shifts
    )
    pad = ((0, rows - tokens), (0, 0))
    own_image = jnp.pad(lax.dynamic_index_in_dim(images, places.plane // 2, 0, False), pad)
    own_cot = jnp.pad(lax.dynamic_index_in_dim(cotangent, places.plane // 2, 0, False), pad)
    kept = forward_call(fsdp, head, tokens, rows, direct, own_image, own_cot, packed, extras)
    block_out, input_grad, grads, small = backward_call(fsdp, head, tokens, rows, direct, kept)
    if not direct:
        grads, small = scatter_roles(places, grads), scatter_roles(places, small)
    grads = grads.astype(f32).reshape(LAYERS, 3, TP, 256, cols)
    attn = grads[:, 0].reshape(LAYERS, TP, 4, HD, cols).transpose(0, 2, 1, 3, 4).reshape(LAYERS, 4, TP * HD, cols)
    small = small.astype(f32).reshape(TP, LAYERS, 16, cols)
    features = small[0, :, 0:6]
    units = small[:, :, 6].transpose(1, 0, 2)
    qv = units[:, :, 0 : 2 * per].reshape(LAYERS, TP, 2, per).transpose(0, 2, 1, 3).reshape(LAYERS, 2, TP * per, 1)
    inner = units[:, :, 2 * per : 6 * per].reshape(LAYERS, TP * 4 * per, 1)
    return (
        block_out[:, :tokens].astype(f32),
        input_grad[:, :tokens].astype(f32),
        attn[:, :3].transpose(0, 1, 3, 2),
        attn[:, 3],
        grads[:, 1].reshape(LAYERS, TP * 256, cols).transpose(0, 2, 1),
        grads[:, 2].reshape(LAYERS, TP * 256, cols),
        qv,
        inner,
        features[:, 0:2],
        features[:, 2:6],
    )


def solution(mesh):
    placed = (
        P("fsdp", None, None),
        P("fsdp", None, None),
        P(None, None, "fsdp", "head"),
        P(None, "head", "fsdp"),
        P(None, "fsdp", "head"),
        P(None, "head", "fsdp"),
        P(None, None, "head", "fsdp"),
        P(None, "head", "fsdp"),
        P(None, None, "fsdp"),
        P(None, None, "fsdp"),
    )
    return jax.shard_map(
        body, mesh=mesh, in_specs=placed, out_specs=placed, check_vma=False
    )
```

```python
import functools
import math

import jax
import jax.numpy as jnp
from jax import lax
from jax.experimental import pallas as pl
from jax.experimental.pallas import tpu as pltpu
from jax.sharding import PartitionSpec as P

D = 1024
HD = 64
LAYERS = 2
TP = 4
HALF = D // 2
AXES = ("fsdp", "head")
MESH = pl.DeviceIdType.MESH
epsilon = 1e-06
f32, bf16 = jnp.float32, jnp.bfloat16


def dot(left, right, left_dim, right_dim):
    return lax.dot_general(
        left, right, (((left_dim,), (right_dim,)), ((), ())), preferred_element_type=f32
    )


def flip1(n):
    return n + 1 - 2 * (n % 2)


def flip2(n):
    return n + 2 - 4 * ((n // 2) % 2)


def flip(n, bits):
    if bits & 1:
        n = flip1(n)
    if bits & 2:
        n = flip2(n)
    return n


class Spot:
    def __init__(self, fsdp, head):
        self.blocks = fsdp // TP
        self.planes = head
        index = lax.axis_index("fsdp")
        self.index = index
        self.block, self.role, self.plane = index // TP, index % TP, lax.axis_index("head")
        self.core, self.side = self.role % 2, self.role // 2

    def at(self, block=None, role=None, plane=None):
        block = self.block if block is None else block
        role = self.role if role is None else role
        plane = self.plane if plane is None else plane
        return (block * TP + role, plane)

    def partners(self):
        found = [self.at(role=flip(self.role, o)) for o in (1, 2, 3)]
        found += [self.at(plane=flip(self.plane, o)) for o in (1, 2, 3)]
        found += [self.at(block=(self.block + s) % self.blocks) for s in range(1, self.blocks)]
        return found


def greet(partners):
    barrier = pltpu.get_barrier_semaphore()
    for partner in partners:
        pl.semaphore_signal(barrier, inc=1, device_id=partner, device_id_type=MESH)
    pl.semaphore_wait(barrier, len(partners))


def send(source, target, sems, where, device):
    return pltpu.make_async_remote_copy(
        src_ref=source,
        dst_ref=target,
        send_sem=sems[0].at[where],
        recv_sem=sems[1].at[where],
        device_id=device,
        device_id_type=MESH,
    )


def lanes(start, size):
    return pl.ds(pl.multiple_of(start, 128), size)


class Gather:
    def __init__(self, spot, packed, whole, role_sems, plane_sems, block_sems, base, local_sem, direct):
        self.spot, self.packed, self.whole, self.direct = spot, packed, whole, direct
        self.role_sems, self.plane_sems, self.block_sems = role_sems, plane_sems, block_sems
        self.base, self.local_sem = base, local_sem
        self.cols = D // spot.blocks // TP
        self.span = D // spot.blocks

    def piece(self, g, plane, block):
        return self.whole.at[g, plane, :, lanes(block * self.span, self.span)]

    def own(self, g):
        spot = self.spot
        if self.direct:
            return pltpu.make_async_copy(
                self.packed.at[g, spot.role],
                self.whole.at[g, spot.plane, :, lanes(spot.index * self.cols, self.cols)],
                self.local_sem.at[self.base + g],
            )
        return pltpu.make_async_copy(
            self.packed.at[g], self.piece(g, spot.plane, spot.block), self.local_sem.at[self.base + g]
        )

    def to_role(self, g, o):
        spot = self.spot
        other = flip(spot.role, o)
        return send(
            self.packed.at[g, other],
            self.whole.at[g, spot.plane, :, lanes(spot.index * self.cols, self.cols)],
            self.role_sems,
            (self.base + g, o),
            spot.at(role=other),
        )

    def from_role(self, g, o):
        spot = self.spot
        other = flip(spot.role, o)
        place = self.whole.at[
            g, spot.plane, :, lanes((spot.block * TP + other) * self.cols, self.cols)
        ]
        return send(place, place, self.role_sems, (self.base + g, o), spot.at(role=other))

    def hop(self, g, d, up, taken):
        plane = self.spot.plane
        step = 1 if up else -1
        piece = plane - step * d if taken else plane - step * (d - 1)
        place = self.piece(g, piece, self.spot.block)
        other = plane - step if taken else plane + step
        return send(
            place, place, self.plane_sems, (self.base + g, d - 1 + (0 if up else 3)), self.spot.at(plane=other)
        )

    def has(self, d, up):
        return self.spot.plane >= d if up else self.spot.plane + d < self.spot.planes

    def goes(self, d, up):
        plane, last = self.spot.plane, self.spot.planes - 1
        if up:
            return jnp.logical_and(plane >= d, plane < last)
        return jnp.logical_and(plane + d <= last, plane > 0)

    def to_block(self, g, s, d, up, taken=False):
        spot = self.spot
        plane = spot.plane - d if up else spot.plane + d
        shift = spot.blocks - s if taken else s
        block = (spot.block + shift) % spot.blocks
        place = self.piece(g, plane, block if taken else spot.block)
        where = (self.base + g, s, d + (0 if up or d == 0 else 3))
        return send(place, place, self.block_sems, where, spot.at(block=block))

    def begin(self, g):
        self.own(g).start()
        if self.direct:
            for o in (1, 2, 3):
                self.to_role(g, o).start()

    def onward(self, g, d):
        for up in (True, False):
            if d < self.spot.planes - 1:
                @pl.when(self.goes(d, up))
                def _():
                    self.hop(g, d + 1, up, False).start()

    def spread(self, g):
        self.own(g).wait()
        if self.direct:
            for o in (1, 2, 3):
                self.from_role(g, o).wait_recv()
        self.onward(g, 0)
        for s in range(1, self.spot.blocks):
            self.to_block(g, s, 0, True).start()

    def relay(self, g, d):
        for up in (True, False):
            @pl.when(self.has(d, up))
            def _():
                self.hop(g, d, up, True).wait_recv()
        self.onward(g, d)
        for up in (True, False):
            @pl.when(self.has(d, up))
            def _():
                for s in range(1, self.spot.blocks):
                    self.to_block(g, s, d, up).start()

    def complete(self, g):
        for s in range(1, self.spot.blocks):
            self.to_block(g, s, 0, True, True).wait_recv()
            for d in (1, 2, 3):
                for up in (True, False):
                    @pl.when(self.has(d, up))
                    def _():
                        self.to_block(g, s, d, up, True).wait_recv()

    def drain(self, g):
        for d in (0, 1, 2, 3):
            if self.direct and d > 0:
                self.to_role(g, d).wait_send()
            for up in (True, False):
                if d < 3:
                    @pl.when(self.goes(d, up))
                    def _():
                        self.hop(g, d + 1, up, False).wait_send()
                if d > 0:
                    @pl.when(self.has(d, up))
                    def _():
                        for s in range(1, self.spot.blocks):
                            self.to_block(g, s, d, up).wait_send()
        for s in range(1, self.spot.blocks):
            self.to_block(g, s, 0, True).wait_send()


class Exchange:
    def __init__(self, spot, sent, core_in, chip, side_in, full, core_sems, side_sems, back_sems):
        self.spot = spot
        self.sent, self.core_in, self.chip, self.side_in, self.full = sent, core_in, chip, side_in, full
        self.core_sems, self.side_sems, self.back_sems = core_sems, side_sems, back_sems
        self.mine = lanes(spot.core * HALF, HALF)
        self.theirs = lanes((1 - spot.core) * HALF, HALF)

    def core_copy(self, i):
        return send(
            self.sent.at[i], self.core_in.at[i], self.core_sems, (i,),
            self.spot.at(role=flip1(self.spot.role)),
        )

    def side_copy(self, i, slot):
        return send(
            self.chip.at[i], self.side_in.at[i, slot], self.side_sems, (i, slot),
            self.spot.at(role=flip2(self.spot.role)),
        )

    def back_copy(self, i):
        place = self.full.at[i, :, self.mine]
        return send(place, place, self.back_sems, (i,), self.spot.at(role=flip1(self.spot.role)))

    def back_in(self, i):
        place = self.full.at[i, :, self.theirs]
        return send(place, place, self.back_sems, (i,), self.spot.at(role=flip1(self.spot.role)))

    def reduce(self, i, product, kept):
        self.sent[i] = product(self.theirs).astype(bf16)
        self.core_copy(i).start()
        kept[...] = product(self.mine)
        copy = self.core_copy(i)
        copy.wait_recv()
        self.chip[i] = (kept[...] + self.core_in[i].astype(f32)).astype(bf16)
        copy.wait_send()

    def finish(self, i, slot):
        copy = self.side_copy(i, slot)
        copy.wait_recv()
        total = self.chip[i].astype(f32) + self.side_in[i, slot].astype(f32)
        self.full[i, :, self.mine] = total.astype(bf16)
        self.back_copy(i).start()
        copy.wait_send()
        self.back_in(i).wait_recv()
        self.back_copy(i).wait_send()


def each_rows(rows, size, step, unroll=1):
    def one(c, carry):
        step(pl.ds(pl.multiple_of(c * size, size), size))
        return carry

    lax.fori_loop(0, rows // size, one, 0, unroll=unroll)


def unit_picks(held, fsdp):
    cols = D // fsdp
    per = HD // fsdp
    for first, count, offset in ((0, 256, 2 * per), (256, HD, 0), (256 + HD, HD, per)):
        unit = lax.broadcasted_iota(jnp.int32, (count, D), 0)
        place = lax.broadcasted_iota(jnp.int32, (count, D), 1)
        bits = fsdp.bit_length() - 1
        wanted = (unit & (fsdp - 1)) * cols + offset + (unit >> bits)
        held[first : first + count] = jnp.where(place == wanted, 1.0, 0.0).astype(bf16)


def forward_kernel(cfg, *refs):
    fsdp, head, tokens, rows, direct = cfg
    (
        own_image, own_cot, packed, extras,
        weights_out, vec_out, normed_out, unit_out, inverse_out, qkv_out, att_out, lse_out, hidden_out,
        stream_out, chip_out, cot_out,
        whole, extra, vec, pair, cots, stream, normed, unit, inverse, qkv, scores, soft, att_sum, att,
        values, lse_rows, low_hidden, active, kept,
        sent, core_in, chip, side_in, full,
        role_s, role_r, plane_s, plane_r, block_s, block_r, local_sem,
        core_s, core_r, side_s, side_r, back_s, back_r,
        share_s, share_r, store_sem,
    ) = refs
    spot = Spot(fsdp, head)
    groups = 3 * LAYERS
    greet(spot.partners())
    sems = ((role_s, role_r), (plane_s, plane_r), (block_s, block_r))
    small = Gather(spot, extras, extra, *sems, groups, local_sem, direct)
    large = Gather(spot, packed, whole, *sems, 0, local_sem, direct)
    exchange = Exchange(
        spot, sent, core_in, chip, side_in, full, (core_s, core_r), (side_s, side_r), (back_s, back_r)
    )
    owner = spot.core == spot.plane % 2
    x, other_x = spot.side, 1 - spot.side

    small.begin(0)
    large.begin(0)

    def share(source, held, n):
        across = send(
            source, held.at[x], (share_s, share_r), (n, 0), spot.at(role=flip2(spot.role))
        )
        across_in = send(
            held.at[other_x], held.at[other_x], (share_s, share_r), (n, 0), spot.at(role=flip2(spot.role))
        )
        down = [
            send(src, held.at[at], (share_s, share_r), (n, 1 + k), spot.at(role=flip1(spot.role)))
            for k, (src, at) in enumerate(((source, x), (held.at[other_x], other_x)))
        ]
        mine = pltpu.make_async_copy(source, held.at[x], store_sem.at[30 + n])
        return across, across_in, down, mine

    def share_begin(source, held, n):
        across, across_in, down, mine = share(source, held, n)

        @pl.when(owner)
        def _():
            across.start()
            mine.start()
            down[0].start()

    def share_end(source, held, n):
        across, across_in, down, mine = share(source, held, n)

        @pl.when(owner)
        def _():
            across_in.wait_recv()
            down[1].start()
            across.wait_send()
            mine.wait()
            down[0].wait_send()
            down[1].wait_send()

        @pl.when(jnp.logical_not(owner))
        def _():
            down[0].wait_recv()
            down[1].wait_recv()

    share_begin(own_image, pair, 0)
    for g in range(1, groups):
        large.begin(g)
    small.spread(0)
    large.spread(0)
    small.relay(0, 1)
    large.relay(0, 1)
    large.spread(1)
    small.relay(0, 2)
    large.relay(0, 2)
    small.relay(0, 3)
    large.relay(0, 3)
    large.relay(1, 1)
    large.spread(2)
    share_end(own_image, pair, 0)
    small.complete(0)

    unit_picks(active, fsdp)
    for l in range(LAYERS):
        vec[l, 0:6] = extra[0, 0, 16 * l : 16 * l + 16].astype(f32)[0:6]
        for plane in range(4):
            units = dot(extra[0, plane, 16 * l : 16 * l + 16], active[0:384], 1, 1)[6:7]
            vec[l, 6:7, plane * 256 : plane * 256 + 256] = units[:, 0:256]
            if plane % 2 == 0:
                before = units
            else:
                for k in range(2):
                    at = slice(256 + k * HD, 256 + k * HD + HD)
                    to = k * 256 + (plane - 1) * HD
                    vec[l, 7:8, to : to + 128] = jnp.concatenate([before[:, at], units[:, at]], axis=1)
    store_vec = pltpu.make_async_copy(vec, vec_out, store_sem.at[28])
    store_vec.start()
    large.complete(0)

    lane_head = lax.broadcasted_iota(jnp.int32, (1, 256), 1) // HD

    def stores(l, n, i):
        return [
            pltpu.make_async_copy(normed.at[i], normed_out.at[l, n, i], store_sem.at[0 + i]),
            pltpu.make_async_copy(unit.at[i], unit_out.at[l, n, i], store_sem.at[2 + i]),
            pltpu.make_async_copy(inverse.at[i], inverse_out.at[l, n, i], store_sem.at[4 + i]),
        ]

    def norm(l, n, i, v):
        stream[i] = v
        average = jnp.mean(v, axis=-1, keepdims=True)
        centred = v - average
        scale = lax.rsqrt(jnp.mean(centred * centred, axis=-1, keepdims=True) + epsilon)
        u = centred * scale
        unit[i] = u.astype(bf16)
        inverse[i] = jnp.broadcast_to(scale, (rows, 128))
        normed[i] = (u * vec[l, n : n + 1] + vec[l, 2 + n : 3 + n]).astype(bf16)
        for copy in stores(l, n, i):
            copy.start()

    def attn_stage(l, i):
        g = 3 * l

        @pl.when(l > 0)
        def _():
            exchange.finish(i, 1)
            for copy in stores(l - 1, 1, i):
                copy.wait()
            before = jnp.maximum(l - 1, 0)
            norm(l, 0, i, stream[i] + full[i].astype(f32) + vec[before, 5:6])

        @pl.when(l == 0)
        def _():
            norm(l, 0, i, pair[i].astype(f32))

        store_qkv = pltpu.make_async_copy(qkv, qkv_out.at[l, i], store_sem.at[6])
        store_att = pltpu.make_async_copy(att.at[i], att_out.at[l, i], store_sem.at[8 + i])
        store_lse = pltpu.make_async_copy(lse_rows.at[i], lse_out.at[l, i], store_sem.at[10 + i])

        @pl.when(l + i > 0)
        def _():
            store_qkv.wait()

        @pl.when(l > 0)
        def _():
            store_att.wait()
            store_lse.wait()

        for k in range(3):
            w = whole[g, :, k * HD : k * HD + HD].reshape(256, D)
            part = dot(normed[i], w, 1, 1)
            if k == 0:
                part = part + vec[l, 7:8, 0:256]
            if k == 2:
                part = part + vec[l, 7:8, 256:512]
                values[...] = jnp.transpose(part).astype(bf16)
            qkv[:, k * 256 : k * 256 + 256] = part.astype(bf16)
        store_qkv.start()
        edge = tokens // 16 * 16
        late = lax.broadcasted_iota(jnp.int32, (rows - edge, 1), 0) + edge >= tokens

        def one_head(h, carry):
            low_mask = jnp.where(lane_head == h, HD ** (-0.5), 0.0).astype(bf16)
            scores[...] = dot(qkv[:, 256:512], qkv[:, 0:256] * low_mask, 1, 1)
            scores[edge:rows] = jnp.where(late, -1e30, scores[edge:rows])
            largest = jnp.max(scores[...], axis=0, keepdims=True)
            e = jnp.exp(scores[...] - largest)
            total = jnp.sum(e, axis=0, keepdims=True)
            soft[...] = e.astype(bf16)
            lse_rows[i, pl.ds(h, 1)] = largest + jnp.log(total)
            at = pl.ds(pl.multiple_of(h * HD, HD), HD)
            att_sum[at] = dot(values[at], soft[...], 1, 0) * (1.0 / total)
            return carry

        lax.fori_loop(0, 4, one_head, 0)
        att[i] = jnp.transpose(att_sum[...]).astype(bf16)
        store_att.start()
        store_lse.start()
        exchange.reduce(
            i, lambda at: dot(att[i], whole[g, :, 192:256, at].reshape(256, HALF), 1, 0), kept
        )
        exchange.side_copy(i, 0).start()

    def mlp_stage(l, i):
        g = 3 * l
        exchange.finish(i, 0)
        for copy in stores(l, 0, i):
            copy.wait()
        norm(l, 1, i, stream[i] + full[i].astype(f32) + vec[l, 4:5])
        store_hidden = pltpu.make_async_copy(low_hidden.at[i], hidden_out.at[l, i], store_sem.at[12 + i])

        @pl.when(l > 0)
        def _():
            store_hidden.wait()

        for k in range(4):
            at = slice(k * 256, k * 256 + 256)
            v = dot(normed[i], whole[g + 1, k], 1, 1) + vec[l, 6:7, at]
            low_hidden[i, :, at] = v.astype(bf16)
            active[:, at] = (v * (0.5 + 0.5 * lax.erf(v * (0.5**0.5)))).astype(bf16)
        store_hidden.start()

        @pl.when(i == 0)
        def _():
            large.complete(g + 2)

        exchange.reduce(i, lambda at: dot(active[...], whole[g + 2, :, :, at].reshape(D, HALF), 1, 0), kept)

        @pl.when(l < LAYERS - 1)
        def _():
            exchange.side_copy(i, 1).start()

        @pl.when(l == LAYERS - 1)
        def _():
            pltpu.make_async_copy(chip.at[i], chip_out.at[i], store_sem.at[14 + i]).start()
            pltpu.make_async_copy(stream.at[i], stream_out.at[i], store_sem.at[16 + i]).start()

    def store_weights(g):
        return pltpu.make_async_copy(whole.at[g], weights_out.at[g], store_sem.at[18 + g])

    def one_layer(l, carry):
        g = 3 * l

        @pl.when(l > 0)
        def _():
            large.complete(g)

        attn_stage(l, 0)

        @pl.when(l == 0)
        def _():
            share_begin(own_cot, cots, 1)
            large.relay(1, 2)
            large.relay(2, 1)
            large.spread(3)

        @pl.when(l > 0)
        def _():
            large.relay(5, 3)

        attn_stage(l, 1)

        @pl.when(l == 0)
        def _():
            large.relay(1, 3)
            large.relay(2, 2)
            large.relay(3, 1)
            large.spread(4)
            large.relay(2, 3)

        large.complete(g + 1)
        mlp_stage(l, 0)

        @pl.when(l == 0)
        def _():
            large.relay(3, 2)
            large.relay(4, 1)
            large.spread(5)
            large.relay(3, 3)

        mlp_stage(l, 1)

        @pl.when(l == 0)
        def _():
            large.relay(4, 2)
            large.relay(5, 1)
            large.relay(4, 3)
            large.relay(5, 2)

        for k in range(3):
            store_weights(g + k).start()
        return carry

    lax.fori_loop(0, LAYERS, one_layer, 0)
    share_end(own_cot, cots, 1)
    store_cots = pltpu.make_async_copy(cots, cot_out, store_sem.at[29])
    store_cots.start()
    last = LAYERS - 1
    for i in range(2):
        for copy in stores(last, 1, i):
            copy.wait()
        pltpu.make_async_copy(att.at[i], att_out.at[last, i], store_sem.at[8 + i]).wait()
        pltpu.make_async_copy(lse_rows.at[i], lse_out.at[last, i], store_sem.at[10 + i]).wait()
        pltpu.make_async_copy(low_hidden.at[i], hidden_out.at[last, i], store_sem.at[12 + i]).wait()
        pltpu.make_async_copy(chip.at[i], chip_out.at[i], store_sem.at[14 + i]).wait()
        pltpu.make_async_copy(stream.at[i], stream_out.at[i], store_sem.at[16 + i]).wait()
    pltpu.make_async_copy(qkv, qkv_out.at[last, 1], store_sem.at[6]).wait()
    store_vec.wait()
    store_cots.wait()

    def finish_group(g, carry):
        store_weights(g).wait()
        large.drain(g)
        return carry

    lax.fori_loop(0, groups, finish_group, 0)
    small.drain(0)


def forward_call(fsdp, head, tokens, rows, direct, own_image, own_cot, packed, extras):
    groups = 3 * LAYERS
    blocks = fsdp // TP
    anyspace = pl.BlockSpec(memory_space=pl.ANY)
    shape = jax.ShapeDtypeStruct
    dma = pltpu.SemaphoreType.DMA
    out_shape = (
        shape((groups, 4, 256, D), bf16),
        shape((LAYERS, 8, D), f32),
        shape((LAYERS, 2, 2, rows, D), bf16),
        shape((LAYERS, 2, 2, rows, D), bf16),
        shape((LAYERS, 2, 2, rows, 128), f32),
        shape((LAYERS, 2, rows, 768), bf16),
        shape((LAYERS, 2, rows, 256), bf16),
        shape((LAYERS, 2, 8, rows), f32),
        shape((LAYERS, 2, rows, D), bf16),
        shape((2, rows, D), f32),
        shape((2, rows, HALF), bf16),
        shape((2, rows, D), bf16),
    )
    scratch = [
        pltpu.VMEM((groups, 4, 256, D), bf16),
        pltpu.VMEM((1, 4, 32, D), bf16),
        pltpu.VMEM((LAYERS, 8, D), f32),
        pltpu.VMEM((2, rows, D), bf16),
        pltpu.VMEM((2, rows, D), bf16),
        pltpu.VMEM((2, rows, D), f32),
        pltpu.VMEM((2, rows, D), bf16),
        pltpu.VMEM((2, rows, D), bf16),
        pltpu.VMEM((2, rows, 128), f32),
        pltpu.VMEM((rows, 768), bf16),
        pltpu.VMEM((rows, rows), f32),
        pltpu.VMEM((rows, rows), bf16),
        pltpu.VMEM((256, rows), f32),
        pltpu.VMEM((2, rows, 256), bf16),
        pltpu.VMEM((256, rows), bf16),
        pltpu.VMEM((2, 8, rows), f32),
        pltpu.VMEM((2, rows, D), bf16),
        pltpu.VMEM((rows, D), bf16),
        pltpu.VMEM((rows, HALF), f32),
        pltpu.VMEM((2, rows, HALF), bf16),
        pltpu.VMEM((2, rows, HALF), bf16),
        pltpu.VMEM((2, rows, HALF), bf16),
        pltpu.VMEM((2, 2, rows, HALF), bf16),
        pltpu.VMEM((2, rows, D), bf16),
        dma((groups + 1, 4)), dma((groups + 1, 4)),
        dma((groups + 1, 6)), dma((groups + 1, 6)),
        dma((groups + 1, blocks, 7)), dma((groups + 1, blocks, 7)),
        dma((groups + 1,)),
        dma((2,)), dma((2,)),
        dma((2, 2)), dma((2, 2)),
        dma((2,)), dma((2,)),
        dma((2, 3)), dma((2, 3)),
        dma((32,)),
    ]
    return pl.pallas_call(
        functools.partial(forward_kernel, (fsdp, head, tokens, rows, direct)),
        out_shape=out_shape,
        in_specs=[anyspace] * 4,
        out_specs=tuple(anyspace for _ in out_shape),
        scratch_shapes=scratch,
        compiler_params=pltpu.CompilerParams(
            collective_id=0, has_side_effects=True, vmem_limit_bytes=60 << 20
        ),
        name="forward_layers",
    )(own_image, own_cot, packed, extras)


class Scatter:
    def __init__(self, spot, count, term, block_in, total, plane_in, mine, out, block_sems, plane_sems, role_sems, local_sem, block_free, plane_free, direct):
        self.spot, self.count, self.direct = spot, count, direct
        self.term, self.block_in, self.total = term, block_in, total
        self.plane_in, self.mine, self.out = plane_in, mine, out
        self.block_sems, self.plane_sems, self.role_sems, self.local_sem = block_sems, plane_sems, role_sems, local_sem
        self.block_free, self.plane_free = block_free, plane_free
        self.span = D // spot.blocks
        self.cols = self.span // TP
        self.own = lanes(spot.block * self.span, self.span)

    def slot(self, n):
        return n % self.term.shape[0]

    def third(self, n):
        return n % self.total.shape[0]

    def to_block(self, n, s):
        block = (self.spot.block + s) % self.spot.blocks
        a = self.slot(n)
        return send(
            self.term.at[a, :, :, lanes(block * self.span, self.span)],
            self.block_in.at[a, s - 1],
            self.block_sems, (a, s - 1), self.spot.at(block=block),
        )

    def along(self, n, plane, up):
        planes = self.spot.planes
        a, c = self.slot(n), self.third(n)
        first, number = (plane + 1, planes - 1 - plane) if up else (0, plane)
        way = 0 if up else 1
        return send(
            self.total.at[c, first : first + number], self.plane_in.at[a, way, 0:number],
            self.plane_sems, (c, way), self.spot.at(plane=plane + (1 if up else -1)),
        )

    def to_role(self, n, o):
        other = flip(self.spot.role, o)
        g = self.count - 1 - n
        return send(
            self.mine.at[self.slot(n), :, lanes(other * self.cols, self.cols)], self.out.at[g, self.spot.role],
            self.role_sems, (g, o), self.spot.at(role=other),
        )

    def from_role(self, g, o):
        other = flip(self.spot.role, o)
        place = self.out.at[g, other]
        return send(place, place, self.role_sems, (g, o), self.spot.at(role=other))

    def keep(self, n):
        g = self.count - 1 - n
        if self.direct:
            return pltpu.make_async_copy(
                self.mine.at[self.slot(n), :, lanes(self.spot.role * self.cols, self.cols)],
                self.out.at[g, self.spot.role], self.local_sem.at[g],
            )
        return pltpu.make_async_copy(self.mine.at[self.slot(n)], self.out.at[g], self.local_sem.at[g])

    def before_terms(self, n):
        @pl.when(n >= 2)
        def _():
            for s in range(1, self.spot.blocks):
                self.to_block(n - 2, s).wait_send()

    def send_terms(self, n):
        for s in range(1, self.spot.blocks):
            @pl.when(n >= 2)
            def _():
                pl.semaphore_wait(self.block_free.at[self.slot(n), s - 1], 1)

            self.to_block(n, s).start()

    def pass_on(self, n, plane, up):
        @pl.when(n >= 2)
        def _():
            pl.semaphore_wait(self.plane_free.at[self.slot(n), 0 if up else 1], 1)

        self.along(n, plane, up).start()

    def sent_along(self, n):
        for plane in range(self.spot.planes):
            @pl.when(self.spot.plane == plane)
            def _():
                if plane < self.spot.planes - 1:
                    self.along(n, plane, True).wait_send()
                if plane > 0:
                    self.along(n, plane, False).wait_send()

    def sum_blocks(self, n):
        a, c = self.slot(n), self.third(n)
        for s in range(1, self.spot.blocks):
            self.to_block(n, s).wait_recv()

        @pl.when(n >= 3)
        def _():
            self.sent_along(n - 3)

        for plane in range(self.spot.planes):
            value = self.term[a, plane, :, self.own].astype(f32)
            for s in range(1, self.spot.blocks):
                value = value + self.block_in[a, s - 1, plane].astype(f32)
            self.total[c, plane] = value.astype(bf16)

        @pl.when(n + 2 < self.count)
        def _():
            for s in range(1, self.spot.blocks):
                source = (self.spot.block + self.spot.blocks - s) % self.spot.blocks
                pl.semaphore_signal(
                    self.block_free.at[a, s - 1], inc=1, device_id=self.spot.at(block=source), device_id_type=MESH
                )

        last = self.spot.planes - 1

        @pl.when(self.spot.plane == 0)
        def _():
            self.pass_on(n, 0, True)

        @pl.when(self.spot.plane == last)
        def _():
            self.pass_on(n, last, False)

    def take(self, n, plane, up):
        a, c = self.slot(n), self.third(n)
        before = plane - 1 if up else plane + 1
        self.along(n, before, up).wait_recv()
        planes = range(plane, self.spot.planes) if up else range(0, plane + 1)
        for at, p in enumerate(planes):
            value = self.total[c, p].astype(f32) + self.plane_in[a, 0 if up else 1, at].astype(f32)
            self.total[c, p] = value.astype(bf16)

        @pl.when(n + 2 < self.count)
        def _():
            pl.semaphore_signal(
                self.plane_free.at[a, 0 if up else 1], inc=1, device_id=self.spot.at(plane=before), device_id_type=MESH
            )

        if (up and plane < self.spot.planes - 1) or (not up and plane > 0):
            self.pass_on(n, plane, up)

    def hop(self, n, d):
        for plane, up in ((d, True), (self.spot.planes - 1 - d, False)):
            @pl.when(self.spot.plane == plane)
            def _():
                self.take(n, plane, up)

    def hand_out(self, n):
        a = self.slot(n)

        @pl.when(n >= 2)
        def _():
            self.keep(n - 2).wait()
            if self.direct:
                for o in (1, 2, 3):
                    self.to_role(n - 2, o).wait_send()

        self.mine[a] = self.total[self.third(n), self.spot.plane]
        self.keep(n).start()
        if self.direct:
            for o in (1, 2, 3):
                self.to_role(n, o).start()

    def finish(self):
        for n in range(max(0, self.count - 3), self.count):
            self.sent_along(n)
        for n in range(max(0, self.count - 2), self.count):
            self.keep(n).wait()
            for s in range(1, self.spot.blocks):
                self.to_block(n, s).wait_send()
            if self.direct:
                for o in (1, 2, 3):
                    self.to_role(n, o).wait_send()
        if self.direct:
            for g in range(self.count):
                for o in (1, 2, 3):
                    self.from_role(g, o).wait_recv()


def backward_kernel(cfg, *refs):
    fsdp, head, tokens, rows, direct = cfg
    (
        weights_in, vec_in, normed_in, unit_in, inverse_in, qkv_in, att_in, lse_in, hidden_in,
        stream_in, chip_in, cot_in,
        out_pair, in_pair, grads, small_grads,
        weight, vec, up, up_low, hid, gh, normed, unit, inverse, qkv, att, lse, big, soft, low_scores, gab, along,
        sent, core_in, chip, side_in, full, last_in, result, sums, unit_sums,
        term, block_in, total, plane_in, mine,
        small_term, small_block_in, small_total, small_plane_in, small_mine,
        core_s, core_r, side_s, side_r, back_s, back_r,
        block_s, block_r, plane_s, plane_r, role_s, role_r, local_sem, block_free, plane_free,
        small_block_s, small_block_r, small_plane_s, small_plane_r, small_role_s, small_role_r, small_local,
        small_block_free, small_plane_free,
        last_s, last_r, out_s, out_r, line_s, line_r, load_sem, weight_sem,
    ) = refs
    kept = big.at[:, 0:HALF]
    spot = Spot(fsdp, head)
    greet(spot.partners())
    exchange = Exchange(
        spot, sent, core_in, chip, side_in, full, (core_s, core_r), (side_s, side_r), (back_s, back_r)
    )
    scatter = Scatter(
        spot, 3 * LAYERS, term, block_in, total, plane_in, mine, grads, (block_s, block_r), (plane_s, plane_r),
        (role_s, role_r), local_sem, block_free, plane_free, direct,
    )
    small = Scatter(
        spot, 1, small_term, small_block_in, small_total, small_plane_in, small_mine, small_grads,
        (small_block_s, small_block_r), (small_plane_s, small_plane_r), (small_role_s, small_role_r),
        small_local, small_block_free, small_plane_free, direct,
    )
    owner = spot.core == spot.plane % 2
    top = LAYERS - 1

    def load(source, target, n):
        return pltpu.make_async_copy(source, target, load_sem.at[n])

    def load_weight(l, k):
        return pltpu.make_async_copy(weights_in.at[3 * l + k], weight.at[k], weight_sem.at[k])

    load_vec = load(vec_in, vec, 0)
    load_cot = load(cot_in, up_low, 1)
    last_chip = qkv.at[:, :, 0:HALF]
    load_chip = load(chip_in, last_chip, 2)

    def load_hidden(l):
        return load(hidden_in.at[l], hid, 4)

    def load_normed(l, n):
        return load(normed_in.at[l, n], normed, 5)

    def load_unit(l, n):
        return [load(unit_in.at[l, n], unit, 6), load(inverse_in.at[l, n], inverse, 7)]

    def load_attn(l):
        return [load(qkv_in.at[l], qkv, 8), load(att_in.at[l], att, 9), load(lse_in.at[l], lse, 10)]

    load_chip.start()
    load_cot.start()
    load_weight(top, 2).start()
    load_hidden(top).start()
    load_vec.start()
    load_weight(top, 1).start()
    load_weight(top, 0).start()
    load_normed(top, 1).start()
    for copy in load_unit(top, 1):
        copy.start()

    last_copy = send(
        last_chip.at[1 - spot.side], last_in, (last_s, last_r), (0,), spot.at(role=flip2(spot.role))
    )
    half_copy = send(
        result.at[:, exchange.mine], result.at[:, exchange.mine], (last_s, last_r), (1,),
        spot.at(role=flip1(spot.role)),
    )
    half_in = send(
        result.at[:, exchange.theirs], result.at[:, exchange.theirs], (last_s, last_r), (1,),
        spot.at(role=flip1(spot.role)),
    )
    load_chip.wait()
    last_copy.start()

    sums[...] = jnp.zeros_like(sums)
    unit_sums[...] = jnp.zeros_like(unit_sums)
    load_cot.wait()

    def eights(v):
        return jnp.sum(v.reshape(v.shape[0] // 8, 8, v.shape[1]), axis=0)

    for i in range(2):
        for start in range(0, rows, 128):
            r = slice(start, min(rows, start + 128))
            v = up_low[i, r].astype(f32)
            up[i, r] = v
            sums[(top + 1) * 6 + 5] += eights(v)
    load_vec.wait()

    def return_copies(pair_out):
        slot = spot.plane // 2
        mine_copy = pltpu.make_async_copy(result, pair_out.at[slot], load_sem.at[12])
        outs = [
            send(result, pair_out.at[slot], (out_s, out_r), (o,), spot.at(plane=flip(spot.plane, o)))
            for o in (1, 2, 3)
        ]
        return mine_copy, outs

    def return_begin(pair_out):
        @pl.when(owner)
        def _():
            mine_copy, outs = return_copies(pair_out)
            mine_copy.start()
            for copy in outs:
                copy.start()

    def return_end(pair_out):
        for o in (1, 2, 3):
            other = flip(spot.plane, o)

            @pl.when(spot.core == other % 2)
            def _():
                place = pair_out.at[other // 2]
                send(place, place, (out_s, out_r), (o,), spot.at(plane=other)).wait_recv()

        @pl.when(owner)
        def _():
            mine_copy, outs = return_copies(pair_out)
            mine_copy.wait()
            for copy in outs:
                copy.wait_send()

    chunks = [(start, min(160, rows - start)) for start in range(0, rows, 160)]
    last_plane = spot.planes - 1

    def line_copy(s, j, up, first):
        start, size = chunks[j]
        target = in_pair.at[s, start : start + size]
        source = up_low.at[spot.side, start : start + size] if first else target
        return pltpu.make_async_remote_copy(
            src_ref=source, dst_ref=target, send_sem=line_s.at[s, j, 0 if up else 1], recv_sem=line_r.at[s, j],
            device_id=spot.at(plane=spot.plane + (1 if up else -1)), device_id_type=MESH,
        )

    def line_ways(s, act):
        source = 2 * s + spot.core
        for up, edge in ((True, last_plane), (False, 0)):
            beyond = spot.plane > source if up else spot.plane < source

            @pl.when(jnp.logical_and(spot.plane == source, spot.plane != edge))
            def _():
                act(up, True)

            @pl.when(jnp.logical_and(beyond, spot.plane != edge))
            def _():
                act(up, False)

    def line_kept(s):
        return pltpu.make_async_copy(up_low.at[spot.side], in_pair.at[s], load_sem.at[13])

    def line_begin():
        for s in range(2):
            @pl.when(spot.plane == 2 * s + spot.core)
            def _():
                line_kept(s).start()

            for j in range(len(chunks)):
                def act(up, first):
                    if first:
                        line_copy(s, j, up, True).start()

                line_ways(s, act)

    def line_relay():
        for j in range(len(chunks)):
            for s in range(2):
                @pl.when(spot.plane != 2 * s + spot.core)
                def _():
                    line_copy(s, j, True, False).wait_recv()

                def act(up, first):
                    if not first:
                        line_copy(s, j, up, False).start()

                line_ways(s, act)

    def line_end():
        for s in range(2):
            @pl.when(spot.plane == 2 * s + spot.core)
            def _():
                line_kept(s).wait()

            for j in range(len(chunks)):
                line_ways(s, lambda up, first: line_copy(s, j, up, first).wait_send())

    def norm_back(l, n, i):
        base = (l + 1) * 6
        for start in range(0, rows, 128):
            r = slice(start, min(rows, start + 128))
            g = full[i, r].astype(f32)
            u = unit[i, r].astype(f32)
            scaled = g * vec[l, n : n + 1]
            first = jnp.mean(scaled, axis=-1, keepdims=True)
            second = jnp.mean(scaled * u, axis=-1, keepdims=True)
            v = up[i, r] + inverse[i, r, 0:1] * (scaled - first - u * second)
            up[i, r] = v
            up_low[i, r] = v.astype(bf16)
            sums[base + n] += eights(g * u)
            sums[base + 2 + n] += eights(g)
            sums[base + 4 if n == 1 else base - 1] += eights(v)

    def mlp_stage(l, i):
        @pl.when(l < top)
        def _():
            exchange.finish(i, 1)
            norm_back(jnp.minimum(l + 1, top), 0, i)

        @pl.when(i == 0)
        def _():
            load_hidden(l).wait()
            load_weight(l, 2).wait()

        for k in range(4):
            big[:, k * 256 : k * 256 + 256] = dot(up_low[i], weight[2, k], 1, 1)

        def step(r):
            v = hid[i, r].astype(f32)
            below = 0.5 + 0.5 * lax.erf(v * (0.5**0.5))
            slope = below + v * jnp.exp(-0.5 * v * v) * (1.0 / math.sqrt(2.0 * math.pi))
            hid[i, r] = (v * below).astype(bf16)
            low_grad = (big[r, 0:D] * slope).astype(bf16)
            gh[i, r] = low_grad
            unit_sums[l, 0] += eights(low_grad.astype(f32))

        each_rows(rows, 16, step, unroll=2)

        @pl.when(i == 0)
        def _():
            load_weight(l, 1).wait()

        exchange.reduce(i, lambda at: dot(gh[i], weight[1, :, :, at].reshape(D, HALF), 1, 0), kept)
        exchange.side_copy(i, 0).start()

    lane_head = lax.broadcasted_iota(jnp.int32, (1, 256), 1) // HD
    valid = lax.broadcasted_iota(jnp.int32, (rows, 1), 0) < tokens
    head_rows = jnp.where(
        lax.broadcasted_iota(jnp.int32, (16, 256), 1) // HD == lax.broadcasted_iota(jnp.int32, (16, 256), 0), 1.0, 0.0
    ).astype(bf16)

    def attn_stage(l, i):
        exchange.finish(i, 0)

        @pl.when(i == 0)
        def _():
            for copy in load_unit(l, 1):
                copy.wait()

        norm_back(l, 1, i)

        @pl.when(i == 0)
        def _():
            load_weight(l, 0).wait()
            for copy in load_attn(l):
                copy.wait()

        gab[...] = dot(up_low[i], weight[0, :, 192:256].reshape(256, D), 1, 1).astype(bf16)
        product = gab[...].astype(f32) * att[i].astype(f32)
        high = product.astype(bf16)
        rest = (product - high.astype(f32)).astype(bf16)
        along[...] = dot(head_rows, high, 1, 1) + dot(head_rows, rest, 1, 1)

        def one_head(h, carry):
            mask = jnp.where(lane_head == h, 1.0, 0.0)
            low_mask = mask.astype(bf16)
            q = qkv[i, :, 0:256] * low_mask
            big[:, 0:rows] = dot(qkv[i, :, 256:512], q * (HD ** (-0.5)), 1, 1)
            big[:, 640 : 640 + rows] = dot(qkv[i, :, 512:768], gab[...] * low_mask, 1, 1)
            lse_row = lse[i, pl.ds(h, 1)]
            along_row = along[pl.ds(h, 1)]

            p = jnp.exp(big[:, 0:rows] - lse_row)
            p = jnp.where(valid, p, 0.0)
            soft[...] = p.astype(bf16)
            low_scores[...] = (p * (big[:, 640 : 640 + rows] - along_row)).astype(bf16)
            scale = HD ** (-0.5)
            grad_q = dot(low_scores[...], qkv[i, :, 256:512], 0, 0) * (mask * scale)
            grad_k = dot(low_scores[...], q, 1, 0) * (mask * scale)
            grad_v = dot(soft[...], gab[...], 1, 0) * mask
            for m, part in enumerate((grad_q, grad_k, grad_v)):
                part = part.astype(bf16)
                at = slice(m * 256, m * 256 + 256)

                @pl.when(h == 0)
                def _():
                    gh[i, :, at] = part

                @pl.when(h > 0)
                def _():
                    gh[i, :, at] = gh[i, :, at] + part

            return carry

        lax.fori_loop(0, 4, one_head, 0)

        for m in (0, 2):
            at = slice(m * 256, m * 256 + 256)
            unit_sums[l, 1, :, at] += eights(gh[i, :, at].astype(f32))


        def partial(at):
            terms = [
                dot(gh[i, :, m * 256 : m * 256 + 256], weight[0, :, m * HD : m * HD + HD, at].reshape(256, HALF), 1, 0)
                for m in range(3)
            ]
            return terms[0] + terms[1] + terms[2]

        exchange.reduce(i, partial, kept)
        exchange.side_copy(i, 1).start()

    span = D // spot.blocks

    def unit_term(a, left, right):
        def one(plane, carry):
            at = lanes(plane * 256, 256)
            for b in range(spot.blocks):
                to = slice(b * span, b * span + span)
                part = dot(left[0, :, at], right[0, :, to], 0, 0) + dot(left[1, :, at], right[1, :, to], 0, 0)
                term[a, plane, :, to] = part.astype(bf16)
            return carry

        lax.fori_loop(0, 4, one, 0)

    def attn_term(a):
        for m in range(4):
            left = gh if m < 3 else att
            right = normed if m < 3 else up_low
            at = slice(m * 256, m * 256 + 256) if m < 3 else slice(0, 256)
            for b in range(spot.blocks):
                to = slice(b * span, b * span + span)
                part = dot(left[0, :, at], right[0, :, to], 0, 0) + dot(left[1, :, at], right[1, :, to], 0, 0)
                term[a, :, m * HD : m * HD + HD, to] = part.astype(bf16).reshape(4, HD, span)

    def one_layer(step_index, carry):
        l = top - step_index
        again = l < top
        more = l > 0
        n = 3 * step_index

        def mlp_image(i, carry):
            mlp_stage(l, i)

            @pl.when(jnp.logical_and(again, i == 0))
            def _():
                scatter.sum_blocks(n - 2)
                scatter.hop(n - 3, 1)

            return carry

        lax.fori_loop(0, 2, mlp_image, 0)

        @pl.when(l == top)
        def _():
            last_copy.wait_recv()
            load_stream = load(stream_in.at[spot.side], big.at[:, 0:D], 11)
            load_stream.start()

            v = last_chip[spot.side].astype(f32) + last_in[...].astype(f32)
            result[:, exchange.mine] = v.astype(bf16)
            load_stream.wait()

            @pl.when(jnp.logical_not(owner))
            def _():
                half_copy.start()
                half_copy.wait_send()

            @pl.when(owner)
            def _():
                half_in.wait_recv()

                for start in range(0, rows, 128):
                    r = slice(start, min(rows, start + 128))
                    v = big[r, 0:D] + result[r].astype(f32) + vec[top, 5:6]
                    result[r] = v.astype(bf16)

            last_copy.wait_send()
            for copy in load_attn(top):
                copy.start()
            return_begin(out_pair)

        @pl.when(again)
        def _():
            for copy in load_unit(l, 1):
                copy.start()

        @pl.when(again)
        def _():
            scatter.hop(n - 3, 2)
            scatter.sum_blocks(n - 1)
            scatter.hop(n - 2, 1)

        scatter.before_terms(n)
        unit_term(scatter.slot(n), hid, up_low)
        scatter.send_terms(n)
        load_normed(l, 1).wait()
        scatter.before_terms(n + 1)
        unit_term(scatter.slot(n + 1), gh, normed)
        scatter.send_terms(n + 1)

        @pl.when(more)
        def _():
            below = jnp.maximum(l - 1, 0)
            load_hidden(below).start()
            load_weight(below, 1).start()
            load_weight(below, 2).start()

        load_normed(l, 0).start()

        @pl.when(again)
        def _():
            scatter.hop(n - 3, 3)
            scatter.hand_out(n - 3)

        def attn_image(i, carry):
            attn_stage(l, i)

            @pl.when(jnp.logical_and(again, i == 0))
            def _():
                scatter.hop(n - 2, 2)
                scatter.hop(n - 1, 1)

            return carry

        lax.fori_loop(0, 2, attn_image, 0)
        for copy in load_unit(l, 0):
            copy.start()
        load_normed(l, 0).wait()

        @pl.when(again)
        def _():
            scatter.hop(n - 2, 3)
            scatter.hand_out(n - 2)
            scatter.hop(n - 1, 2)

        scatter.sum_blocks(n)
        scatter.before_terms(n + 2)
        attn_term(scatter.slot(n + 2))
        scatter.send_terms(n + 2)

        @pl.when(more)
        def _():
            below = jnp.maximum(l - 1, 0)
            load_weight(below, 0).start()
            load_normed(below, 1).start()
            for copy in load_attn(below):
                copy.start()

        for copy in load_unit(l, 0):
            copy.wait()
        return carry

    lax.fori_loop(0, LAYERS, one_layer, 0)

    end = 3 * LAYERS
    scatter.hop(end - 4, 3)
    scatter.hand_out(end - 4)
    scatter.sum_blocks(end - 2)

    def last_image(i, carry):
        exchange.finish(i, 1)
        norm_back(0, 0, i)
        return carry

    lax.fori_loop(0, 2, last_image, 0)
    line_begin()
    picks = normed.at[0]
    unit_picks(picks, fsdp)
    for l in range(LAYERS):
        features = [jnp.sum(sums[(l + 1) * 6 + n], axis=0, keepdims=True) for n in range(6)]
        inner = jnp.sum(unit_sums[l, 0], axis=0, keepdims=True)
        qkv_sums = jnp.sum(unit_sums[l, 1], axis=0, keepdims=True)
        for plane in range(4):
            parts = [
                inner[:, plane * 256 : plane * 256 + 256],
                qkv_sums[:, plane * HD : plane * HD + HD],
                qkv_sums[:, 512 + plane * HD : 512 + plane * HD + HD],
            ]
            values = jnp.broadcast_to(jnp.concatenate(parts, axis=1), (16, 384)).astype(bf16)
            row = dot(values, picks[0:384], 1, 0)[0:1]
            block = jnp.concatenate(features + [row, jnp.zeros((9, D), f32)], axis=0)
            small_term[0, plane, 16 * l : 16 * l + 16] = block.astype(bf16)
    small.send_terms(0)
    scatter.hop(end - 3, 1)
    scatter.hop(end - 2, 1)
    scatter.hop(end - 3, 2)
    scatter.sum_blocks(end - 1)
    small.sum_blocks(0)
    scatter.hop(end - 3, 3)
    scatter.hand_out(end - 3)
    scatter.hop(end - 2, 2)
    scatter.hop(end - 1, 1)
    small.hop(0, 1)
    scatter.hop(end - 2, 3)
    scatter.hand_out(end - 2)
    scatter.hop(end - 1, 2)
    small.hop(0, 2)
    scatter.hop(end - 1, 3)
    scatter.hand_out(end - 1)
    small.hop(0, 3)
    small.hand_out(0)
    line_relay()
    scatter.finish()
    small.finish()
    return_end(out_pair)
    line_end()


def backward_call(fsdp, head, tokens, rows, direct, kept):
    groups = 3 * LAYERS
    blocks = fsdp // TP
    span = D // blocks
    cols = span // TP
    anyspace = pl.BlockSpec(memory_space=pl.ANY)
    shape = jax.ShapeDtypeStruct
    dma, plain = pltpu.SemaphoreType.DMA, pltpu.SemaphoreType.REGULAR
    out_shape = (
        shape((2, rows, D), bf16),
        shape((2, rows, D), bf16),
        shape((groups, TP, 256, cols) if direct else (groups, 256, span), bf16),
        shape((1, TP, 32, cols) if direct else (1, 32, span), bf16),
    )
    scratch = [
        pltpu.VMEM((3, 4, 256, D), bf16),
        pltpu.VMEM((LAYERS, 8, D), f32),
        pltpu.VMEM((2, rows, D), f32),
        pltpu.VMEM((2, rows, D), bf16),
        pltpu.VMEM((2, rows, D), bf16),
        pltpu.VMEM((2, rows, D), bf16),
        pltpu.VMEM((2, rows, D), bf16),
        pltpu.VMEM((2, rows, D), bf16),
        pltpu.VMEM((2, rows, 128), f32),
        pltpu.VMEM((2, rows, 768), bf16),
        pltpu.VMEM((2, rows, 256), bf16),
        pltpu.VMEM((2, 8, rows), f32),
        pltpu.VMEM((rows, 640 + -(-rows // 128) * 128), f32),
        pltpu.VMEM((rows, rows), bf16),
        pltpu.VMEM((rows, rows), bf16),
        pltpu.VMEM((rows, 256), bf16),
        pltpu.VMEM((16, rows), f32),
        pltpu.VMEM((2, rows, HALF), bf16),
        pltpu.VMEM((2, rows, HALF), bf16),
        pltpu.VMEM((2, rows, HALF), bf16),
        pltpu.VMEM((2, 2, rows, HALF), bf16),
        pltpu.VMEM((2, rows, D), bf16),
        pltpu.VMEM((rows, HALF), bf16),
        pltpu.VMEM((rows, D), bf16),
        pltpu.VMEM((6 * (LAYERS + 1), 8, D), f32),
        pltpu.VMEM((LAYERS, 2, 8, D), f32),
    ]
    for slots, thirds, units in ((2, 3, 256), (1, 1, 32)):
        scratch += [
            pltpu.VMEM((slots, 4, units, D), bf16),
            pltpu.VMEM((slots, blocks - 1, 4, units, span), bf16),
            pltpu.VMEM((thirds, 4, units, span), bf16),
            pltpu.VMEM((slots, 2, 3, units, span), bf16),
            pltpu.VMEM((slots, units, span), bf16),
        ]
    scratch += [dma((2,)), dma((2,)), dma((2, 2)), dma((2, 2)), dma((2,)), dma((2,))]
    for slots, thirds, count in ((2, 3, groups), (1, 1, 1)):
        scratch += [
            dma((slots, blocks - 1)), dma((slots, blocks - 1)),
            dma((thirds, 2)), dma((thirds, 2)),
            dma((count, 4)), dma((count, 4)),
            dma((count,)),
            plain((slots, blocks - 1)), plain((slots, 2)),
        ]
    scratch += [dma((2,)), dma((2,)), dma((4,)), dma((4,)), dma((2, 4, 2)), dma((2, 4)), dma((16,)), dma((3,))]
    return pl.pallas_call(
        functools.partial(backward_kernel, (fsdp, head, tokens, rows, direct)),
        out_shape=out_shape,
        in_specs=[anyspace] * len(kept),
        out_specs=tuple(anyspace for _ in out_shape),
        scratch_shapes=scratch,
        compiler_params=pltpu.CompilerParams(
            collective_id=1, has_side_effects=True, vmem_limit_bytes=63 << 20
        ),
        name="backward_layers",
    )(*kept)


class Places:
    def __init__(self, fsdp, head):
        self.fsdp, self.head = fsdp, head
        self.blocks = fsdp // TP
        index, plane = lax.axis_index("fsdp"), lax.axis_index("head")
        self.block, self.role, self.plane = index // TP, index % TP, plane

    def pairs(self, move, sends=None):
        found = []
        for block in range(self.blocks):
            for role in range(TP):
                for plane in range(self.head):
                    if sends is not None and not sends(block, role, plane):
                        continue
                    to_block, to_role, to_plane = move(block, role, plane)
                    found.append(
                        (
                            (block * TP + role) * self.head + plane,
                            (to_block * TP + to_role) * self.head + to_plane,
                        )
                    )
        return found

    def role_xor(self, v, bits, sends=None):
        return lax.ppermute(v, AXES, self.pairs(lambda b, r, p: (b, r ^ bits, p), sends))


def by_xor(parts, index):
    a, b, c, d = parts
    odd = (index & 1) == 1
    a, b = jnp.where(odd, b, a), jnp.where(odd, a, b)
    c, d = jnp.where(odd, d, c), jnp.where(odd, c, d)
    top = (index & 2) == 2
    return [jnp.where(top, c, a), jnp.where(top, d, b), jnp.where(top, a, c), jnp.where(top, b, d)]


def pack_inputs(pl, w_qkv, w_out, w_in, w_down, qv_bias, in_bias, gains, shifts):
    fsdp = lax.axis_size("fsdp")
    cols = w_qkv.shape[2]
    groups = []
    small = []
    for l in range(LAYERS):
        attn = jnp.concatenate([w_qkv[l].transpose(0, 2, 1), w_out[l][None]]).reshape(4, TP, HD, cols)
        groups.append(attn.transpose(1, 0, 2, 3).reshape(TP, 256, cols))
        groups.append(w_in[l].T.reshape(TP, 256, cols))
        groups.append(w_down[l].reshape(TP, 256, cols))
        features = jnp.concatenate([gains[l], shifts[l]])
        features = jnp.broadcast_to(features[None], (TP, 6, cols))
        qv = qv_bias[l].reshape(2, TP, -1).transpose(1, 0, 2).reshape(TP, -1)
        units = jnp.concatenate([qv, in_bias[l].reshape(TP, -1)], axis=1)
        units = jnp.pad(units, ((0, 0), (0, cols - units.shape[1])))[:, None]
        small.append(jnp.pad(jnp.concatenate([features, units], axis=1), ((0, 0), (0, 9), (0, 0))))
    packed, extras = jnp.stack(groups), jnp.concatenate(small, axis=1)[None]
    if cols % 128 == 0:
        return packed, extras, True
    return gather_roles(pl, packed), gather_roles(pl, extras), False


def gather_roles(pl, pack):
    exchanged = [lax.dynamic_index_in_dim(pack, pl.role, 1, False)]
    for bits in (1, 2, 3):
        exchanged.append(pl.role_xor(lax.dynamic_index_in_dim(pack, pl.role ^ bits, 1, False), bits))
    return jnp.concatenate(by_xor(exchanged, pl.role), axis=-1)


def scatter_roles(pl, mine):
    groups, units, width = mine.shape
    mine = mine.reshape(groups, units, TP, width // TP)
    exchanged = [lax.dynamic_index_in_dim(mine, pl.role, 2, False)]
    for bits in (1, 2, 3):
        exchanged.append(pl.role_xor(lax.dynamic_index_in_dim(mine, pl.role ^ bits, 2, False), bits))
    return jnp.stack(by_xor(exchanged, pl.role), axis=1)


def body(images, cotangent, w_qkv, w_out, w_in, w_down, qv_bias, in_bias, gains, shifts):
    fsdp, head = lax.axis_size("fsdp"), lax.axis_size("head")
    places = Places(fsdp, head)
    cols = w_qkv.shape[2]
    per = HD // fsdp
    tokens = images.shape[1]
    rows = -(-tokens // 32) * 32
    packed, extras, direct = pack_inputs(
        places, w_qkv, w_out, w_in, w_down, qv_bias, in_bias, gains, shifts
    )
    pad = ((0, rows - tokens), (0, 0))
    own_image = jnp.pad(lax.dynamic_index_in_dim(images, places.plane // 2, 0, False), pad)
    own_cot = jnp.pad(lax.dynamic_index_in_dim(cotangent, places.plane // 2, 0, False), pad)
    kept = forward_call(fsdp, head, tokens, rows, direct, own_image, own_cot, packed, extras)
    block_out, input_grad, grads, small = backward_call(fsdp, head, tokens, rows, direct, kept)
    if not direct:
        grads, small = scatter_roles(places, grads), scatter_roles(places, small)
    grads = grads.astype(f32).reshape(LAYERS, 3, TP, 256, cols)
    attn = grads[:, 0].reshape(LAYERS, TP, 4, HD, cols).transpose(0, 2, 1, 3, 4).reshape(LAYERS, 4, TP * HD, cols)
    small = small.astype(f32).reshape(TP, LAYERS, 16, cols)
    features = small[0, :, 0:6]
    units = small[:, :, 6].transpose(1, 0, 2)
    qv = units[:, :, 0 : 2 * per].reshape(LAYERS, TP, 2, per).transpose(0, 2, 1, 3).reshape(LAYERS, 2, TP * per, 1)
    inner = units[:, :, 2 * per : 6 * per].reshape(LAYERS, TP * 4 * per, 1)
    return (
        block_out[:, :tokens].astype(f32),
        input_grad[:, :tokens].astype(f32),
        attn[:, :3].transpose(0, 1, 3, 2),
        attn[:, 3],
        grads[:, 1].reshape(LAYERS, TP * 256, cols).transpose(0, 2, 1),
        grads[:, 2].reshape(LAYERS, TP * 256, cols),
        qv,
        inner,
        features[:, 0:2],
        features[:, 2:6],
    )


def solution(mesh):
    placed = (
        P("fsdp", None, None),
        P("fsdp", None, None),
        P(None, None, "fsdp", "head"),
        P(None, "head", "fsdp"),
        P(None, "fsdp", "head"),
        P(None, "head", "fsdp"),
        P(None, None, "head", "fsdp"),
        P(None, "head", "fsdp"),
        P(None, None, "fsdp"),
        P(None, None, "fsdp"),
    )
    return jax.shard_map(
        body, mesh=mesh, in_specs=placed, out_specs=placed, check_vma=False
    )
```

```python
import functools
import math

import jax
import jax.numpy as jnp
from jax import lax
from jax.experimental import pallas as pl
from jax.experimental.pallas import tpu as pltpu
from jax.sharding import PartitionSpec as P

D = 1024
HD = 64
LAYERS = 2
TP = 4
HALF = D // 2
AXES = ("fsdp", "head")
MESH = pl.DeviceIdType.MESH
epsilon = 1e-06
f32, bf16 = jnp.float32, jnp.bfloat16


def dot(left, right, left_dim, right_dim):
    return lax.dot_general(
        left, right, (((left_dim,), (right_dim,)), ((), ())), preferred_element_type=f32
    )


def flip1(n):
    return n + 1 - 2 * (n % 2)


def flip2(n):
    return n + 2 - 4 * ((n // 2) % 2)


def flip(n, bits):
    if bits & 1:
        n = flip1(n)
    if bits & 2:
        n = flip2(n)
    return n


class Spot:
    def __init__(self, fsdp, head):
        self.blocks = fsdp // TP
        self.planes = head
        index = lax.axis_index("fsdp")
        self.index = index
        self.block, self.role, self.plane = index // TP, index % TP, lax.axis_index("head")
        self.core, self.side = self.role % 2, self.role // 2

    def at(self, block=None, role=None, plane=None):
        block = self.block if block is None else block
        role = self.role if role is None else role
        plane = self.plane if plane is None else plane
        return (block * TP + role, plane)

    def partners(self):
        found = [self.at(role=flip(self.role, o)) for o in (1, 2, 3)]
        found += [self.at(plane=flip(self.plane, o)) for o in (1, 2, 3)]
        found += [self.at(block=(self.block + s) % self.blocks) for s in range(1, self.blocks)]
        return found


def greet(partners):
    barrier = pltpu.get_barrier_semaphore()
    for partner in partners:
        pl.semaphore_signal(barrier, inc=1, device_id=partner, device_id_type=MESH)
    pl.semaphore_wait(barrier, len(partners))


def send(source, target, sems, where, device):
    return pltpu.make_async_remote_copy(
        src_ref=source,
        dst_ref=target,
        send_sem=sems[0].at[where],
        recv_sem=sems[1].at[where],
        device_id=device,
        device_id_type=MESH,
    )


def lanes(start, size):
    return pl.ds(pl.multiple_of(start, 128), size)


class Gather:
    def __init__(self, spot, source, whole, role_sems, plane_sems, block_sems, base, local_sem, direct):
        self.spot, self.source, self.whole, self.direct = spot, source, whole, direct
        self.role_sems, self.plane_sems, self.block_sems = role_sems, plane_sems, block_sems
        self.base, self.local_sem = base, local_sem
        self.blocks_first = ()
        self.cols = D // spot.blocks // TP
        self.span = D // spot.blocks

    def piece(self, g, plane, block):
        return self.whole.at[g, plane, :, :, lanes(block * self.span, self.span)]

    def own(self, g):
        spot = self.spot
        if self.direct:
            return pltpu.make_async_copy(
                self.source(g, spot.role),
                self.whole.at[g, spot.plane, :, :, lanes(spot.index * self.cols, self.cols)],
                self.local_sem.at[self.base + g],
            )
        return pltpu.make_async_copy(
            self.source(g, None), self.piece(g, spot.plane, spot.block), self.local_sem.at[self.base + g]
        )

    def to_role(self, g, o):
        spot = self.spot
        other = flip(spot.role, o)
        return send(
            self.source(g, other),
            self.whole.at[g, spot.plane, :, :, lanes(spot.index * self.cols, self.cols)],
            self.role_sems,
            (self.base + g, o),
            spot.at(role=other),
        )

    def from_role(self, g, o):
        spot = self.spot
        other = flip(spot.role, o)
        place = self.whole.at[
            g, spot.plane, :, :, lanes((spot.block * TP + other) * self.cols, self.cols)
        ]
        return send(place, place, self.role_sems, (self.base + g, o), spot.at(role=other))

    def hop(self, g, d, up, taken):
        plane = self.spot.plane
        step = 1 if up else -1
        piece = plane - step * d if taken else plane - step * (d - 1)
        place = self.whole.at[g, piece] if g in self.blocks_first else self.piece(g, piece, self.spot.block)
        other = plane - step if taken else plane + step
        return send(
            place, place, self.plane_sems, (self.base + g, d - 1 + (0 if up else 3)), self.spot.at(plane=other)
        )

    def has(self, d, up):
        return self.spot.plane >= d if up else self.spot.plane + d < self.spot.planes

    def goes(self, d, up):
        plane, last = self.spot.plane, self.spot.planes - 1
        if up:
            return jnp.logical_and(plane >= d, plane < last)
        return jnp.logical_and(plane + d <= last, plane > 0)

    def to_block(self, g, s, d, up, taken=False):
        spot = self.spot
        plane = spot.plane - d if up else spot.plane + d
        shift = spot.blocks - s if taken else s
        block = (spot.block + shift) % spot.blocks
        place = self.piece(g, plane, block if taken else spot.block)
        where = (self.base + g, s, d + (0 if up or d == 0 else 3))
        return send(place, place, self.block_sems, where, spot.at(block=block))

    def begin(self, g):
        self.own(g).start()
        if self.direct:
            for o in (1, 2, 3):
                self.to_role(g, o).start()

    def onward(self, g, d):
        for up in (True, False):
            if d < self.spot.planes - 1:
                @pl.when(self.goes(d, up))
                def _():
                    self.hop(g, d + 1, up, False).start()

    def spread(self, g):
        self.own(g).wait()
        if self.direct:
            for o in (1, 2, 3):
                self.from_role(g, o).wait_recv()
        if g not in self.blocks_first:
            self.onward(g, 0)
        for s in range(1, self.spot.blocks):
            self.to_block(g, s, 0, True).start()

    def lift(self, g):
        for s in range(1, self.spot.blocks):
            self.to_block(g, s, 0, True, True).wait_recv()
        self.onward(g, 0)

    def relay(self, g, d):
        for up in (True, False):
            @pl.when(self.has(d, up))
            def _():
                self.hop(g, d, up, True).wait_recv()
        self.onward(g, d)
        if g in self.blocks_first:
            return
        for up in (True, False):
            @pl.when(self.has(d, up))
            def _():
                for s in range(1, self.spot.blocks):
                    self.to_block(g, s, d, up).start()

    def complete(self, g):
        for s in range(1, self.spot.blocks):
            self.to_block(g, s, 0, True, True).wait_recv()
            for d in (1, 2, 3):
                for up in (True, False):
                    @pl.when(self.has(d, up))
                    def _():
                        self.to_block(g, s, d, up, True).wait_recv()

    def drain(self, g):
        for d in (0, 1, 2, 3):
            if self.direct and d > 0:
                self.to_role(g, d).wait_send()
            for up in (True, False):
                if d < 3:
                    @pl.when(self.goes(d, up))
                    def _():
                        self.hop(g, d + 1, up, False).wait_send()
                if d > 0 and g not in self.blocks_first:
                    @pl.when(self.has(d, up))
                    def _():
                        for s in range(1, self.spot.blocks):
                            self.to_block(g, s, d, up).wait_send()
        for s in range(1, self.spot.blocks):
            self.to_block(g, s, 0, True).wait_send()


class Exchange:
    def __init__(self, spot, sent, core_in, chip, side_in, full, core_sems, side_sems, back_sems):
        self.spot = spot
        self.sent, self.core_in, self.chip, self.side_in, self.full = sent, core_in, chip, side_in, full
        self.core_sems, self.side_sems, self.back_sems = core_sems, side_sems, back_sems
        self.mine = lanes(spot.core * HALF, HALF)
        self.theirs = lanes((1 - spot.core) * HALF, HALF)

    def core_copy(self, i):
        return send(
            self.sent.at[i], self.core_in.at[i], self.core_sems, (i,),
            self.spot.at(role=flip1(self.spot.role)),
        )

    def side_copy(self, i, slot):
        return send(
            self.chip.at[i], self.side_in.at[i, slot], self.side_sems, (i, slot),
            self.spot.at(role=flip2(self.spot.role)),
        )

    def back_copy(self, i):
        place = self.full.at[i, :, self.mine]
        return send(place, place, self.back_sems, (i,), self.spot.at(role=flip1(self.spot.role)))

    def back_in(self, i):
        place = self.full.at[i, :, self.theirs]
        return send(place, place, self.back_sems, (i,), self.spot.at(role=flip1(self.spot.role)))

    def reduce(self, i, product, kept):
        self.sent[i] = product(self.theirs).astype(bf16)
        self.core_copy(i).start()
        kept[...] = product(self.mine)
        copy = self.core_copy(i)
        copy.wait_recv()
        self.chip[i] = (kept[...] + self.core_in[i].astype(f32)).astype(bf16)
        copy.wait_send()

    def finish(self, i, slot):
        copy = self.side_copy(i, slot)
        copy.wait_recv()
        total = self.chip[i].astype(f32) + self.side_in[i, slot].astype(f32)
        self.full[i, :, self.mine] = total.astype(bf16)
        self.back_copy(i).start()
        copy.wait_send()
        self.back_in(i).wait_recv()
        self.back_copy(i).wait_send()


def each_rows(rows, size, step, unroll=1):
    def one(c, carry):
        step(pl.ds(pl.multiple_of(c * size, size), size))
        return carry

    lax.fori_loop(0, rows // size, one, 0, unroll=unroll)


def unit_picks(held, fsdp, role):
    cols = D // fsdp
    per = HD // fsdp
    bits = fsdp.bit_length() - 1
    for first, count, offset in (
        (0, 256, role * (4 * per)), (256, HD, role * per), (256 + HD, HD, TP * per + role * per)
    ):
        unit = lax.broadcasted_iota(jnp.int32, (count, D), 0)
        place = lax.broadcasted_iota(jnp.int32, (count, D), 1)
        wanted = (unit & (fsdp - 1)) * cols + (unit >> bits) + offset
        held[first : first + count] = jnp.where(place == wanted, 1.0, 0.0).astype(bf16)


def forward_kernel(cfg, *refs):
    fsdp, head, tokens, rows, direct = cfg
    (
        images, cotangents, attn_source, in_source, down_source, extras,
        weights_out, vec_out, normed_out, unit_out, inverse_out, qkv_out, att_out, lse_out, hidden_out,
        stream_out, chip_out, cot_out,
        whole, extra, vec, pair, cots, stream, normed, unit, inverse, qkv, att_sum, att,
        values, lse_rows, low_hidden, active, kept,
        sent, core_in, chip, side_in, full,
        role_s, role_r, plane_s, plane_r, block_s, block_r, local_sem,
        core_s, core_r, side_s, side_r, back_s, back_r,
        share_s, share_r, store_sem,
    ) = refs
    spot = Spot(fsdp, head)
    groups = 3 * LAYERS
    greet(spot.partners())
    sems = ((role_s, role_r), (plane_s, plane_r), (block_s, block_r))

    def source(g, role):
        l, k = g // 3, g % 3
        held = (attn_source, in_source, down_source)[k]
        if role is None:
            return held.at[l]
        return held.at[l, :, role] if k == 0 else held.at[l, role]

    small = Gather(spot, lambda g, role: extras, extra, *sems, groups, local_sem, direct)
    large = Gather(spot, source, whole, *sems, 0, local_sem, direct)
    large.blocks_first = (groups - 1,)
    own_image, own_cot = images.at[spot.plane // 2], cotangents.at[spot.plane // 2]
    exchange = Exchange(
        spot, sent, core_in, chip, side_in, full, (core_s, core_r), (side_s, side_r), (back_s, back_r)
    )
    owner = spot.core == spot.plane % 2
    x, other_x = spot.side, 1 - spot.side

    small.begin(0)
    large.begin(0)

    def share(source, held, n):
        across = send(
            source, held.at[x], (share_s, share_r), (n, 0), spot.at(role=flip2(spot.role))
        )
        across_in = send(
            held.at[other_x], held.at[other_x], (share_s, share_r), (n, 0), spot.at(role=flip2(spot.role))
        )
        down = [
            send(src, held.at[at], (share_s, share_r), (n, 1 + k), spot.at(role=flip1(spot.role)))
            for k, (src, at) in enumerate(((source, x), (held.at[other_x], other_x)))
        ]
        mine = pltpu.make_async_copy(source, held.at[x], store_sem.at[30 + n])
        return across, across_in, down, mine

    def share_begin(source, held, n):
        across, across_in, down, mine = share(source, held, n)

        @pl.when(owner)
        def _():
            across.start()
            mine.start()
            down[0].start()

    def share_end(source, held, n):
        across, across_in, down, mine = share(source, held, n)

        @pl.when(owner)
        def _():
            across_in.wait_recv()
            down[1].start()
            across.wait_send()
            mine.wait()
            down[0].wait_send()
            down[1].wait_send()

        @pl.when(jnp.logical_not(owner))
        def _():
            down[0].wait_recv()
            down[1].wait_recv()

    share_begin(own_image, pair, 0)
    for g in range(1, groups):
        large.begin(g)
    small.spread(0)
    large.spread(0)
    small.relay(0, 1)
    large.relay(0, 1)
    large.spread(1)
    small.relay(0, 2)
    large.relay(0, 2)
    small.relay(0, 3)
    large.relay(0, 3)
    large.relay(1, 1)
    large.spread(2)
    large.spread(5)
    share_end(own_image, pair, 0)
    small.complete(0)

    unit_picks(active, fsdp, spot.role)
    for l in range(LAYERS):
        vec[l, 0:6] = extra[0, 0, 0, 16 * l : 16 * l + 16].astype(f32)[0:6]
        for plane in range(4):
            units = dot(extra[0, plane, 0, 16 * l : 16 * l + 16], active[0:384], 1, 1)
            vec[l, 6:7, plane * 256 : plane * 256 + 256] = units[6:7, 0:256]
            if plane % 2 == 0:
                before = units
            else:
                for k in range(2):
                    at = slice(256 + k * HD, 256 + k * HD + HD)
                    to = k * 256 + (plane - 1) * HD
                    vec[l, 7:8, to : to + 128] = jnp.concatenate([before[7:8, at], units[7:8, at]], axis=1)
    store_vec = pltpu.make_async_copy(vec, vec_out, store_sem.at[28])
    store_vec.start()
    large.complete(0)

    lane_pair = lax.broadcasted_iota(jnp.int32, (1, 128), 1) // HD
    valid = lax.broadcasted_iota(jnp.int32, (rows, 1), 0) < tokens

    def stores(l, n, i):
        return [
            pltpu.make_async_copy(normed.at[i], normed_out.at[l, n, i], store_sem.at[0 + i]),
            pltpu.make_async_copy(unit.at[i], unit_out.at[l, n, i], store_sem.at[2 + i]),
            pltpu.make_async_copy(inverse.at[i], inverse_out.at[l, n, i], store_sem.at[4 + i]),
        ]

    def norm(l, n, i, v):
        stream[i] = v
        average = jnp.mean(v, axis=-1, keepdims=True)
        centred = v - average
        scale = lax.rsqrt(jnp.mean(centred * centred, axis=-1, keepdims=True) + epsilon)
        u = centred * scale
        unit[i] = u.astype(bf16)
        inverse[i] = jnp.broadcast_to(scale, (rows, 128))
        normed[i] = (u * vec[l, n : n + 1] + vec[l, 2 + n : 3 + n]).astype(bf16)
        for copy in stores(l, n, i):
            copy.start()

    def attn_stage(l, i):
        g = 3 * l

        @pl.when(l > 0)
        def _():
            exchange.finish(i, 1)
            for copy in stores(l - 1, 1, i):
                copy.wait()
            before = jnp.maximum(l - 1, 0)
            norm(l, 0, i, stream[i] + full[i].astype(f32) + vec[before, 5:6])

        @pl.when(l == 0)
        def _():
            norm(l, 0, i, pair[i].astype(f32))

        store_qkv = pltpu.make_async_copy(qkv, qkv_out.at[l, i], store_sem.at[6])
        store_att = pltpu.make_async_copy(att.at[i], att_out.at[l, i], store_sem.at[8 + i])
        store_lse = pltpu.make_async_copy(lse_rows.at[i], lse_out.at[l, i], store_sem.at[10 + i])

        @pl.when(l + i > 0)
        def _():
            store_qkv.wait()

        @pl.when(l > 0)
        def _():
            store_att.wait()
            store_lse.wait()

        for k in range(3):
            w = whole[g, :, k].reshape(256, D)
            part = dot(normed[i], w, 1, 1)
            if k == 0:
                part = part + vec[l, 7:8, 0:256]
            if k == 2:
                part = part + vec[l, 7:8, 256:512]
                values[...] = jnp.transpose(part).astype(bf16)
            qkv[:, k * 256 : k * 256 + 256] = part.astype(bf16)
        store_qkv.start()
        def one_head(h, carry):
            two = lanes(h // 2 * 128, 128)
            key_two = lanes(256 + h // 2 * 128, 128)
            low_mask = jnp.where(lane_pair == h % 2, HD ** (-0.5), 0.0).astype(bf16)
            s = dot(qkv[:, key_two], qkv[:, two] * low_mask, 1, 1)
            s = jnp.where(valid, s, -1e30)
            largest = jnp.max(s, axis=0, keepdims=True)
            e = jnp.exp(s - largest)
            total = jnp.sum(e, axis=0, keepdims=True)
            lse_rows[i, pl.ds(h, 1)] = largest + jnp.log(total)
            at = pl.ds(pl.multiple_of(h * HD, HD), HD)
            att_sum[at] = dot(values[at], e.astype(bf16), 1, 0) * (1.0 / total)
            return carry

        lax.fori_loop(0, 4, one_head, 0)
        att[i] = jnp.transpose(att_sum[...]).astype(bf16)
        store_att.start()
        store_lse.start()
        exchange.reduce(
            i, lambda at: dot(att[i], whole[g, :, 3, :, at].reshape(256, HALF), 1, 0), kept
        )
        exchange.side_copy(i, 0).start()

    def mlp_stage(l, i):
        g = 3 * l
        exchange.finish(i, 0)
        for copy in stores(l, 0, i):
            copy.wait()
        norm(l, 1, i, stream[i] + full[i].astype(f32) + vec[l, 4:5])
        store_hidden = pltpu.make_async_copy(low_hidden.at[i], hidden_out.at[l, i], store_sem.at[12 + i])

        @pl.when(l > 0)
        def _():
            store_hidden.wait()

        for k in range(4):
            at = slice(k * 256, k * 256 + 256)
            v = dot(normed[i], whole[g + 1, k].reshape(256, D), 1, 1) + vec[l, 6:7, at]
            low_hidden[i, :, at] = v.astype(bf16)
            active[:, at] = (v * (0.5 + 0.5 * lax.erf(v * (0.5**0.5)))).astype(bf16)
        store_hidden.start()

        @pl.when(jnp.logical_and(i == 0, l < LAYERS - 1))
        def _():
            large.complete(g + 2)


        exchange.reduce(i, lambda at: dot(active[...], whole[g + 2, :, :, :, at].reshape(D, HALF), 1, 0), kept)

        @pl.when(l < LAYERS - 1)
        def _():
            exchange.side_copy(i, 1).start()

        @pl.when(l == LAYERS - 1)
        def _():
            pltpu.make_async_copy(chip.at[i], chip_out.at[i], store_sem.at[14 + i]).start()
            pltpu.make_async_copy(stream.at[i], stream_out.at[i], store_sem.at[16 + i]).start()

    def store_weights(g):
        return pltpu.make_async_copy(whole.at[g], weights_out.at[g], store_sem.at[18 + g])

    def one_layer(l, carry):
        g = 3 * l

        @pl.when(l > 0)
        def _():
            large.complete(g)

        def attn_image(i, carry):
            attn_stage(l, i)

            @pl.when(jnp.logical_and(l == 0, i == 0))
            def _():
                share_begin(own_cot, cots, 1)
                large.relay(1, 2)
                large.relay(2, 1)
                large.spread(3)

            @pl.when(jnp.logical_and(l > 0, i == 0))
            def _():
                large.relay(5, 3)

            return carry

        lax.fori_loop(0, 2, attn_image, 0)

        @pl.when(l == 0)
        def _():
            large.relay(1, 3)
            large.relay(2, 2)
            large.relay(3, 1)
            large.spread(4)
            large.relay(2, 3)
            large.lift(5)

        large.complete(g + 1)

        def mlp_image(i, carry):
            mlp_stage(l, i)

            @pl.when(jnp.logical_and(l == 0, i == 0))
            def _():
                large.relay(3, 2)
                large.relay(4, 1)
                large.relay(3, 3)
                large.relay(5, 1)

            return carry

        lax.fori_loop(0, 2, mlp_image, 0)

        @pl.when(l == 0)
        def _():
            large.relay(4, 2)
            large.relay(4, 3)
            large.relay(5, 2)

        for k in range(3):
            store_weights(g + k).start()
        return carry

    lax.fori_loop(0, LAYERS, one_layer, 0)
    share_end(own_cot, cots, 1)
    store_cots = pltpu.make_async_copy(cots, cot_out, store_sem.at[29])
    store_cots.start()
    last = LAYERS - 1
    for i in range(2):
        for copy in stores(last, 1, i):
            copy.wait()
        pltpu.make_async_copy(att.at[i], att_out.at[last, i], store_sem.at[8 + i]).wait()
        pltpu.make_async_copy(lse_rows.at[i], lse_out.at[last, i], store_sem.at[10 + i]).wait()
        pltpu.make_async_copy(low_hidden.at[i], hidden_out.at[last, i], store_sem.at[12 + i]).wait()
        pltpu.make_async_copy(chip.at[i], chip_out.at[i], store_sem.at[14 + i]).wait()
        pltpu.make_async_copy(stream.at[i], stream_out.at[i], store_sem.at[16 + i]).wait()
    pltpu.make_async_copy(qkv, qkv_out.at[last, 1], store_sem.at[6]).wait()
    store_vec.wait()
    store_cots.wait()

    for g in range(groups):
        store_weights(g).wait()
        large.drain(g)
    small.drain(0)


def forward_call(fsdp, head, tokens, rows, direct, *operands):
    groups = 3 * LAYERS
    blocks = fsdp // TP
    anyspace = pl.BlockSpec(memory_space=pl.ANY)
    shape = jax.ShapeDtypeStruct
    dma = pltpu.SemaphoreType.DMA
    out_shape = (
        shape((groups, 4, 4, HD, D), bf16),
        shape((LAYERS, 8, D), f32),
        shape((LAYERS, 2, 2, rows, D), bf16),
        shape((LAYERS, 2, 2, rows, D), bf16),
        shape((LAYERS, 2, 2, rows, 128), f32),
        shape((LAYERS, 2, rows, 768), bf16),
        shape((LAYERS, 2, rows, 256), bf16),
        shape((LAYERS, 2, 8, rows), f32),
        shape((LAYERS, 2, rows, D), bf16),
        shape((2, rows, D), f32),
        shape((2, rows, HALF), bf16),
        shape((2, rows, D), bf16),
    )
    scratch = [
        pltpu.VMEM((groups, 4, 4, HD, D), bf16),
        pltpu.VMEM((1, 4, 1, 32, D), bf16),
        pltpu.VMEM((LAYERS, 8, D), f32),
        pltpu.VMEM((2, rows, D), bf16),
        pltpu.VMEM((2, rows, D), bf16),
        pltpu.VMEM((2, rows, D), f32),
        pltpu.VMEM((2, rows, D), bf16),
        pltpu.VMEM((2, rows, D), bf16),
        pltpu.VMEM((2, rows, 128), f32),
        pltpu.VMEM((rows, 768), bf16),
        pltpu.VMEM((256, rows), f32),
        pltpu.VMEM((2, rows, 256), bf16),
        pltpu.VMEM((256, rows), bf16),
        pltpu.VMEM((2, 8, rows), f32),
        pltpu.VMEM((2, rows, D), bf16),
        pltpu.VMEM((rows, D), bf16),
        pltpu.VMEM((rows, HALF), f32),
        pltpu.VMEM((2, rows, HALF), bf16),
        pltpu.VMEM((2, rows, HALF), bf16),
        pltpu.VMEM((2, rows, HALF), bf16),
        pltpu.VMEM((2, 2, rows, HALF), bf16),
        pltpu.VMEM((2, rows, D), bf16),
        dma((groups + 1, 4)), dma((groups + 1, 4)),
        dma((groups + 1, 6)), dma((groups + 1, 6)),
        dma((groups + 1, blocks, 7)), dma((groups + 1, blocks, 7)),
        dma((groups + 1,)),
        dma((2,)), dma((2,)),
        dma((2, 2)), dma((2, 2)),
        dma((2,)), dma((2,)),
        dma((2, 3)), dma((2, 3)),
        dma((32,)),
    ]
    return pl.pallas_call(
        functools.partial(forward_kernel, (fsdp, head, tokens, rows, direct)),
        out_shape=out_shape,
        in_specs=[anyspace] * len(operands),
        out_specs=tuple(anyspace for _ in out_shape),
        scratch_shapes=scratch,
        compiler_params=pltpu.CompilerParams(
            collective_id=0, has_side_effects=True, vmem_limit_bytes=60 << 20
        ),
        name="forward_layers",
    )(*operands)


class Scatter:
    def __init__(self, spot, count, term, block_in, total, plane_in, mine, out, block_sems, plane_sems, role_sems, local_sem, block_free, plane_free, direct):
        self.spot, self.count, self.direct = spot, count, direct
        self.term, self.block_in, self.total = term, block_in, total
        self.plane_in, self.mine, self.out = plane_in, mine, out
        self.block_sems, self.plane_sems, self.role_sems, self.local_sem = block_sems, plane_sems, role_sems, local_sem
        self.block_free, self.plane_free = block_free, plane_free
        self.span = D // spot.blocks
        self.cols = self.span // TP
        self.own = lanes(spot.block * self.span, self.span)

    def slot(self, n):
        return n % self.term.shape[0]

    def third(self, n):
        return n % self.total.shape[0]

    def rows(self, part):
        units = self.term.shape[2]
        return slice(0, units) if part is None else slice(part * units // 2, (part + 1) * units // 2)

    def to_block(self, n, s, part=None):
        block = (self.spot.block + s) % self.spot.blocks
        a, r = self.slot(n), self.rows(part)
        return send(
            self.term.at[a, :, r, lanes(block * self.span, self.span)],
            self.block_in.at[a, s - 1, :, r],
            self.block_sems, (a, s - 1, part or 0), self.spot.at(block=block),
        )

    def along(self, n, plane, up, part=None):
        planes = self.spot.planes
        a, c = self.slot(n), self.third(n)
        first, number = (plane + 1, planes - 1 - plane) if up else (0, plane)
        way, r = 0 if up else 1, self.rows(part)
        return send(
            self.total.at[c, first : first + number, r], self.plane_in.at[a, way, 0:number, r],
            self.plane_sems, (c, way, part or 0), self.spot.at(plane=plane + (1 if up else -1)),
        )

    def to_role(self, n, o, part=None):
        other = flip(self.spot.role, o)
        g, r = self.count - 1 - n, self.rows(part)
        return send(
            self.mine.at[self.slot(n), r, lanes(other * self.cols, self.cols)],
            self.out.at[g, self.spot.role, r],
            self.role_sems, (g, o, part or 0), self.spot.at(role=other),
        )

    def from_role(self, g, o, part=None):
        other = flip(self.spot.role, o)
        place = self.out.at[g, other, self.rows(part)]
        return send(place, place, self.role_sems, (g, o, part or 0), self.spot.at(role=other))

    def keep(self, n, part=None):
        g, r = self.count - 1 - n, self.rows(part)
        if self.direct:
            return pltpu.make_async_copy(
                self.mine.at[self.slot(n), r, lanes(self.spot.role * self.cols, self.cols)],
                self.out.at[g, self.spot.role, r], self.local_sem.at[g, part or 0],
            )
        return pltpu.make_async_copy(
            self.mine.at[self.slot(n), r], self.out.at[g, r], self.local_sem.at[g, part or 0]
        )

    def before_terms(self, n):
        @pl.when(n >= 2)
        def _():
            for s in range(1, self.spot.blocks):
                self.to_block(n - 2, s).wait_send()

    def send_terms(self, n, parts=(None,)):
        for s in range(1, self.spot.blocks):
            @pl.when(n >= 2)
            def _():
                pl.semaphore_wait(self.block_free.at[self.slot(n), s - 1], 1)

            for part in parts:
                self.to_block(n, s, part).start()

    def pass_on(self, n, plane, up, part=None):
        if not part:
            @pl.when(n >= 2)
            def _():
                pl.semaphore_wait(self.plane_free.at[self.slot(n), 0 if up else 1], 1)

        self.along(n, plane, up, part).start()

    def sent_along(self, n, part=None):
        for plane in range(self.spot.planes):
            @pl.when(self.spot.plane == plane)
            def _():
                if plane < self.spot.planes - 1:
                    self.along(n, plane, True, part).wait_send()
                if plane > 0:
                    self.along(n, plane, False, part).wait_send()

    def sum_blocks(self, n, part=None):
        a, c, r = self.slot(n), self.third(n), self.rows(part)
        for s in range(1, self.spot.blocks):
            self.to_block(n, s, part).wait_recv()

        if not part:
            @pl.when(n >= 3)
            def _():
                self.sent_along(n - 3)

        for plane in range(self.spot.planes):
            value = self.term[a, plane, r, self.own].astype(f32)
            for s in range(1, self.spot.blocks):
                value = value + self.block_in[a, s - 1, plane, r].astype(f32)
            self.total[c, plane, r] = value.astype(bf16)

        @pl.when(n + 2 < self.count)
        def _():
            for s in range(1, self.spot.blocks):
                source = (self.spot.block + self.spot.blocks - s) % self.spot.blocks
                pl.semaphore_signal(
                    self.block_free.at[a, s - 1], inc=1, device_id=self.spot.at(block=source), device_id_type=MESH
                )

        last = self.spot.planes - 1

        @pl.when(self.spot.plane == 0)
        def _():
            self.pass_on(n, 0, True, part)

        @pl.when(self.spot.plane == last)
        def _():
            self.pass_on(n, last, False, part)

    def take(self, n, plane, up, part):
        a, c, r = self.slot(n), self.third(n), self.rows(part)
        before = plane - 1 if up else plane + 1
        self.along(n, before, up, part).wait_recv()
        planes = range(plane, self.spot.planes) if up else range(0, plane + 1)
        for at, p in enumerate(planes):
            value = self.total[c, p, r].astype(f32) + self.plane_in[a, 0 if up else 1, at, r].astype(f32)
            self.total[c, p, r] = value.astype(bf16)

        @pl.when(n + 2 < self.count)
        def _():
            pl.semaphore_signal(
                self.plane_free.at[a, 0 if up else 1], inc=1, device_id=self.spot.at(plane=before), device_id_type=MESH
            )

        if (up and plane < self.spot.planes - 1) or (not up and plane > 0):
            self.pass_on(n, plane, up, part)

    def hop(self, n, d, part=None):
        for plane, up in ((d, True), (self.spot.planes - 1 - d, False)):
            @pl.when(self.spot.plane == plane)
            def _():
                self.take(n, plane, up, part)

    def hand_out(self, n, part=None):
        a, r = self.slot(n), self.rows(part)

        if not part:
            @pl.when(n >= 2)
            def _():
                self.keep(n - 2).wait()
                if self.direct:
                    for o in (1, 2, 3):
                        self.to_role(n - 2, o).wait_send()

        self.mine[a, r] = self.total[self.third(n), self.spot.plane, r]
        self.keep(n, part).start()
        if self.direct:
            for o in (1, 2, 3):
                self.to_role(n, o, part).start()

    def finish(self, parts=(None,)):
        last = self.count - 1
        for n in range(max(0, last - 2), last + 1):
            for part in parts if n == last else (None,):
                self.sent_along(n, part)
        for n in range(max(0, last - 1), last + 1):
            for part in parts if n == last else (None,):
                self.keep(n, part).wait()
                for s in range(1, self.spot.blocks):
                    self.to_block(n, s, part).wait_send()
                if self.direct:
                    for o in (1, 2, 3):
                        self.to_role(n, o, part).wait_send()
        if self.direct:
            for g in range(self.count):
                for o in (1, 2, 3):
                    for part in parts if g == 0 else (None,):
                        self.from_role(g, o, part).wait_recv()


def backward_kernel(cfg, *refs):
    fsdp, head, tokens, rows, direct = cfg
    (
        weights_in, vec_in, normed_in, unit_in, inverse_in, qkv_in, att_in, lse_in, hidden_in,
        stream_in, chip_in, cot_in,
        out_pair, in_pair, grads, small_grads,
        weight, vec, up, up_low, hid, gh, normed, unit, inverse, qkv, att, lse, big, grad_rows, flipped, gab, along,
        sent, core_in, chip, side_in, full, last_in, result, sums, unit_sums,
        term, block_in, total, plane_in, mine,
        small_term, small_block_in, small_total, small_plane_in, small_mine,
        core_s, core_r, side_s, side_r, back_s, back_r,
        block_s, block_r, plane_s, plane_r, role_s, role_r, local_sem, block_free, plane_free,
        small_block_s, small_block_r, small_plane_s, small_plane_r, small_role_s, small_role_r, small_local,
        small_block_free, small_plane_free,
        last_s, last_r, out_s, out_r, line_s, line_r, load_sem, weight_sem,
    ) = refs
    kept = big.at[:, 0:HALF]
    spot = Spot(fsdp, head)
    greet(spot.partners())
    exchange = Exchange(
        spot, sent, core_in, chip, side_in, full, (core_s, core_r), (side_s, side_r), (back_s, back_r)
    )
    scatter = Scatter(
        spot, 3 * LAYERS, term, block_in, total, plane_in, mine, grads, (block_s, block_r), (plane_s, plane_r),
        (role_s, role_r), local_sem, block_free, plane_free, direct,
    )
    small = Scatter(
        spot, 1, small_term, small_block_in, small_total, small_plane_in, small_mine, small_grads,
        (small_block_s, small_block_r), (small_plane_s, small_plane_r), (small_role_s, small_role_r),
        small_local, small_block_free, small_plane_free, direct,
    )
    owner = spot.core == spot.plane % 2
    top = LAYERS - 1

    def load(source, target, n):
        return pltpu.make_async_copy(source, target, load_sem.at[n])

    def load_weight(l, k):
        return pltpu.make_async_copy(weights_in.at[3 * l + k], weight.at[k], weight_sem.at[k])

    load_vec = load(vec_in, vec, 0)
    load_cot = load(cot_in, up_low, 1)
    last_chip = qkv.at[:, :, 0:HALF]
    load_chip = load(chip_in, last_chip, 2)

    def load_hidden(l):
        return load(hidden_in.at[l], hid, 4)

    def load_normed(l, n):
        return load(normed_in.at[l, n], normed, 5)

    def load_unit(l, n):
        return [load(unit_in.at[l, n], unit, 6), load(inverse_in.at[l, n], inverse, 7)]

    def load_attn(l):
        return [load(qkv_in.at[l], qkv, 8), load(att_in.at[l], att, 9), load(lse_in.at[l], lse, 10)]

    load_chip.start()
    load_cot.start()
    load_weight(top, 2).start()
    load_hidden(top).start()
    load_vec.start()
    load_weight(top, 1).start()
    load_weight(top, 0).start()
    load_normed(top, 1).start()
    for copy in load_unit(top, 1):
        copy.start()

    last_copy = send(
        last_chip.at[1 - spot.side], last_in, (last_s, last_r), (0,), spot.at(role=flip2(spot.role))
    )
    half_copy = send(
        result.at[:, exchange.mine], result.at[:, exchange.mine], (last_s, last_r), (1,),
        spot.at(role=flip1(spot.role)),
    )
    half_in = send(
        result.at[:, exchange.theirs], result.at[:, exchange.theirs], (last_s, last_r), (1,),
        spot.at(role=flip1(spot.role)),
    )
    load_chip.wait()
    last_copy.start()

    sums[...] = jnp.zeros_like(sums)
    unit_sums[...] = jnp.zeros_like(unit_sums)
    load_cot.wait()

    def eights(v):
        return jnp.sum(v.reshape(v.shape[0] // 8, 8, v.shape[1]), axis=0)

    for i in range(2):
        for start in range(0, rows, 128):
            r = slice(start, min(rows, start + 128))
            v = up_low[i, r].astype(f32)
            up[i, r] = v
            sums[(top + 1) * 6 + 5] += eights(v)
    load_vec.wait()

    def return_copies(pair_out):
        slot = spot.plane // 2
        mine_copy = pltpu.make_async_copy(result, pair_out.at[slot], load_sem.at[12])
        outs = [
            send(result, pair_out.at[slot], (out_s, out_r), (o,), spot.at(plane=flip(spot.plane, o)))
            for o in (1, 2, 3)
        ]
        return mine_copy, outs

    def return_begin(pair_out):
        @pl.when(owner)
        def _():
            mine_copy, outs = return_copies(pair_out)
            mine_copy.start()
            for copy in outs:
                copy.start()

    def return_end(pair_out):
        for o in (1, 2, 3):
            other = flip(spot.plane, o)

            @pl.when(spot.core == other % 2)
            def _():
                place = pair_out.at[other // 2]
                send(place, place, (out_s, out_r), (o,), spot.at(plane=other)).wait_recv()

        @pl.when(owner)
        def _():
            mine_copy, outs = return_copies(pair_out)
            mine_copy.wait()
            for copy in outs:
                copy.wait_send()

    chunks = [(start, min(160, rows - start)) for start in range(0, 640, 160)]
    assert sum(size for _, size in chunks) == rows
    last_plane = spot.planes - 1

    def line_copy(s, j, up, first):
        start, size = chunks[j]
        target = in_pair.at[s, start : start + size]
        source = up_low.at[spot.side, start : start + size] if first else target
        return pltpu.make_async_remote_copy(
            src_ref=source, dst_ref=target, send_sem=line_s.at[s, j, 0 if up else 1], recv_sem=line_r.at[s, j],
            device_id=spot.at(plane=spot.plane + (1 if up else -1)), device_id_type=MESH,
        )

    def line_ways(s, act):
        source = 2 * s + spot.core
        for up, edge in ((True, last_plane), (False, 0)):
            beyond = spot.plane > source if up else spot.plane < source

            @pl.when(jnp.logical_and(spot.plane == source, spot.plane != edge))
            def _():
                act(up, True)

            @pl.when(jnp.logical_and(beyond, spot.plane != edge))
            def _():
                act(up, False)

    def line_kept(s):
        return pltpu.make_async_copy(up_low.at[spot.side], in_pair.at[s], load_sem.at[13])

    def line_begin():
        for s in range(2):
            @pl.when(spot.plane == 2 * s + spot.core)
            def _():
                line_kept(s).start()

            for j in range(len(chunks)):
                def act(up, first):
                    if first:
                        line_copy(s, j, up, True).start()

                line_ways(s, act)

    def line_relay(j):
        for s in range(2):
            @pl.when(spot.plane != 2 * s + spot.core)
            def _():
                line_copy(s, j, True, False).wait_recv()

            def act(up, first):
                if not first:
                    line_copy(s, j, up, False).start()

            line_ways(s, act)

    def line_end():
        for s in range(2):
            @pl.when(spot.plane == 2 * s + spot.core)
            def _():
                line_kept(s).wait()

            for j in range(len(chunks)):
                line_ways(s, lambda up, first: line_copy(s, j, up, first).wait_send())

    def norm_back(l, n, i):
        base = (l + 1) * 6
        for start in range(0, rows, 128):
            r = slice(start, min(rows, start + 128))
            g = full[i, r].astype(f32)
            u = unit[i, r].astype(f32)
            scaled = g * vec[l, n : n + 1]
            first = jnp.mean(scaled, axis=-1, keepdims=True)
            second = jnp.mean(scaled * u, axis=-1, keepdims=True)
            v = up[i, r] + inverse[i, r, 0:1] * (scaled - first - u * second)
            up[i, r] = v
            up_low[i, r] = v.astype(bf16)
            sums[base + n] += eights(g * u)
            sums[base + 2 + n] += eights(g)
            sums[base + 4 if n == 1 else base - 1] += eights(v)

    def mlp_stage(l, i, n):
        @pl.when(l < top)
        def _():
            exchange.finish(i, 1)
            norm_back(jnp.minimum(l + 1, top), 0, i)

        @pl.when(i == 0)
        def _():
            load_hidden(l).wait()
            load_weight(l, 2).wait()

        for k in range(4):
            at = slice(k * 256, k * 256 + 256)
            grad_active = dot(up_low[i], weight[2, k].reshape(256, D), 1, 1)
            v = hid[i, :, at].astype(f32)
            below = 0.5 + 0.5 * lax.erf(v * (0.5**0.5))
            slope = below + v * jnp.exp(-0.5 * v * v) * (1.0 / math.sqrt(2.0 * math.pi))
            hid[i, :, at] = (v * below).astype(bf16)
            low_grad = (grad_active * slope).astype(bf16)
            gh[i, :, at] = low_grad
            unit_sums[l, 0, :, at] += eights(low_grad.astype(f32))

        @pl.when(i == 1)
        def _():
            scatter.before_terms(n)
            unit_term(scatter.slot(n), hid, up_low)
            scatter.send_terms(n)

        @pl.when(i == 0)
        def _():
            load_weight(l, 1).wait()

        exchange.reduce(i, lambda at: dot(gh[i], weight[1, :, :, :, at].reshape(D, HALF), 1, 0), kept)
        exchange.side_copy(i, 0).start()

    lane_pair = lax.broadcasted_iota(jnp.int32, (1, 128), 1) // HD
    valid = lax.broadcasted_iota(jnp.int32, (rows, 1), 0) < tokens
    head_rows = jnp.where(
        lax.broadcasted_iota(jnp.int32, (16, 256), 1) // HD == lax.broadcasted_iota(jnp.int32, (16, 256), 0), 1.0, 0.0
    ).astype(bf16)

    def attn_stage(l, i):
        exchange.finish(i, 0)

        @pl.when(i == 0)
        def _():
            for copy in load_unit(l, 1):
                copy.wait()

        norm_back(l, 1, i)

        @pl.when(i == 0)
        def _():
            load_weight(l, 0).wait()
            for copy in load_attn(l):
                copy.wait()

        gab[...] = dot(up_low[i], weight[0, :, 3].reshape(256, D), 1, 1).astype(bf16)
        product = gab[...].astype(f32) * att[i].astype(f32)
        high = product.astype(bf16)
        rest = (product - high.astype(f32)).astype(bf16)
        along[...] = dot(head_rows, high, 1, 1) + dot(head_rows, rest, 1, 1)

        flipped[0:256] = jnp.transpose(qkv[i, :, 256:512])
        flipped[256:512] = jnp.transpose(qkv[i, :, 0:256])
        flipped[512:768] = jnp.transpose(gab[...])
        def one_head(h, carry):
            two, key_two, value_two = [lanes(m * 256 + h // 2 * 128, 128) for m in range(3)]
            low_mask = jnp.where(lane_pair == h % 2, 1.0, 0.0).astype(bf16)
            q = qkv[i, :, two] * (low_mask * HD ** (-0.5))
            p = jnp.exp(dot(qkv[i, :, key_two], q, 1, 1) - lse[i, pl.ds(h, 1)])
            p = jnp.where(valid, p, 0.0)
            grad_p = dot(qkv[i, :, value_two], gab[:, two] * low_mask, 1, 1)
            ds = (p * (grad_p - along[pl.ds(h, 1)])).astype(bf16)
            at = [pl.ds(pl.multiple_of(m * 256 + h * HD, HD), HD) for m in range(3)]
            grad_rows[at[0]] = (dot(flipped[at[0]], ds, 1, 0) * HD ** (-0.5)).astype(bf16)
            grad_rows[at[1]] = (dot(flipped[at[1]], ds, 1, 1) * HD ** (-0.5)).astype(bf16)
            grad_rows[at[2]] = dot(flipped[at[2]], p.astype(bf16), 1, 1).astype(bf16)
            return carry

        lax.fori_loop(0, 4, one_head, 0)
        for m in range(3):
            gh[i, :, m * 256 : m * 256 + 256] = jnp.transpose(grad_rows[m * 256 : m * 256 + 256])
        for m in (0, 2):
            at = slice(m * 256, m * 256 + 256)
            unit_sums[l, 1, :, at] += eights(gh[i, :, at].astype(f32))


        def partial(at):
            terms = [
                dot(gh[i, :, m * 256 : m * 256 + 256], weight[0, :, m, :, at].reshape(256, HALF), 1, 0)
                for m in range(3)
            ]
            return terms[0] + terms[1] + terms[2]

        exchange.reduce(i, partial, kept)
        exchange.side_copy(i, 1).start()

    span = D // spot.blocks

    def unit_term(a, left, right):
        def one(plane, carry):
            at = lanes(plane * 256, 256)
            for b in range(spot.blocks):
                to = slice(b * span, b * span + span)
                part = dot(left[0, :, at], right[0, :, to], 0, 0) + dot(left[1, :, at], right[1, :, to], 0, 0)
                term[a, plane, :, to] = part.astype(bf16)
            return carry

        lax.fori_loop(0, 4, one, 0)

    def attn_term(a):
        for m in range(4):
            left = gh if m < 3 else att
            right = normed if m < 3 else up_low
            at = slice(m * 256, m * 256 + 256) if m < 3 else slice(0, 256)
            for b in range(spot.blocks):
                to = slice(b * span, b * span + span)
                part = dot(left[0, :, at], right[0, :, to], 0, 0) + dot(left[1, :, at], right[1, :, to], 0, 0)
                term[a, :, m * HD : m * HD + HD, to] = part.astype(bf16).reshape(4, HD, span)

    def one_layer(step_index, carry):
        l = top - step_index
        again = l < top
        more = l > 0
        n = 3 * step_index

        def mlp_image(i, carry):
            mlp_stage(l, i, n)

            @pl.when(jnp.logical_and(again, i == 0))
            def _():
                scatter.sum_blocks(n - 2)
                scatter.hop(n - 3, 1)

            return carry

        lax.fori_loop(0, 2, mlp_image, 0)

        @pl.when(l == top)
        def _():
            last_copy.wait_recv()
            load_stream = load(stream_in.at[spot.side], big.at[:, 0:D], 11)
            load_stream.start()

            v = last_chip[spot.side].astype(f32) + last_in[...].astype(f32)
            result[:, exchange.mine] = v.astype(bf16)
            load_stream.wait()

            @pl.when(jnp.logical_not(owner))
            def _():
                half_copy.start()
                half_copy.wait_send()

            @pl.when(owner)
            def _():
                half_in.wait_recv()

                for start in range(0, rows, 128):
                    r = slice(start, min(rows, start + 128))
                    v = big[r, 0:D] + result[r].astype(f32) + vec[top, 5:6]
                    result[r] = v.astype(bf16)

            last_copy.wait_send()
            for copy in load_attn(top):
                copy.start()
            return_begin(out_pair)

        @pl.when(again)
        def _():
            for copy in load_unit(l, 1):
                copy.start()

        load_normed(l, 1).wait()

        @pl.when(again)
        def _():
            scatter.hop(n - 3, 2)
            scatter.sum_blocks(n - 1)
            scatter.hop(n - 2, 1)

        scatter.before_terms(n + 1)
        unit_term(scatter.slot(n + 1), gh, normed)
        scatter.send_terms(n + 1)

        @pl.when(more)
        def _():
            below = jnp.maximum(l - 1, 0)
            load_hidden(below).start()
            load_weight(below, 1).start()
            load_weight(below, 2).start()

        load_normed(l, 0).start()

        @pl.when(again)
        def _():
            scatter.hop(n - 3, 3)
            scatter.hand_out(n - 3)

        def attn_image(i, carry):
            attn_stage(l, i)

            @pl.when(jnp.logical_and(again, i == 0))
            def _():
                scatter.hop(n - 2, 2)
                scatter.hop(n - 1, 1)

            return carry

        lax.fori_loop(0, 2, attn_image, 0)
        for copy in load_unit(l, 0):
            copy.start()
        load_normed(l, 0).wait()

        @pl.when(again)
        def _():
            scatter.hop(n - 2, 3)
            scatter.hand_out(n - 2)
            scatter.hop(n - 1, 2)

        scatter.sum_blocks(n)
        scatter.before_terms(n + 2)
        attn_term(scatter.slot(n + 2))

        @pl.when(more)
        def _():
            scatter.send_terms(n + 2)

        @pl.when(jnp.logical_not(more))
        def _():
            scatter.send_terms(3 * LAYERS - 1, (0, 1))

        @pl.when(more)
        def _():
            below = jnp.maximum(l - 1, 0)
            load_weight(below, 0).start()
            load_normed(below, 1).start()
            for copy in load_attn(below):
                copy.start()

        for copy in load_unit(l, 0):
            copy.wait()
        return carry

    lax.fori_loop(0, LAYERS, one_layer, 0)

    end = 3 * LAYERS
    def last_image(i, carry):
        exchange.finish(i, 1)
        norm_back(0, 0, i)
        return carry

    lax.fori_loop(0, 2, last_image, 0)
    line_begin()
    picks = normed.at[0]
    unit_picks(picks, fsdp, spot.role)
    for l in range(LAYERS):
        features = [jnp.sum(sums[(l + 1) * 6 + n], axis=0, keepdims=True) for n in range(6)]
        inner = jnp.sum(unit_sums[l, 0], axis=0, keepdims=True)
        qkv_sums = jnp.sum(unit_sums[l, 1], axis=0, keepdims=True)
        for plane in range(4):
            parts = [
                inner[:, plane * 256 : plane * 256 + 256],
                qkv_sums[:, plane * HD : plane * HD + HD],
                qkv_sums[:, 512 + plane * HD : 512 + plane * HD + HD],
            ]
            values = jnp.broadcast_to(jnp.concatenate(parts, axis=1), (16, 384)).astype(bf16)
            row = dot(values[:, 0:256], picks[0:256], 1, 0)[0:1]
            other_row = dot(values[:, 256:384], picks[256:384], 1, 0)[0:1]
            block = jnp.concatenate(features + [row, other_row, jnp.zeros((8, D), f32)], axis=0)
            small_term[0, plane, 16 * l : 16 * l + 16] = block.astype(bf16)
    small.send_terms(0)
    scatter.hop(end - 4, 3)
    scatter.hand_out(end - 4)
    scatter.hop(end - 3, 1)
    line_relay(0)
    scatter.sum_blocks(end - 2)
    scatter.hop(end - 3, 2)
    line_relay(1)
    scatter.sum_blocks(end - 1, 0)
    small.sum_blocks(0)
    line_relay(2)
    scatter.hop(end - 2, 1)
    scatter.sum_blocks(end - 1, 1)
    scatter.hop(end - 3, 3)
    scatter.hand_out(end - 3)
    line_relay(3)
    scatter.hop(end - 2, 2)
    scatter.hop(end - 1, 1, 0)
    small.hop(0, 1)
    scatter.hop(end - 2, 3)
    scatter.hand_out(end - 2)
    scatter.hop(end - 1, 1, 1)
    scatter.hop(end - 1, 2, 0)
    small.hop(0, 2)
    scatter.hop(end - 1, 2, 1)
    scatter.hop(end - 1, 3, 0)
    scatter.hand_out(end - 1, 0)
    scatter.hop(end - 1, 3, 1)
    scatter.hand_out(end - 1, 1)
    small.hop(0, 3)
    small.hand_out(0)
    scatter.finish((0, 1))
    small.finish()
    return_end(out_pair)
    line_end()


def backward_call(fsdp, head, tokens, rows, direct, kept):
    groups = 3 * LAYERS
    blocks = fsdp // TP
    span = D // blocks
    cols = span // TP
    anyspace = pl.BlockSpec(memory_space=pl.ANY)
    shape = jax.ShapeDtypeStruct
    dma, plain = pltpu.SemaphoreType.DMA, pltpu.SemaphoreType.REGULAR
    out_shape = (
        shape((2, rows, D), bf16),
        shape((2, rows, D), bf16),
        shape((groups, TP, 256, cols) if direct else (groups, 256, span), bf16),
        shape((1, TP, 32, cols) if direct else (1, 32, span), bf16),
    )
    scratch = [
        pltpu.VMEM((3, 4, 4, HD, D), bf16),
        pltpu.VMEM((LAYERS, 8, D), f32),
        pltpu.VMEM((2, rows, D), f32),
        pltpu.VMEM((2, rows, D), bf16),
        pltpu.VMEM((2, rows, D), bf16),
        pltpu.VMEM((2, rows, D), bf16),
        pltpu.VMEM((2, rows, D), bf16),
        pltpu.VMEM((2, rows, D), bf16),
        pltpu.VMEM((2, rows, 128), f32),
        pltpu.VMEM((2, rows, 768), bf16),
        pltpu.VMEM((2, rows, 256), bf16),
        pltpu.VMEM((2, 8, rows), f32),
        pltpu.VMEM((rows, D), f32),
        pltpu.VMEM((768, rows), bf16),
        pltpu.VMEM((768, rows), bf16),
        pltpu.VMEM((rows, 256), bf16),
        pltpu.VMEM((16, rows), f32),
        pltpu.VMEM((2, rows, HALF), bf16),
        pltpu.VMEM((2, rows, HALF), bf16),
        pltpu.VMEM((2, rows, HALF), bf16),
        pltpu.VMEM((2, 2, rows, HALF), bf16),
        pltpu.VMEM((2, rows, D), bf16),
        pltpu.VMEM((rows, HALF), bf16),
        pltpu.VMEM((rows, D), bf16),
        pltpu.VMEM((6 * (LAYERS + 1), 8, D), f32),
        pltpu.VMEM((LAYERS, 2, 8, D), f32),
    ]
    for slots, thirds, units in ((2, 3, 256), (1, 1, 32)):
        scratch += [
            pltpu.VMEM((slots, 4, units, D), bf16),
            pltpu.VMEM((slots, blocks - 1, 4, units, span), bf16),
            pltpu.VMEM((thirds, 4, units, span), bf16),
            pltpu.VMEM((slots, 2, 3, units, span), bf16),
            pltpu.VMEM((slots, units, span), bf16),
        ]
    scratch += [dma((2,)), dma((2,)), dma((2, 2)), dma((2, 2)), dma((2,)), dma((2,))]
    for slots, thirds, count in ((2, 3, groups), (1, 1, 1)):
        scratch += [
            dma((slots, blocks - 1, 2)), dma((slots, blocks - 1, 2)),
            dma((thirds, 2, 2)), dma((thirds, 2, 2)),
            dma((count, 4, 2)), dma((count, 4, 2)),
            dma((count, 2)),
            plain((slots, blocks - 1)), plain((slots, 2)),
        ]
    scratch += [dma((2,)), dma((2,)), dma((4,)), dma((4,)), dma((2, 4, 2)), dma((2, 4)), dma((16,)), dma((3,))]
    return pl.pallas_call(
        functools.partial(backward_kernel, (fsdp, head, tokens, rows, direct)),
        out_shape=out_shape,
        in_specs=[anyspace] * len(kept),
        out_specs=tuple(anyspace for _ in out_shape),
        scratch_shapes=scratch,
        compiler_params=pltpu.CompilerParams(
            collective_id=1, has_side_effects=True, vmem_limit_bytes=63 << 20
        ),
        name="backward_layers",
    )(*kept)


class Places:
    def __init__(self, fsdp, head):
        self.fsdp, self.head = fsdp, head
        self.blocks = fsdp // TP
        index, plane = lax.axis_index("fsdp"), lax.axis_index("head")
        self.block, self.role, self.plane = index // TP, index % TP, plane

    def pairs(self, move, sends=None):
        found = []
        for block in range(self.blocks):
            for role in range(TP):
                for plane in range(self.head):
                    if sends is not None and not sends(block, role, plane):
                        continue
                    to_block, to_role, to_plane = move(block, role, plane)
                    found.append(
                        (
                            (block * TP + role) * self.head + plane,
                            (to_block * TP + to_role) * self.head + to_plane,
                        )
                    )
        return found

    def role_xor(self, v, bits, sends=None):
        return lax.ppermute(v, AXES, self.pairs(lambda b, r, p: (b, r ^ bits, p), sends))


def by_xor(parts, index):
    a, b, c, d = parts
    odd = (index & 1) == 1
    a, b = jnp.where(odd, b, a), jnp.where(odd, a, b)
    c, d = jnp.where(odd, d, c), jnp.where(odd, c, d)
    top = (index & 2) == 2
    return [jnp.where(top, c, a), jnp.where(top, d, b), jnp.where(top, a, c), jnp.where(top, b, d)]


def pack_inputs(pl, w_qkv, w_out, w_in, w_down, qv_bias, in_bias, gains, shifts):
    cols = w_qkv.shape[2]
    attn = jnp.concatenate([w_qkv.transpose(0, 1, 3, 2), w_out[:, None]], axis=1).reshape(LAYERS, 4, TP, HD, cols)
    inner = w_in.transpose(0, 2, 1).reshape(LAYERS, TP, 4, HD, cols)
    down = w_down.reshape(LAYERS, TP, 4, HD, cols)
    qv = qv_bias.reshape(LAYERS, 1, -1)
    small = jnp.concatenate(
        [
            gains, shifts, in_bias.reshape(LAYERS, 1, cols),
            jnp.pad(qv, ((0, 0), (0, 0), (0, cols - qv.shape[2]))),
            jnp.zeros((LAYERS, 8, cols), bf16),
        ],
        axis=1,
    ).reshape(1, 16 * LAYERS, cols)
    if cols % 128 == 0:
        return attn, inner, down, small, True
    attn = gather_roles(pl, attn.transpose(0, 2, 1, 3, 4).reshape(LAYERS, TP, 256, cols))
    inner, down = [gather_roles(pl, v.reshape(LAYERS, TP, 256, cols)) for v in (inner, down)]
    small = gather_roles(pl, jnp.broadcast_to(small[:, None], (1, TP) + small.shape[1:]))
    attn, inner, down = [v.reshape(LAYERS, 4, HD, TP * cols) for v in (attn, inner, down)]
    return attn, inner, down, small, False


def gather_roles(pl, pack):
    exchanged = [lax.dynamic_index_in_dim(pack, pl.role, 1, False)]
    for bits in (1, 2, 3):
        exchanged.append(pl.role_xor(lax.dynamic_index_in_dim(pack, pl.role ^ bits, 1, False), bits))
    return jnp.concatenate(by_xor(exchanged, pl.role), axis=-1)


def scatter_roles(pl, mine):
    groups, units, width = mine.shape
    mine = mine.reshape(groups, units, TP, width // TP)
    exchanged = [lax.dynamic_index_in_dim(mine, pl.role, 2, False)]
    for bits in (1, 2, 3):
        exchanged.append(pl.role_xor(lax.dynamic_index_in_dim(mine, pl.role ^ bits, 2, False), bits))
    return jnp.stack(by_xor(exchanged, pl.role), axis=1)


def body(images, cotangent, w_qkv, w_out, w_in, w_down, qv_bias, in_bias, gains, shifts):
    fsdp, head = lax.axis_size("fsdp"), lax.axis_size("head")
    places = Places(fsdp, head)
    cols = w_qkv.shape[2]
    per = HD // fsdp
    tokens = images.shape[1]
    rows = -(-tokens // 32) * 32
    attn, inner, down, extras, direct = pack_inputs(
        places, w_qkv, w_out, w_in, w_down, qv_bias, in_bias, gains, shifts
    )
    pad = ((0, 0), (0, rows - tokens), (0, 0))
    kept = forward_call(
        fsdp, head, tokens, rows, direct, jnp.pad(images, pad), jnp.pad(cotangent, pad), attn, inner, down, extras
    )
    block_out, input_grad, grads, small = backward_call(fsdp, head, tokens, rows, direct, kept)
    if not direct:
        grads, small = scatter_roles(places, grads), scatter_roles(places, small)
    grads = grads.astype(f32).reshape(LAYERS, 3, TP, 256, cols)
    attn = grads[:, 0].reshape(LAYERS, TP, 4, HD, cols).transpose(0, 2, 1, 3, 4).reshape(LAYERS, 4, TP * HD, cols)
    small = small.astype(f32).reshape(TP, LAYERS, 16, cols)
    features = small[0, :, 0:6]
    units = jnp.sum(small[:, :, 6:8], axis=0)
    qv = units[:, 1, 0 : 2 * TP * per].reshape(LAYERS, 2, TP * per, 1)
    inner = units[:, 0].reshape(LAYERS, cols, 1)
    return (
        block_out[:, :tokens].astype(f32),
        input_grad[:, :tokens].astype(f32),
        attn[:, :3].transpose(0, 1, 3, 2),
        attn[:, 3],
        grads[:, 1].reshape(LAYERS, TP * 256, cols).transpose(0, 2, 1),
        grads[:, 2].reshape(LAYERS, TP * 256, cols),
        qv,
        inner,
        features[:, 0:2],
        features[:, 2:6],
    )


def solution(mesh):
    placed = (
        P("fsdp", None, None),
        P("fsdp", None, None),
        P(None, None, "fsdp", "head"),
        P(None, "head", "fsdp"),
        P(None, "fsdp", "head"),
        P(None, "head", "fsdp"),
        P(None, None, "head", "fsdp"),
        P(None, "head", "fsdp"),
        P(None, None, "fsdp"),
        P(None, None, "fsdp"),
    )
    return jax.shard_map(
        body, mesh=mesh, in_specs=placed, out_specs=placed, check_vma=False
    )
```

```python
import functools
import math

import jax
import jax.numpy as jnp
from jax import lax
from jax.experimental import pallas as pl
from jax.experimental.pallas import tpu as pltpu
from jax.sharding import PartitionSpec as P

D = 1024
HD = 64
LAYERS = 2
TP = 4
HALF = D // 2
AXES = ("fsdp", "head")
MESH = pl.DeviceIdType.MESH
epsilon = 1e-06
f32, bf16 = jnp.float32, jnp.bfloat16


def dot(left, right, left_dim, right_dim):
    return lax.dot_general(
        left, right, (((left_dim,), (right_dim,)), ((), ())), preferred_element_type=f32
    )


def flip1(n):
    return n + 1 - 2 * (n % 2)


def flip2(n):
    return n + 2 - 4 * ((n // 2) % 2)


def flip(n, bits):
    if bits & 1:
        n = flip1(n)
    if bits & 2:
        n = flip2(n)
    return n


class Spot:
    def __init__(self, fsdp, head):
        self.blocks = fsdp // TP
        self.planes = head
        index = lax.axis_index("fsdp")
        self.index = index
        self.block, self.role, self.plane = index // TP, index % TP, lax.axis_index("head")
        self.core = self.role % 2
        self.image = (self.role // 2 + self.plane) % 2

    def at(self, block=None, role=None, plane=None):
        block = self.block if block is None else block
        role = self.role if role is None else role
        plane = self.plane if plane is None else plane
        return (block * TP + role, plane)

    def partners(self):
        found = [self.at(role=flip(self.role, o)) for o in (1, 2, 3)]
        found += [self.at(plane=flip(self.plane, o)) for o in (1, 2, 3)]
        found += [self.at(block=(self.block + s) % self.blocks) for s in range(1, self.blocks)]
        return found


def greet(partners):
    barrier = pltpu.get_barrier_semaphore()
    for partner in partners:
        pl.semaphore_signal(barrier, inc=1, device_id=partner, device_id_type=MESH)
    pl.semaphore_wait(barrier, len(partners))


def send(source, target, sems, where, device):
    return pltpu.make_async_remote_copy(
        src_ref=source,
        dst_ref=target,
        send_sem=sems[0].at[where],
        recv_sem=sems[1].at[where],
        device_id=device,
        device_id_type=MESH,
    )


def lanes(start, size):
    return pl.ds(pl.multiple_of(start, 128), size)


class Gather:
    def __init__(self, spot, source, whole, role_sems, plane_sems, block_sems, base, local_sem, direct):
        self.spot, self.source, self.whole, self.direct = spot, source, whole, direct
        self.role_sems, self.plane_sems, self.block_sems = role_sems, plane_sems, block_sems
        self.base, self.local_sem = base, local_sem
        self.blocks_first = ()
        self.cols = D // spot.blocks // TP
        self.span = D // spot.blocks

    def piece(self, g, plane, block):
        return self.whole.at[g, plane, :, :, lanes(block * self.span, self.span)]

    def own(self, g):
        spot = self.spot
        if self.direct:
            return pltpu.make_async_copy(
                self.source(g, spot.role),
                self.whole.at[g, spot.plane, :, :, lanes(spot.index * self.cols, self.cols)],
                self.local_sem.at[self.base + g],
            )
        return pltpu.make_async_copy(
            self.source(g, None), self.piece(g, spot.plane, spot.block), self.local_sem.at[self.base + g]
        )

    def to_role(self, g, o):
        spot = self.spot
        other = flip(spot.role, o)
        return send(
            self.source(g, other),
            self.whole.at[g, spot.plane, :, :, lanes(spot.index * self.cols, self.cols)],
            self.role_sems,
            (self.base + g, o),
            spot.at(role=other),
        )

    def from_role(self, g, o):
        spot = self.spot
        other = flip(spot.role, o)
        place = self.whole.at[
            g, spot.plane, :, :, lanes((spot.block * TP + other) * self.cols, self.cols)
        ]
        return send(place, place, self.role_sems, (self.base + g, o), spot.at(role=other))

    def hop(self, g, d, up, taken):
        plane = self.spot.plane
        step = 1 if up else -1
        piece = plane - step * d if taken else plane - step * (d - 1)
        place = self.whole.at[g, piece] if g in self.blocks_first else self.piece(g, piece, self.spot.block)
        other = plane - step if taken else plane + step
        return send(
            place, place, self.plane_sems, (self.base + g, d - 1 + (0 if up else 3)), self.spot.at(plane=other)
        )

    def has(self, d, up):
        return self.spot.plane >= d if up else self.spot.plane + d < self.spot.planes

    def goes(self, d, up):
        plane, last = self.spot.plane, self.spot.planes - 1
        if up:
            return jnp.logical_and(plane >= d, plane < last)
        return jnp.logical_and(plane + d <= last, plane > 0)

    def to_block(self, g, s, d, up, taken=False):
        spot = self.spot
        plane = spot.plane - d if up else spot.plane + d
        shift = spot.blocks - s if taken else s
        block = (spot.block + shift) % spot.blocks
        place = self.piece(g, plane, block if taken else spot.block)
        where = (self.base + g, s, d + (0 if up or d == 0 else 3))
        return send(place, place, self.block_sems, where, spot.at(block=block))

    def begin(self, g):
        self.own(g).start()
        if self.direct:
            for o in (1, 2, 3):
                self.to_role(g, o).start()

    def onward(self, g, d):
        for up in (True, False):
            if d < self.spot.planes - 1:
                @pl.when(self.goes(d, up))
                def _():
                    self.hop(g, d + 1, up, False).start()

    def spread(self, g):
        self.own(g).wait()
        if self.direct:
            for o in (1, 2, 3):
                self.from_role(g, o).wait_recv()
        if g not in self.blocks_first:
            self.onward(g, 0)
        for s in range(1, self.spot.blocks):
            self.to_block(g, s, 0, True).start()

    def lift(self, g):
        for s in range(1, self.spot.blocks):
            self.to_block(g, s, 0, True, True).wait_recv()
        self.onward(g, 0)

    def relay(self, g, d):
        for up in (True, False):
            @pl.when(self.has(d, up))
            def _():
                self.hop(g, d, up, True).wait_recv()
        self.onward(g, d)
        if g in self.blocks_first:
            return
        for up in (True, False):
            @pl.when(self.has(d, up))
            def _():
                for s in range(1, self.spot.blocks):
                    self.to_block(g, s, d, up).start()

    def complete(self, g):
        for s in range(1, self.spot.blocks):
            self.to_block(g, s, 0, True, True).wait_recv()
            for d in (1, 2, 3):
                for up in (True, False):
                    @pl.when(self.has(d, up))
                    def _():
                        self.to_block(g, s, d, up, True).wait_recv()

    def drain(self, g):
        for d in (0, 1, 2, 3):
            if self.direct and d > 0:
                self.to_role(g, d).wait_send()
            for up in (True, False):
                if d < 3:
                    @pl.when(self.goes(d, up))
                    def _():
                        self.hop(g, d + 1, up, False).wait_send()
                if d > 0 and g not in self.blocks_first:
                    @pl.when(self.has(d, up))
                    def _():
                        for s in range(1, self.spot.blocks):
                            self.to_block(g, s, d, up).wait_send()
        for s in range(1, self.spot.blocks):
            self.to_block(g, s, 0, True).wait_send()


class Exchange:
    def __init__(self, spot, sent, core_in, chip, side_in, full, core_sems, side_sems, back_sems):
        self.spot = spot
        self.sent, self.core_in, self.chip, self.side_in, self.full = sent, core_in, chip, side_in, full
        self.core_sems, self.side_sems, self.back_sems = core_sems, side_sems, back_sems
        self.mine = lanes(spot.core * HALF, HALF)
        self.theirs = lanes((1 - spot.core) * HALF, HALF)

    def core_copy(self, i):
        return send(
            self.sent.at[i], self.core_in.at[i], self.core_sems, (i,),
            self.spot.at(role=flip1(self.spot.role)),
        )

    def side_copy(self, i, slot):
        return send(
            self.chip.at[i], self.side_in.at[i, slot], self.side_sems, (i, slot),
            self.spot.at(role=flip2(self.spot.role)),
        )

    def back_copy(self, i):
        place = self.full.at[i, :, self.mine]
        return send(place, place, self.back_sems, (i,), self.spot.at(role=flip1(self.spot.role)))

    def back_in(self, i):
        place = self.full.at[i, :, self.theirs]
        return send(place, place, self.back_sems, (i,), self.spot.at(role=flip1(self.spot.role)))

    def reduce(self, i, product, kept):
        self.sent[i] = product(self.theirs).astype(bf16)
        self.core_copy(i).start()
        kept[...] = product(self.mine)
        copy = self.core_copy(i)
        copy.wait_recv()
        self.chip[i] = (kept[...] + self.core_in[i].astype(f32)).astype(bf16)
        copy.wait_send()

    def finish(self, i, slot):
        copy = self.side_copy(i, slot)
        copy.wait_recv()
        total = self.chip[i].astype(f32) + self.side_in[i, slot].astype(f32)
        self.full[i, :, self.mine] = total.astype(bf16)
        self.back_copy(i).start()
        copy.wait_send()
        self.back_in(i).wait_recv()
        self.back_copy(i).wait_send()


def each_rows(rows, size, step, unroll=1):
    def one(c, carry):
        step(pl.ds(pl.multiple_of(c * size, size), size))
        return carry

    lax.fori_loop(0, rows // size, one, 0, unroll=unroll)


def unit_picks(held, fsdp, role):
    cols = D // fsdp
    per = HD // fsdp
    bits = fsdp.bit_length() - 1
    for first, count, offset in (
        (0, 256, role * (4 * per)), (256, HD, role * per), (256 + HD, HD, TP * per + role * per)
    ):
        unit = lax.broadcasted_iota(jnp.int32, (count, D), 0)
        place = lax.broadcasted_iota(jnp.int32, (count, D), 1)
        wanted = (unit & (fsdp - 1)) * cols + (unit >> bits) + offset
        held[first : first + count] = jnp.where(place == wanted, 1.0, 0.0).astype(bf16)


def forward_kernel(cfg, *refs):
    fsdp, head, tokens, rows, direct = cfg
    (
        images, cotangents, attn_source, in_source, down_source, extras,
        weights_out, vec_out, normed_out, unit_out, inverse_out, qkv_out, att_out, lse_out, hidden_out,
        stream_out, chip_out, cot_out,
        whole, extra, vec, pair, cots, stream, normed, unit, inverse, qkv, att_sum, att,
        values, lse_rows, low_hidden, active, kept,
        sent, core_in, chip, side_in, full,
        role_s, role_r, plane_s, plane_r, block_s, block_r, local_sem,
        core_s, core_r, side_s, side_r, back_s, back_r,
        share_s, share_r, store_sem,
    ) = refs
    spot = Spot(fsdp, head)
    groups = 3 * LAYERS
    greet(spot.partners())
    sems = ((role_s, role_r), (plane_s, plane_r), (block_s, block_r))

    def source(g, role):
        l, k = g // 3, g % 3
        held = (attn_source, in_source, down_source)[k]
        if role is None:
            return held.at[l]
        return held.at[l, :, role] if k == 0 else held.at[l, role]

    small = Gather(spot, lambda g, role: extras, extra, *sems, groups, local_sem, direct)
    large = Gather(spot, source, whole, *sems, 0, local_sem, direct)
    large.blocks_first = (groups - 1,)
    own_image, own_cot = images.at[spot.plane // 2], cotangents.at[spot.plane // 2]
    exchange = Exchange(
        spot, sent, core_in, chip, side_in, full, (core_s, core_r), (side_s, side_r), (back_s, back_r)
    )
    owner = spot.core == spot.plane % 2
    x, other_x = spot.image, 1 - spot.image

    small.begin(0)
    large.begin(0)

    def share(source, held, n):
        across = send(
            source, held.at[x], (share_s, share_r), (n, 0), spot.at(role=flip2(spot.role))
        )
        across_in = send(
            held.at[other_x], held.at[other_x], (share_s, share_r), (n, 0), spot.at(role=flip2(spot.role))
        )
        down = [
            send(src, held.at[at], (share_s, share_r), (n, 1 + k), spot.at(role=flip1(spot.role)))
            for k, (src, at) in enumerate(((source, x), (held.at[other_x], other_x)))
        ]
        mine = pltpu.make_async_copy(source, held.at[x], store_sem.at[30 + n])
        return across, across_in, down, mine

    def share_begin(source, held, n):
        across, across_in, down, mine = share(source, held, n)

        @pl.when(owner)
        def _():
            across.start()
            mine.start()
            down[0].start()

    def share_end(source, held, n):
        across, across_in, down, mine = share(source, held, n)

        @pl.when(owner)
        def _():
            across_in.wait_recv()
            down[1].start()
            across.wait_send()
            mine.wait()
            down[0].wait_send()
            down[1].wait_send()

        @pl.when(jnp.logical_not(owner))
        def _():
            down[0].wait_recv()
            down[1].wait_recv()

    large.spread(0)
    small.spread(0)
    large.begin(1)
    share_begin(own_image, pair, 0)
    for g in (2, 5, 3, 4):
        large.begin(g)
    small.relay(0, 1)
    large.relay(0, 1)
    large.spread(1)
    small.relay(0, 2)
    large.relay(0, 2)
    small.relay(0, 3)
    large.relay(0, 3)
    large.relay(1, 1)
    large.spread(2)
    large.spread(5)
    share_end(own_image, pair, 0)
    small.complete(0)

    unit_picks(active, fsdp, spot.role)
    for l in range(LAYERS):
        vec[l, 0:6] = extra[0, 0, 0, 16 * l : 16 * l + 16].astype(f32)[0:6]
        for plane in range(4):
            units = dot(extra[0, plane, 0, 16 * l : 16 * l + 16], active[0:384], 1, 1)
            vec[l, 6:7, plane * 256 : plane * 256 + 256] = units[6:7, 0:256]
            if plane % 2 == 0:
                before = units
            else:
                for k in range(2):
                    at = slice(256 + k * HD, 256 + k * HD + HD)
                    to = k * 256 + (plane - 1) * HD
                    vec[l, 7:8, to : to + 128] = jnp.concatenate([before[7:8, at], units[7:8, at]], axis=1)
    store_vec = pltpu.make_async_copy(vec, vec_out, store_sem.at[28])
    store_vec.start()
    large.complete(0)

    lane_pair = lax.broadcasted_iota(jnp.int32, (1, 128), 1) // HD
    valid = lax.broadcasted_iota(jnp.int32, (rows, 1), 0) < tokens

    def stores(l, n, i):
        return [
            pltpu.make_async_copy(normed.at[i], normed_out.at[l, n, i], store_sem.at[0 + i]),
            pltpu.make_async_copy(unit.at[i], unit_out.at[l, n, i], store_sem.at[2 + i]),
            pltpu.make_async_copy(inverse.at[i], inverse_out.at[l, n, i], store_sem.at[4 + i]),
        ]

    def norm(l, n, i, v):
        stream[i] = v
        average = jnp.mean(v, axis=-1, keepdims=True)
        centred = v - average
        scale = lax.rsqrt(jnp.mean(centred * centred, axis=-1, keepdims=True) + epsilon)
        u = centred * scale
        unit[i] = u.astype(bf16)
        inverse[i] = jnp.broadcast_to(scale, (rows, 128))
        normed[i] = (u * vec[l, n : n + 1] + vec[l, 2 + n : 3 + n]).astype(bf16)
        for copy in stores(l, n, i):
            copy.start()

    def attn_stage(l, i):
        g = 3 * l

        @pl.when(l > 0)
        def _():
            exchange.finish(i, 1)
            for copy in stores(l - 1, 1, i):
                copy.wait()
            before = jnp.maximum(l - 1, 0)
            norm(l, 0, i, stream[i] + full[i].astype(f32) + vec[before, 5:6])

        @pl.when(l == 0)
        def _():
            norm(l, 0, i, pair[i].astype(f32))

        store_qkv = pltpu.make_async_copy(qkv, qkv_out.at[l, i], store_sem.at[6])
        store_att = pltpu.make_async_copy(att.at[i], att_out.at[l, i], store_sem.at[8 + i])
        store_lse = pltpu.make_async_copy(lse_rows.at[i], lse_out.at[l, i], store_sem.at[10 + i])

        @pl.when(l + i > 0)
        def _():
            store_qkv.wait()

        @pl.when(l > 0)
        def _():
            store_att.wait()
            store_lse.wait()

        for k in range(3):
            w = whole[g, :, k].reshape(256, D)
            part = dot(normed[i], w, 1, 1)
            if k == 0:
                part = part + vec[l, 7:8, 0:256]
            if k == 2:
                part = part + vec[l, 7:8, 256:512]
                values[...] = jnp.transpose(part).astype(bf16)
            qkv[:, k * 256 : k * 256 + 256] = part.astype(bf16)
        store_qkv.start()
        def one_head(h, carry):
            two = lanes(h // 2 * 128, 128)
            key_two = lanes(256 + h // 2 * 128, 128)
            low_mask = jnp.where(lane_pair == h % 2, HD ** (-0.5), 0.0).astype(bf16)
            s = dot(qkv[:, key_two], qkv[:, two] * low_mask, 1, 1)
            s = jnp.where(valid, s, -1e30)
            largest = jnp.max(s, axis=0, keepdims=True)
            e = jnp.exp(s - largest)
            total = jnp.sum(e, axis=0, keepdims=True)
            lse_rows[i, pl.ds(h, 1)] = largest + jnp.log(total)
            at = pl.ds(pl.multiple_of(h * HD, HD), HD)
            att_sum[at] = dot(values[at], e.astype(bf16), 1, 0) * (1.0 / total)
            return carry

        lax.fori_loop(0, 4, one_head, 0)
        att[i] = jnp.transpose(att_sum[...]).astype(bf16)
        store_att.start()
        store_lse.start()

        @pl.when(jnp.logical_and(l == 0, i == 0))
        def _():
            large.relay(1, 2)

        @pl.when(jnp.logical_and(l == 0, i == 1))
        def _():
            large.relay(1, 3)
            large.relay(2, 2)

        exchange.reduce(
            i, lambda at: dot(att[i], whole[g, :, 3, :, at].reshape(256, HALF), 1, 0), kept
        )
        exchange.side_copy(i, 0).start()

    def mlp_stage(l, i):
        g = 3 * l
        exchange.finish(i, 0)
        for copy in stores(l, 0, i):
            copy.wait()
        norm(l, 1, i, stream[i] + full[i].astype(f32) + vec[l, 4:5])
        store_hidden = pltpu.make_async_copy(low_hidden.at[i], hidden_out.at[l, i], store_sem.at[12 + i])

        @pl.when(l > 0)
        def _():
            store_hidden.wait()

        for k in range(4):
            at = slice(k * 256, k * 256 + 256)
            v = dot(normed[i], whole[g + 1, k].reshape(256, D), 1, 1) + vec[l, 6:7, at]
            low_hidden[i, :, at] = v.astype(bf16)
            active[:, at] = (v * (0.5 + 0.5 * lax.erf(v * (0.5**0.5)))).astype(bf16)
        store_hidden.start()

        @pl.when(jnp.logical_and(l == 0, i == 0))
        def _():
            large.relay(3, 2)

        @pl.when(jnp.logical_and(l == 0, i == 1))
        def _():
            large.relay(5, 1)
            large.relay(4, 2)

        @pl.when(jnp.logical_and(i == 0, l < LAYERS - 1))
        def _():
            large.complete(g + 2)


        exchange.reduce(i, lambda at: dot(active[...], whole[g + 2, :, :, :, at].reshape(D, HALF), 1, 0), kept)

        @pl.when(l < LAYERS - 1)
        def _():
            exchange.side_copy(i, 1).start()

        @pl.when(l == LAYERS - 1)
        def _():
            pltpu.make_async_copy(chip.at[i], chip_out.at[i], store_sem.at[14 + i]).start()
            pltpu.make_async_copy(stream.at[i], stream_out.at[i], store_sem.at[16 + i]).start()

    def store_weights(g):
        return pltpu.make_async_copy(whole.at[g], weights_out.at[g], store_sem.at[18 + g])

    def one_layer(l, carry):
        g = 3 * l

        @pl.when(l > 0)
        def _():
            large.complete(g)

        def attn_image(i, carry):
            attn_stage(l, i)

            @pl.when(jnp.logical_and(l == 0, i == 0))
            def _():
                share_begin(own_cot, cots, 1)
                large.relay(2, 1)
                large.spread(3)

            @pl.when(jnp.logical_and(l > 0, i == 0))
            def _():
                large.relay(5, 3)

            return carry

        lax.fori_loop(0, 2, attn_image, 0)

        @pl.when(l == 0)
        def _():
            large.relay(3, 1)
            large.spread(4)
            large.relay(2, 3)
            large.lift(5)

        large.complete(g + 1)

        def mlp_image(i, carry):
            mlp_stage(l, i)

            @pl.when(jnp.logical_and(l == 0, i == 0))
            def _():
                large.relay(4, 1)
                large.relay(3, 3)

            return carry

        lax.fori_loop(0, 2, mlp_image, 0)

        @pl.when(l == 0)
        def _():
            large.relay(4, 3)
            large.relay(5, 2)

        for k in range(3):
            store_weights(g + k).start()
        return carry

    lax.fori_loop(0, LAYERS, one_layer, 0)
    share_end(own_cot, cots, 1)
    store_cots = pltpu.make_async_copy(cots, cot_out, store_sem.at[29])
    store_cots.start()
    last = LAYERS - 1
    for i in range(2):
        for copy in stores(last, 1, i):
            copy.wait()
        pltpu.make_async_copy(att.at[i], att_out.at[last, i], store_sem.at[8 + i]).wait()
        pltpu.make_async_copy(lse_rows.at[i], lse_out.at[last, i], store_sem.at[10 + i]).wait()
        pltpu.make_async_copy(low_hidden.at[i], hidden_out.at[last, i], store_sem.at[12 + i]).wait()
        pltpu.make_async_copy(chip.at[i], chip_out.at[i], store_sem.at[14 + i]).wait()
        pltpu.make_async_copy(stream.at[i], stream_out.at[i], store_sem.at[16 + i]).wait()
    pltpu.make_async_copy(qkv, qkv_out.at[last, 1], store_sem.at[6]).wait()
    store_vec.wait()
    store_cots.wait()

    for g in range(groups):
        store_weights(g).wait()
        large.drain(g)
    small.drain(0)


def forward_call(fsdp, head, tokens, rows, direct, *operands):
    groups = 3 * LAYERS
    blocks = fsdp // TP
    anyspace = pl.BlockSpec(memory_space=pl.ANY)
    shape = jax.ShapeDtypeStruct
    dma = pltpu.SemaphoreType.DMA
    out_shape = (
        shape((groups, 4, 4, HD, D), bf16),
        shape((LAYERS, 8, D), f32),
        shape((LAYERS, 2, 2, rows, D), bf16),
        shape((LAYERS, 2, 2, rows, D), bf16),
        shape((LAYERS, 2, 2, rows, 128), f32),
        shape((LAYERS, 2, rows, 768), bf16),
        shape((LAYERS, 2, rows, 256), bf16),
        shape((LAYERS, 2, 8, rows), f32),
        shape((LAYERS, 2, rows, D), bf16),
        shape((2, rows, D), f32),
        shape((2, rows, HALF), bf16),
        shape((2, rows, D), bf16),
    )
    scratch = [
        pltpu.VMEM((groups, 4, 4, HD, D), bf16),
        pltpu.VMEM((1, 4, 1, 32, D), bf16),
        pltpu.VMEM((LAYERS, 8, D), f32),
        pltpu.VMEM((2, rows, D), bf16),
        pltpu.VMEM((2, rows, D), bf16),
        pltpu.VMEM((2, rows, D), f32),
        pltpu.VMEM((2, rows, D), bf16),
        pltpu.VMEM((2, rows, D), bf16),
        pltpu.VMEM((2, rows, 128), f32),
        pltpu.VMEM((rows, 768), bf16),
        pltpu.VMEM((256, rows), f32),
        pltpu.VMEM((2, rows, 256), bf16),
        pltpu.VMEM((256, rows), bf16),
        pltpu.VMEM((2, 8, rows), f32),
        pltpu.VMEM((2, rows, D), bf16),
        pltpu.VMEM((rows, D), bf16),
        pltpu.VMEM((rows, HALF), f32),
        pltpu.VMEM((2, rows, HALF), bf16),
        pltpu.VMEM((2, rows, HALF), bf16),
        pltpu.VMEM((2, rows, HALF), bf16),
        pltpu.VMEM((2, 2, rows, HALF), bf16),
        pltpu.VMEM((2, rows, D), bf16),
        dma((groups + 1, 4)), dma((groups + 1, 4)),
        dma((groups + 1, 6)), dma((groups + 1, 6)),
        dma((groups + 1, blocks, 7)), dma((groups + 1, blocks, 7)),
        dma((groups + 1,)),
        dma((2,)), dma((2,)),
        dma((2, 2)), dma((2, 2)),
        dma((2,)), dma((2,)),
        dma((2, 3)), dma((2, 3)),
        dma((32,)),
    ]
    return pl.pallas_call(
        functools.partial(forward_kernel, (fsdp, head, tokens, rows, direct)),
        out_shape=out_shape,
        in_specs=[anyspace] * len(operands),
        out_specs=tuple(anyspace for _ in out_shape),
        scratch_shapes=scratch,
        compiler_params=pltpu.CompilerParams(
            collective_id=0, has_side_effects=True, vmem_limit_bytes=60 << 20
        ),
        name="forward_layers",
    )(*operands)


class Scatter:
    def __init__(self, spot, count, term, block_in, total, plane_in, mine, out, block_sems, plane_sems, role_sems, local_sem, block_free, plane_free, direct):
        self.spot, self.count, self.direct = spot, count, direct
        self.term, self.block_in, self.total = term, block_in, total
        self.plane_in, self.mine, self.out = plane_in, mine, out
        self.block_sems, self.plane_sems, self.role_sems, self.local_sem = block_sems, plane_sems, role_sems, local_sem
        self.block_free, self.plane_free = block_free, plane_free
        self.span = D // spot.blocks
        self.cols = self.span // TP
        self.own = lanes(spot.block * self.span, self.span)

    def slot(self, n):
        return n % self.term.shape[0]

    def third(self, n):
        return n % self.total.shape[0]

    def rows(self, part):
        units = self.term.shape[2]
        return slice(0, units) if part is None else slice(part * units // 2, (part + 1) * units // 2)

    def to_block(self, n, s, part=None):
        block = (self.spot.block + s) % self.spot.blocks
        a, r = self.slot(n), self.rows(part)
        return send(
            self.term.at[a, :, r, lanes(block * self.span, self.span)],
            self.block_in.at[a, s - 1, :, r],
            self.block_sems, (a, s - 1, part or 0), self.spot.at(block=block),
        )

    def along(self, n, plane, up, part=None):
        planes = self.spot.planes
        a, c = self.slot(n), self.third(n)
        first, number = (plane + 1, planes - 1 - plane) if up else (0, plane)
        way, r = 0 if up else 1, self.rows(part)
        return send(
            self.total.at[c, first : first + number, r], self.plane_in.at[a, way, 0:number, r],
            self.plane_sems, (c, way, part or 0), self.spot.at(plane=plane + (1 if up else -1)),
        )

    def to_role(self, n, o, part=None):
        other = flip(self.spot.role, o)
        g, r = self.count - 1 - n, self.rows(part)
        return send(
            self.mine.at[self.slot(n), r, lanes(other * self.cols, self.cols)],
            self.out.at[g, self.spot.role, r],
            self.role_sems, (g, o, part or 0), self.spot.at(role=other),
        )

    def from_role(self, g, o, part=None):
        other = flip(self.spot.role, o)
        place = self.out.at[g, other, self.rows(part)]
        return send(place, place, self.role_sems, (g, o, part or 0), self.spot.at(role=other))

    def keep(self, n, part=None):
        g, r = self.count - 1 - n, self.rows(part)
        if self.direct:
            return pltpu.make_async_copy(
                self.mine.at[self.slot(n), r, lanes(self.spot.role * self.cols, self.cols)],
                self.out.at[g, self.spot.role, r], self.local_sem.at[g, part or 0],
            )
        return pltpu.make_async_copy(
            self.mine.at[self.slot(n), r], self.out.at[g, r], self.local_sem.at[g, part or 0]
        )

    def before_terms(self, n):
        @pl.when(n >= 2)
        def _():
            for s in range(1, self.spot.blocks):
                self.to_block(n - 2, s).wait_send()

    def send_terms(self, n, parts=(None,)):
        for s in range(1, self.spot.blocks):
            @pl.when(n >= 2)
            def _():
                pl.semaphore_wait(self.block_free.at[self.slot(n), s - 1], 1)

            for part in parts:
                self.to_block(n, s, part).start()

    def pass_on(self, n, plane, up, part=None):
        if not part:
            @pl.when(n >= 2)
            def _():
                pl.semaphore_wait(self.plane_free.at[self.slot(n), 0 if up else 1], 1)

        self.along(n, plane, up, part).start()

    def sent_along(self, n, part=None):
        for plane in range(self.spot.planes):
            @pl.when(self.spot.plane == plane)
            def _():
                if plane < self.spot.planes - 1:
                    self.along(n, plane, True, part).wait_send()
                if plane > 0:
                    self.along(n, plane, False, part).wait_send()

    def sum_blocks(self, n, part=None):
        a, c, r = self.slot(n), self.third(n), self.rows(part)
        for s in range(1, self.spot.blocks):
            self.to_block(n, s, part).wait_recv()

        if not part:
            @pl.when(n >= 3)
            def _():
                self.sent_along(n - 3)

        for plane in range(self.spot.planes):
            value = self.term[a, plane, r, self.own].astype(f32)
            for s in range(1, self.spot.blocks):
                value = value + self.block_in[a, s - 1, plane, r].astype(f32)
            self.total[c, plane, r] = value.astype(bf16)

        @pl.when(n + 2 < self.count)
        def _():
            for s in range(1, self.spot.blocks):
                source = (self.spot.block + self.spot.blocks - s) % self.spot.blocks
                pl.semaphore_signal(
                    self.block_free.at[a, s - 1], inc=1, device_id=self.spot.at(block=source), device_id_type=MESH
                )

        last = self.spot.planes - 1

        @pl.when(self.spot.plane == 0)
        def _():
            self.pass_on(n, 0, True, part)

        @pl.when(self.spot.plane == last)
        def _():
            self.pass_on(n, last, False, part)

    def take(self, n, plane, up, part):
        a, c, r = self.slot(n), self.third(n), self.rows(part)
        before = plane - 1 if up else plane + 1
        self.along(n, before, up, part).wait_recv()
        planes = range(plane, self.spot.planes) if up else range(0, plane + 1)
        for at, p in enumerate(planes):
            value = self.total[c, p, r].astype(f32) + self.plane_in[a, 0 if up else 1, at, r].astype(f32)
            self.total[c, p, r] = value.astype(bf16)

        @pl.when(n + 2 < self.count)
        def _():
            pl.semaphore_signal(
                self.plane_free.at[a, 0 if up else 1], inc=1, device_id=self.spot.at(plane=before), device_id_type=MESH
            )

        if (up and plane < self.spot.planes - 1) or (not up and plane > 0):
            self.pass_on(n, plane, up, part)

    def hop(self, n, d, part=None):
        for plane, up in ((d, True), (self.spot.planes - 1 - d, False)):
            @pl.when(self.spot.plane == plane)
            def _():
                self.take(n, plane, up, part)

    def hand_out(self, n, part=None):
        a, r = self.slot(n), self.rows(part)

        if not part:
            @pl.when(n >= 2)
            def _():
                self.keep(n - 2).wait()
                if self.direct:
                    for o in (1, 2, 3):
                        self.to_role(n - 2, o).wait_send()

        self.mine[a, r] = self.total[self.third(n), self.spot.plane, r]
        self.keep(n, part).start()
        if self.direct:
            for o in (1, 2, 3):
                self.to_role(n, o, part).start()

    def finish(self, parts=(None,)):
        last = self.count - 1
        for n in range(max(0, last - 2), last + 1):
            for part in parts if n == last else (None,):
                self.sent_along(n, part)
        for n in range(max(0, last - 1), last + 1):
            for part in parts if n == last else (None,):
                self.keep(n, part).wait()
                for s in range(1, self.spot.blocks):
                    self.to_block(n, s, part).wait_send()
                if self.direct:
                    for o in (1, 2, 3):
                        self.to_role(n, o, part).wait_send()
        if self.direct:
            for g in range(self.count):
                for o in (1, 2, 3):
                    for part in parts if g == 0 else (None,):
                        self.from_role(g, o, part).wait_recv()


def backward_kernel(cfg, *refs):
    fsdp, head, tokens, rows, direct = cfg
    (
        weights_in, vec_in, normed_in, unit_in, inverse_in, qkv_in, att_in, lse_in, hidden_in,
        stream_in, chip_in, cot_in,
        out_pair, in_pair, grads, small_grads,
        weight, vec, up, up_low, hid, gh, normed, unit, inverse, qkv, att, lse, big, grad_rows, flipped, gab, along,
        sent, core_in, chip, side_in, full, last_in, result, sums, unit_sums,
        term, block_in, total, plane_in, mine,
        small_term, small_block_in, small_total, small_plane_in, small_mine,
        core_s, core_r, side_s, side_r, back_s, back_r,
        block_s, block_r, plane_s, plane_r, role_s, role_r, local_sem, block_free, plane_free,
        small_block_s, small_block_r, small_plane_s, small_plane_r, small_role_s, small_role_r, small_local,
        small_block_free, small_plane_free,
        last_s, last_r, out_s, out_r, line_s, line_r, load_sem, weight_sem,
    ) = refs
    kept = big.at[:, 0:HALF]
    spot = Spot(fsdp, head)
    greet(spot.partners())
    exchange = Exchange(
        spot, sent, core_in, chip, side_in, full, (core_s, core_r), (side_s, side_r), (back_s, back_r)
    )
    scatter = Scatter(
        spot, 3 * LAYERS, term, block_in, total, plane_in, mine, grads, (block_s, block_r), (plane_s, plane_r),
        (role_s, role_r), local_sem, block_free, plane_free, direct,
    )
    small = Scatter(
        spot, 1, small_term, small_block_in, small_total, small_plane_in, small_mine, small_grads,
        (small_block_s, small_block_r), (small_plane_s, small_plane_r), (small_role_s, small_role_r),
        small_local, small_block_free, small_plane_free, direct,
    )
    owner = spot.core == spot.plane % 2
    top = LAYERS - 1

    def load(source, target, n):
        return pltpu.make_async_copy(source, target, load_sem.at[n])

    def load_weight(l, k):
        return pltpu.make_async_copy(weights_in.at[3 * l + k], weight.at[k], weight_sem.at[k])

    load_vec = load(vec_in, vec, 0)
    load_cot = load(cot_in, up_low, 1)
    last_chip = qkv.at[:, :, 0:HALF]
    load_chip = load(chip_in, last_chip, 2)

    def load_hidden(l):
        return load(hidden_in.at[l], hid, 4)

    def load_normed(l, n):
        return load(normed_in.at[l, n], normed, 5)

    def load_unit(l, n):
        return [load(unit_in.at[l, n], unit, 6), load(inverse_in.at[l, n], inverse, 7)]

    def load_attn(l):
        return [load(qkv_in.at[l], qkv, 8), load(att_in.at[l], att, 9), load(lse_in.at[l], lse, 10)]

    load_chip.start()
    load_cot.start()
    load_weight(top, 2).start()
    load_hidden(top).start()
    load_vec.start()
    load_weight(top, 1).start()
    load_weight(top, 0).start()
    load_normed(top, 1).start()
    for copy in load_unit(top, 1):
        copy.start()

    last_copy = send(
        last_chip.at[1 - spot.image], last_in, (last_s, last_r), (0,), spot.at(role=flip2(spot.role))
    )
    half_copy = send(
        result.at[:, exchange.mine], result.at[:, exchange.mine], (last_s, last_r), (1,),
        spot.at(role=flip1(spot.role)),
    )
    half_in = send(
        result.at[:, exchange.theirs], result.at[:, exchange.theirs], (last_s, last_r), (1,),
        spot.at(role=flip1(spot.role)),
    )
    load_chip.wait()
    last_copy.start()

    sums[...] = jnp.zeros_like(sums)
    unit_sums[...] = jnp.zeros_like(unit_sums)
    load_cot.wait()

    def eights(v):
        return jnp.sum(v.reshape(v.shape[0] // 8, 8, v.shape[1]), axis=0)

    for i in range(2):
        for start in range(0, rows, 128):
            r = slice(start, min(rows, start + 128))
            v = up_low[i, r].astype(f32)
            up[i, r] = v
            sums[(top + 1) * 6 + 5] += eights(v)
    load_vec.wait()

    def return_copies(pair_out):
        slot = spot.plane // 2
        mine_copy = pltpu.make_async_copy(result, pair_out.at[slot], load_sem.at[12])
        outs = [
            send(result, pair_out.at[slot], (out_s, out_r), (o,), spot.at(plane=flip(spot.plane, o)))
            for o in (1, 2, 3)
        ]
        return mine_copy, outs

    def return_begin(pair_out):
        @pl.when(owner)
        def _():
            mine_copy, outs = return_copies(pair_out)
            mine_copy.start()
            for copy in outs:
                copy.start()

    def return_end(pair_out):
        for o in (1, 2, 3):
            other = flip(spot.plane, o)

            @pl.when(spot.core == other % 2)
            def _():
                place = pair_out.at[other // 2]
                send(place, place, (out_s, out_r), (o,), spot.at(plane=other)).wait_recv()

        @pl.when(owner)
        def _():
            mine_copy, outs = return_copies(pair_out)
            mine_copy.wait()
            for copy in outs:
                copy.wait_send()

    chunk = -(-rows // 4 // 16) * 16
    chunks = [(start, min(chunk, rows - start)) for start in range(0, rows, chunk)]
    last_plane = spot.planes - 1

    def line_copy(s, j, up, first):
        start, size = chunks[j]
        target = in_pair.at[s, start : start + size]
        source = up_low.at[spot.image, start : start + size] if first else target
        return pltpu.make_async_remote_copy(
            src_ref=source, dst_ref=target, send_sem=line_s.at[s, j, 0 if up else 1], recv_sem=line_r.at[s, j],
            device_id=spot.at(plane=spot.plane + (1 if up else -1)), device_id_type=MESH,
        )

    def line_ways(s, act):
        source = 2 * s + spot.core
        for up, edge in ((True, last_plane), (False, 0)):
            beyond = spot.plane > source if up else spot.plane < source

            @pl.when(jnp.logical_and(spot.plane == source, spot.plane != edge))
            def _():
                act(up, True)

            @pl.when(jnp.logical_and(beyond, spot.plane != edge))
            def _():
                act(up, False)

    def line_kept(s):
        return pltpu.make_async_copy(up_low.at[spot.image], in_pair.at[s], load_sem.at[13])

    def line_begin():
        for s in range(2):
            @pl.when(spot.plane == 2 * s + spot.core)
            def _():
                line_kept(s).start()

            for j in range(len(chunks)):
                def act(up, first):
                    if first:
                        line_copy(s, j, up, True).start()

                line_ways(s, act)

    def line_relay(j):
        for s in range(2):
            @pl.when(spot.plane != 2 * s + spot.core)
            def _():
                line_copy(s, j, True, False).wait_recv()

            def act(up, first):
                if not first:
                    line_copy(s, j, up, False).start()

            line_ways(s, act)

    def line_end():
        for s in range(2):
            @pl.when(spot.plane == 2 * s + spot.core)
            def _():
                line_kept(s).wait()

            for j in range(len(chunks)):
                line_ways(s, lambda up, first: line_copy(s, j, up, first).wait_send())

    def norm_back(l, n, i):
        base = (l + 1) * 6
        for start in range(0, rows, 128):
            r = slice(start, min(rows, start + 128))
            g = full[i, r].astype(f32)
            u = unit[i, r].astype(f32)
            scaled = g * vec[l, n : n + 1]
            first = jnp.mean(scaled, axis=-1, keepdims=True)
            second = jnp.mean(scaled * u, axis=-1, keepdims=True)
            v = up[i, r] + inverse[i, r, 0:1] * (scaled - first - u * second)
            up[i, r] = v
            up_low[i, r] = v.astype(bf16)
            sums[base + n] += eights(g * u)
            sums[base + 2 + n] += eights(g)
            sums[base + 4 if n == 1 else base - 1] += eights(v)

    def mlp_stage(l, i, n):
        @pl.when(l < top)
        def _():
            exchange.finish(i, 1)
            norm_back(jnp.minimum(l + 1, top), 0, i)

        @pl.when(i == 0)
        def _():
            load_hidden(l).wait()
            load_weight(l, 2).wait()

        for k in range(4):
            at = slice(k * 256, k * 256 + 256)
            grad_active = dot(up_low[i], weight[2, k].reshape(256, D), 1, 1)
            v = hid[i, :, at].astype(f32)
            below = 0.5 + 0.5 * lax.erf(v * (0.5**0.5))
            slope = below + v * jnp.exp(-0.5 * v * v) * (1.0 / math.sqrt(2.0 * math.pi))
            hid[i, :, at] = (v * below).astype(bf16)
            low_grad = (grad_active * slope).astype(bf16)
            gh[i, :, at] = low_grad
            unit_sums[l, 0, :, at] += eights(low_grad.astype(f32))

        @pl.when(i == 1)
        def _():
            scatter.before_terms(n)
            unit_term(scatter.slot(n), hid, up_low)
            scatter.send_terms(n)

        @pl.when(i == 0)
        def _():
            load_weight(l, 1).wait()

        exchange.reduce(i, lambda at: dot(gh[i], weight[1, :, :, :, at].reshape(D, HALF), 1, 0), kept)
        exchange.side_copy(i, 0).start()

    lane_pair = lax.broadcasted_iota(jnp.int32, (1, 128), 1) // HD
    valid = lax.broadcasted_iota(jnp.int32, (rows, 1), 0) < tokens
    head_rows = jnp.where(
        lax.broadcasted_iota(jnp.int32, (16, 256), 1) // HD == lax.broadcasted_iota(jnp.int32, (16, 256), 0), 1.0, 0.0
    ).astype(bf16)

    def attn_stage(l, i):
        exchange.finish(i, 0)

        @pl.when(i == 0)
        def _():
            for copy in load_unit(l, 1):
                copy.wait()

        norm_back(l, 1, i)

        @pl.when(i == 0)
        def _():
            load_weight(l, 0).wait()
            for copy in load_attn(l):
                copy.wait()

        gab[...] = dot(up_low[i], weight[0, :, 3].reshape(256, D), 1, 1).astype(bf16)
        product = gab[...].astype(f32) * att[i].astype(f32)
        high = product.astype(bf16)
        rest = (product - high.astype(f32)).astype(bf16)
        along[...] = dot(head_rows, high, 1, 1) + dot(head_rows, rest, 1, 1)

        flipped[0:256] = jnp.transpose(qkv[i, :, 256:512])
        flipped[256:512] = jnp.transpose(qkv[i, :, 0:256])
        flipped[512:768] = jnp.transpose(gab[...])
        def one_head(h, carry):
            two, key_two, value_two = [lanes(m * 256 + h // 2 * 128, 128) for m in range(3)]
            low_mask = jnp.where(lane_pair == h % 2, 1.0, 0.0).astype(bf16)
            q = qkv[i, :, two] * (low_mask * HD ** (-0.5))
            p = jnp.exp(dot(qkv[i, :, key_two], q, 1, 1) - lse[i, pl.ds(h, 1)])
            p = jnp.where(valid, p, 0.0)
            grad_p = dot(qkv[i, :, value_two], gab[:, two] * low_mask, 1, 1)
            ds = (p * (grad_p - along[pl.ds(h, 1)])).astype(bf16)
            at = [pl.ds(pl.multiple_of(m * 256 + h * HD, HD), HD) for m in range(3)]
            grad_rows[at[0]] = (dot(flipped[at[0]], ds, 1, 0) * HD ** (-0.5)).astype(bf16)
            grad_rows[at[1]] = (dot(flipped[at[1]], ds, 1, 1) * HD ** (-0.5)).astype(bf16)
            grad_rows[at[2]] = dot(flipped[at[2]], p.astype(bf16), 1, 1).astype(bf16)
            return carry

        lax.fori_loop(0, 4, one_head, 0)
        for m in range(3):
            gh[i, :, m * 256 : m * 256 + 256] = jnp.transpose(grad_rows[m * 256 : m * 256 + 256])
        for m in (0, 2):
            at = slice(m * 256, m * 256 + 256)
            unit_sums[l, 1, :, at] += eights(gh[i, :, at].astype(f32))


        def partial(at):
            terms = [
                dot(gh[i, :, m * 256 : m * 256 + 256], weight[0, :, m, :, at].reshape(256, HALF), 1, 0)
                for m in range(3)
            ]
            return terms[0] + terms[1] + terms[2]

        exchange.reduce(i, partial, kept)
        exchange.side_copy(i, 1).start()

    span = D // spot.blocks

    def unit_term(a, left, right):
        def one(plane, carry):
            at = lanes(plane * 256, 256)
            for b in range(spot.blocks):
                to = slice(b * span, b * span + span)
                part = dot(left[0, :, at], right[0, :, to], 0, 0) + dot(left[1, :, at], right[1, :, to], 0, 0)
                term[a, plane, :, to] = part.astype(bf16)
            return carry

        lax.fori_loop(0, 4, one, 0)

    def attn_term(a):
        for m in range(4):
            left = gh if m < 3 else att
            right = normed if m < 3 else up_low
            at = slice(m * 256, m * 256 + 256) if m < 3 else slice(0, 256)
            for b in range(spot.blocks):
                to = slice(b * span, b * span + span)
                part = dot(left[0, :, at], right[0, :, to], 0, 0) + dot(left[1, :, at], right[1, :, to], 0, 0)
                term[a, :, m * HD : m * HD + HD, to] = part.astype(bf16).reshape(4, HD, span)

    def one_layer(step_index, carry):
        l = top - step_index
        again = l < top
        more = l > 0
        n = 3 * step_index

        def mlp_image(i, carry):
            mlp_stage(l, i, n)

            @pl.when(jnp.logical_and(again, i == 0))
            def _():
                scatter.sum_blocks(n - 2)
                scatter.hop(n - 3, 1)

            return carry

        lax.fori_loop(0, 2, mlp_image, 0)

        @pl.when(l == top)
        def _():
            last_copy.wait_recv()
            load_stream = load(stream_in.at[spot.image], big.at[:, 0:D], 11)
            load_stream.start()

            v = last_chip[spot.image].astype(f32) + last_in[...].astype(f32)
            result[:, exchange.mine] = v.astype(bf16)
            load_stream.wait()

            @pl.when(jnp.logical_not(owner))
            def _():
                half_copy.start()
                half_copy.wait_send()

            @pl.when(owner)
            def _():
                half_in.wait_recv()

                for start in range(0, rows, 128):
                    r = slice(start, min(rows, start + 128))
                    v = big[r, 0:D] + result[r].astype(f32) + vec[top, 5:6]
                    result[r] = v.astype(bf16)

            last_copy.wait_send()
            for copy in load_attn(top):
                copy.start()
            return_begin(out_pair)

        @pl.when(again)
        def _():
            for copy in load_unit(l, 1):
                copy.start()

        load_normed(l, 1).wait()

        @pl.when(again)
        def _():
            scatter.hop(n - 3, 2)
            scatter.sum_blocks(n - 1)
            scatter.hop(n - 2, 1)

        scatter.before_terms(n + 1)
        unit_term(scatter.slot(n + 1), gh, normed)
        scatter.send_terms(n + 1)

        @pl.when(more)
        def _():
            below = jnp.maximum(l - 1, 0)
            load_hidden(below).start()
            load_weight(below, 1).start()
            load_weight(below, 2).start()

        load_normed(l, 0).start()

        @pl.when(again)
        def _():
            scatter.hop(n - 3, 3)
            scatter.hand_out(n - 3)

        def attn_image(i, carry):
            attn_stage(l, i)

            @pl.when(jnp.logical_and(again, i == 0))
            def _():
                scatter.hop(n - 2, 2)
                scatter.hop(n - 1, 1)

            return carry

        lax.fori_loop(0, 2, attn_image, 0)
        for copy in load_unit(l, 0):
            copy.start()
        load_normed(l, 0).wait()

        @pl.when(again)
        def _():
            scatter.hop(n - 2, 3)
            scatter.hand_out(n - 2)
            scatter.hop(n - 1, 2)

        scatter.sum_blocks(n)
        scatter.before_terms(n + 2)
        attn_term(scatter.slot(n + 2))

        @pl.when(more)
        def _():
            scatter.send_terms(n + 2)

        @pl.when(jnp.logical_not(more))
        def _():
            scatter.send_terms(3 * LAYERS - 1, (0, 1))

        @pl.when(more)
        def _():
            below = jnp.maximum(l - 1, 0)
            load_weight(below, 0).start()
            load_normed(below, 1).start()
            for copy in load_attn(below):
                copy.start()

        for copy in load_unit(l, 0):
            copy.wait()
        return carry

    lax.fori_loop(0, LAYERS, one_layer, 0)

    end = 3 * LAYERS
    def last_image(i, carry):
        exchange.finish(i, 1)
        norm_back(0, 0, i)

        @pl.when(i == spot.image)
        def _():
            line_begin()

        return carry

    lax.fori_loop(0, 2, last_image, 0)
    picks = normed.at[0]
    unit_picks(picks, fsdp, spot.role)
    for l in range(LAYERS):
        features = [jnp.sum(sums[(l + 1) * 6 + n], axis=0, keepdims=True) for n in range(6)]
        inner = jnp.sum(unit_sums[l, 0], axis=0, keepdims=True)
        qkv_sums = jnp.sum(unit_sums[l, 1], axis=0, keepdims=True)
        for plane in range(4):
            parts = [
                inner[:, plane * 256 : plane * 256 + 256],
                qkv_sums[:, plane * HD : plane * HD + HD],
                qkv_sums[:, 512 + plane * HD : 512 + plane * HD + HD],
            ]
            values = jnp.broadcast_to(jnp.concatenate(parts, axis=1), (16, 384)).astype(bf16)
            row = dot(values[:, 0:256], picks[0:256], 1, 0)[0:1]
            other_row = dot(values[:, 256:384], picks[256:384], 1, 0)[0:1]
            block = jnp.concatenate(features + [row, other_row, jnp.zeros((8, D), f32)], axis=0)
            small_term[0, plane, 16 * l : 16 * l + 16] = block.astype(bf16)
    small.send_terms(0)
    scatter.hop(end - 3, 1)
    scatter.hop(end - 4, 3)
    scatter.hand_out(end - 4)
    scatter.sum_blocks(end - 2)
    line_relay(0)
    scatter.hop(end - 3, 2)
    scatter.sum_blocks(end - 1, 0)
    line_relay(1)
    small.sum_blocks(0)
    scatter.hop(end - 2, 1)
    scatter.sum_blocks(end - 1, 1)
    scatter.hop(end - 1, 1, 0)
    line_relay(2)
    small.hop(0, 1)
    scatter.hop(end - 3, 3)
    scatter.hand_out(end - 3)
    scatter.hop(end - 1, 1, 1)
    scatter.hop(end - 2, 2)
    scatter.hop(end - 1, 2, 0)
    line_relay(3)
    small.hop(0, 2)
    scatter.hop(end - 1, 2, 1)
    scatter.hop(end - 2, 3)
    scatter.hand_out(end - 2)
    scatter.hop(end - 1, 3, 0)
    scatter.hand_out(end - 1, 0)
    small.hop(0, 3)
    small.hand_out(0)
    scatter.hop(end - 1, 3, 1)
    scatter.hand_out(end - 1, 1)
    scatter.finish((0, 1))
    small.finish()
    return_end(out_pair)
    line_end()


def backward_call(fsdp, head, tokens, rows, direct, kept):
    groups = 3 * LAYERS
    blocks = fsdp // TP
    span = D // blocks
    cols = span // TP
    anyspace = pl.BlockSpec(memory_space=pl.ANY)
    shape = jax.ShapeDtypeStruct
    dma, plain = pltpu.SemaphoreType.DMA, pltpu.SemaphoreType.REGULAR
    out_shape = (
        shape((2, rows, D), bf16),
        shape((2, rows, D), bf16),
        shape((groups, TP, 256, cols) if direct else (groups, 256, span), bf16),
        shape((1, TP, 32, cols) if direct else (1, 32, span), bf16),
    )
    scratch = [
        pltpu.VMEM((3, 4, 4, HD, D), bf16),
        pltpu.VMEM((LAYERS, 8, D), f32),
        pltpu.VMEM((2, rows, D), f32),
        pltpu.VMEM((2, rows, D), bf16),
        pltpu.VMEM((2, rows, D), bf16),
        pltpu.VMEM((2, rows, D), bf16),
        pltpu.VMEM((2, rows, D), bf16),
        pltpu.VMEM((2, rows, D), bf16),
        pltpu.VMEM((2, rows, 128), f32),
        pltpu.VMEM((2, rows, 768), bf16),
        pltpu.VMEM((2, rows, 256), bf16),
        pltpu.VMEM((2, 8, rows), f32),
        pltpu.VMEM((rows, D), f32),
        pltpu.VMEM((768, rows), bf16),
        pltpu.VMEM((768, rows), bf16),
        pltpu.VMEM((rows, 256), bf16),
        pltpu.VMEM((16, rows), f32),
        pltpu.VMEM((2, rows, HALF), bf16),
        pltpu.VMEM((2, rows, HALF), bf16),
        pltpu.VMEM((2, rows, HALF), bf16),
        pltpu.VMEM((2, 2, rows, HALF), bf16),
        pltpu.VMEM((2, rows, D), bf16),
        pltpu.VMEM((rows, HALF), bf16),
        pltpu.VMEM((rows, D), bf16),
        pltpu.VMEM((6 * (LAYERS + 1), 8, D), f32),
        pltpu.VMEM((LAYERS, 2, 8, D), f32),
    ]
    for slots, thirds, units in ((2, 3, 256), (1, 1, 32)):
        scratch += [
            pltpu.VMEM((slots, 4, units, D), bf16),
            pltpu.VMEM((slots, blocks - 1, 4, units, span), bf16),
            pltpu.VMEM((thirds, 4, units, span), bf16),
            pltpu.VMEM((slots, 2, 3, units, span), bf16),
            pltpu.VMEM((slots, units, span), bf16),
        ]
    scratch += [dma((2,)), dma((2,)), dma((2, 2)), dma((2, 2)), dma((2,)), dma((2,))]
    for slots, thirds, count in ((2, 3, groups), (1, 1, 1)):
        scratch += [
            dma((slots, blocks - 1, 2)), dma((slots, blocks - 1, 2)),
            dma((thirds, 2, 2)), dma((thirds, 2, 2)),
            dma((count, 4, 2)), dma((count, 4, 2)),
            dma((count, 2)),
            plain((slots, blocks - 1)), plain((slots, 2)),
        ]
    scratch += [dma((2,)), dma((2,)), dma((4,)), dma((4,)), dma((2, 4, 2)), dma((2, 4)), dma((16,)), dma((3,))]
    return pl.pallas_call(
        functools.partial(backward_kernel, (fsdp, head, tokens, rows, direct)),
        out_shape=out_shape,
        in_specs=[anyspace] * len(kept),
        out_specs=tuple(anyspace for _ in out_shape),
        scratch_shapes=scratch,
        compiler_params=pltpu.CompilerParams(
            collective_id=1, has_side_effects=True, vmem_limit_bytes=63 << 20
        ),
        name="backward_layers",
    )(*kept)


class Places:
    def __init__(self, fsdp, head):
        self.fsdp, self.head = fsdp, head
        self.blocks = fsdp // TP
        index, plane = lax.axis_index("fsdp"), lax.axis_index("head")
        self.block, self.role, self.plane = index // TP, index % TP, plane

    def pairs(self, move, sends=None):
        found = []
        for block in range(self.blocks):
            for role in range(TP):
                for plane in range(self.head):
                    if sends is not None and not sends(block, role, plane):
                        continue
                    to_block, to_role, to_plane = move(block, role, plane)
                    found.append(
                        (
                            (block * TP + role) * self.head + plane,
                            (to_block * TP + to_role) * self.head + to_plane,
                        )
                    )
        return found

    def role_xor(self, v, bits, sends=None):
        return lax.ppermute(v, AXES, self.pairs(lambda b, r, p: (b, r ^ bits, p), sends))


def by_xor(parts, index):
    a, b, c, d = parts
    odd = (index & 1) == 1
    a, b = jnp.where(odd, b, a), jnp.where(odd, a, b)
    c, d = jnp.where(odd, d, c), jnp.where(odd, c, d)
    top = (index & 2) == 2
    return [jnp.where(top, c, a), jnp.where(top, d, b), jnp.where(top, a, c), jnp.where(top, b, d)]


def pack_inputs(pl, w_qkv, w_out, w_in, w_down, qv_bias, in_bias, gains, shifts):
    cols = w_qkv.shape[2]
    attn = jnp.concatenate([w_qkv.transpose(0, 1, 3, 2), w_out[:, None]], axis=1).reshape(LAYERS, 4, TP, HD, cols)
    inner = w_in.transpose(0, 2, 1).reshape(LAYERS, TP, 4, HD, cols)
    down = w_down.reshape(LAYERS, TP, 4, HD, cols)
    qv = qv_bias.reshape(LAYERS, 1, -1)
    small = jnp.concatenate(
        [
            gains, shifts, in_bias.reshape(LAYERS, 1, cols),
            jnp.pad(qv, ((0, 0), (0, 0), (0, cols - qv.shape[2]))),
            jnp.zeros((LAYERS, 8, cols), bf16),
        ],
        axis=1,
    ).reshape(1, 16 * LAYERS, cols)
    if cols % 128 == 0:
        return attn, inner, down, small, True
    attn = gather_roles(pl, attn.transpose(0, 2, 1, 3, 4).reshape(LAYERS, TP, 256, cols))
    inner, down = [gather_roles(pl, v.reshape(LAYERS, TP, 256, cols)) for v in (inner, down)]
    small = gather_roles(pl, jnp.broadcast_to(small[:, None], (1, TP) + small.shape[1:]))
    attn, inner, down = [v.reshape(LAYERS, 4, HD, TP * cols) for v in (attn, inner, down)]
    return attn, inner, down, small, False


def gather_roles(pl, pack):
    exchanged = [lax.dynamic_index_in_dim(pack, pl.role, 1, False)]
    for bits in (1, 2, 3):
        exchanged.append(pl.role_xor(lax.dynamic_index_in_dim(pack, pl.role ^ bits, 1, False), bits))
    return jnp.concatenate(by_xor(exchanged, pl.role), axis=-1)


def scatter_roles(pl, mine):
    groups, units, width = mine.shape
    mine = mine.reshape(groups, units, TP, width // TP)
    exchanged = [lax.dynamic_index_in_dim(mine, pl.role, 2, False)]
    for bits in (1, 2, 3):
        exchanged.append(pl.role_xor(lax.dynamic_index_in_dim(mine, pl.role ^ bits, 2, False), bits))
    return jnp.stack(by_xor(exchanged, pl.role), axis=1)


def body(images, cotangent, w_qkv, w_out, w_in, w_down, qv_bias, in_bias, gains, shifts):
    fsdp, head = lax.axis_size("fsdp"), lax.axis_size("head")
    places = Places(fsdp, head)
    cols = w_qkv.shape[2]
    per = HD // fsdp
    tokens = images.shape[1]
    rows = -(-tokens // 16) * 16
    attn, inner, down, extras, direct = pack_inputs(
        places, w_qkv, w_out, w_in, w_down, qv_bias, in_bias, gains, shifts
    )
    pad = ((0, 0), (0, rows - tokens), (0, 0))
    kept = forward_call(
        fsdp, head, tokens, rows, direct, jnp.pad(images, pad), jnp.pad(cotangent, pad), attn, inner, down, extras
    )
    block_out, input_grad, grads, small = backward_call(fsdp, head, tokens, rows, direct, kept)
    if not direct:
        grads, small = scatter_roles(places, grads), scatter_roles(places, small)
    grads = grads.astype(f32).reshape(LAYERS, 3, TP, 256, cols)
    attn = grads[:, 0].reshape(LAYERS, TP, 4, HD, cols).transpose(0, 2, 1, 3, 4).reshape(LAYERS, 4, TP * HD, cols)
    small = small.astype(f32).reshape(TP, LAYERS, 16, cols)
    features = small[0, :, 0:6]
    units = jnp.sum(small[:, :, 6:8], axis=0)
    qv = units[:, 1, 0 : 2 * TP * per].reshape(LAYERS, 2, TP * per, 1)
    inner = units[:, 0].reshape(LAYERS, cols, 1)
    return (
        lax.optimization_barrier(block_out[:, :tokens]).astype(f32),
        lax.optimization_barrier(input_grad[:, :tokens]).astype(f32),
        attn[:, :3].transpose(0, 1, 3, 2),
        attn[:, 3],
        grads[:, 1].reshape(LAYERS, TP * 256, cols).transpose(0, 2, 1),
        grads[:, 2].reshape(LAYERS, TP * 256, cols),
        qv,
        inner,
        features[:, 0:2],
        features[:, 2:6],
    )


def solution(mesh):
    placed = (
        P("fsdp", None, None),
        P("fsdp", None, None),
        P(None, None, "fsdp", "head"),
        P(None, "head", "fsdp"),
        P(None, "fsdp", "head"),
        P(None, "head", "fsdp"),
        P(None, None, "head", "fsdp"),
        P(None, "head", "fsdp"),
        P(None, None, "fsdp"),
        P(None, None, "fsdp"),
    )
    return jax.shard_map(
        body, mesh=mesh, in_specs=placed, out_specs=placed, check_vma=False
    )
```

```python
import functools
import math

import jax
import jax.numpy as jnp
from jax import lax
from jax.experimental import pallas as pl
from jax.experimental.pallas import tpu as pltpu
from jax.sharding import PartitionSpec as P

D = 1024
HD = 64
LAYERS = 2
TP = 4
HALF = D // 2
AXES = ("fsdp", "head")
MESH = pl.DeviceIdType.MESH
epsilon = 1e-06
f32, bf16 = jnp.float32, jnp.bfloat16


def dot(left, right, left_dim, right_dim):
    return lax.dot_general(
        left, right, (((left_dim,), (right_dim,)), ((), ())), preferred_element_type=f32
    )


def flip1(n):
    return n + 1 - 2 * (n % 2)


def flip2(n):
    return n + 2 - 4 * ((n // 2) % 2)


def flip(n, bits):
    if bits & 1:
        n = flip1(n)
    if bits & 2:
        n = flip2(n)
    return n


class Spot:
    def __init__(self, fsdp, head):
        self.blocks = fsdp // TP
        self.planes = head
        index = lax.axis_index("fsdp")
        self.index = index
        self.block, self.role, self.plane = index // TP, index % TP, lax.axis_index("head")
        self.core = self.role % 2
        self.image = (self.role // 2 + self.plane) % 2

    def at(self, block=None, role=None, plane=None):
        block = self.block if block is None else block
        role = self.role if role is None else role
        plane = self.plane if plane is None else plane
        return (block * TP + role, plane)

    def partners(self):
        found = [self.at(role=flip(self.role, o)) for o in (1, 2, 3)]
        found += [self.at(plane=flip(self.plane, o)) for o in (1, 2, 3)]
        found += [self.at(block=(self.block + s) % self.blocks) for s in range(1, self.blocks)]
        return found


def greet(partners):
    barrier = pltpu.get_barrier_semaphore()
    for partner in partners:
        pl.semaphore_signal(barrier, inc=1, device_id=partner, device_id_type=MESH)
    pl.semaphore_wait(barrier, len(partners))


def send(source, target, sems, where, device):
    return pltpu.make_async_remote_copy(
        src_ref=source,
        dst_ref=target,
        send_sem=sems[0].at[where],
        recv_sem=sems[1].at[where],
        device_id=device,
        device_id_type=MESH,
    )


def lanes(start, size):
    return pl.ds(pl.multiple_of(start, 128), size)


class Gather:
    def __init__(self, spot, source, whole, role_sems, plane_sems, block_sems, base, local_sem, direct):
        self.spot, self.source, self.whole, self.direct = spot, source, whole, direct
        self.role_sems, self.plane_sems, self.block_sems = role_sems, plane_sems, block_sems
        self.base, self.local_sem = base, local_sem
        self.blocks_first = ()
        self.cols = D // spot.blocks // TP
        self.span = D // spot.blocks

    def piece(self, g, plane, block):
        return self.whole.at[g, plane, :, :, lanes(block * self.span, self.span)]

    def own(self, g):
        spot = self.spot
        if self.direct:
            return pltpu.make_async_copy(
                self.source(g, spot.role),
                self.whole.at[g, spot.plane, :, :, lanes(spot.index * self.cols, self.cols)],
                self.local_sem.at[self.base + g],
            )
        return pltpu.make_async_copy(
            self.source(g, None), self.piece(g, spot.plane, spot.block), self.local_sem.at[self.base + g]
        )

    def to_role(self, g, o):
        spot = self.spot
        other = flip(spot.role, o)
        return send(
            self.source(g, other),
            self.whole.at[g, spot.plane, :, :, lanes(spot.index * self.cols, self.cols)],
            self.role_sems,
            (self.base + g, o),
            spot.at(role=other),
        )

    def from_role(self, g, o):
        spot = self.spot
        other = flip(spot.role, o)
        place = self.whole.at[
            g, spot.plane, :, :, lanes((spot.block * TP + other) * self.cols, self.cols)
        ]
        return send(place, place, self.role_sems, (self.base + g, o), spot.at(role=other))

    def hop(self, g, d, up, taken):
        plane = self.spot.plane
        step = 1 if up else -1
        piece = plane - step * d if taken else plane - step * (d - 1)
        place = self.whole.at[g, piece] if g in self.blocks_first else self.piece(g, piece, self.spot.block)
        other = plane - step if taken else plane + step
        return send(
            place, place, self.plane_sems, (self.base + g, d - 1 + (0 if up else 3)), self.spot.at(plane=other)
        )

    def has(self, d, up):
        return self.spot.plane >= d if up else self.spot.plane + d < self.spot.planes

    def goes(self, d, up):
        plane, last = self.spot.plane, self.spot.planes - 1
        if up:
            return jnp.logical_and(plane >= d, plane < last)
        return jnp.logical_and(plane + d <= last, plane > 0)

    def to_block(self, g, s, d, up, taken=False):
        spot = self.spot
        plane = spot.plane - d if up else spot.plane + d
        shift = spot.blocks - s if taken else s
        block = (spot.block + shift) % spot.blocks
        place = self.piece(g, plane, block if taken else spot.block)
        where = (self.base + g, s, d + (0 if up or d == 0 else 3))
        return send(place, place, self.block_sems, where, spot.at(block=block))

    def begin(self, g):
        self.own(g).start()
        if self.direct:
            for o in (1, 2, 3):
                self.to_role(g, o).start()

    def onward(self, g, d):
        for up in (True, False):
            if d < self.spot.planes - 1:
                @pl.when(self.goes(d, up))
                def _():
                    self.hop(g, d + 1, up, False).start()

    def spread(self, g):
        self.own(g).wait()
        if self.direct:
            for o in (1, 2, 3):
                self.from_role(g, o).wait_recv()
        if g not in self.blocks_first:
            self.onward(g, 0)
        for s in range(1, self.spot.blocks):
            self.to_block(g, s, 0, True).start()

    def lift(self, g):
        for s in range(1, self.spot.blocks):
            self.to_block(g, s, 0, True, True).wait_recv()
        self.onward(g, 0)

    def relay(self, g, d):
        for up in (True, False):
            @pl.when(self.has(d, up))
            def _():
                self.hop(g, d, up, True).wait_recv()
        self.onward(g, d)
        if g in self.blocks_first:
            return
        for up in (True, False):
            @pl.when(self.has(d, up))
            def _():
                for s in range(1, self.spot.blocks):
                    self.to_block(g, s, d, up).start()

    def complete(self, g):
        for s in range(1, self.spot.blocks):
            self.to_block(g, s, 0, True, True).wait_recv()
            for d in (1, 2, 3):
                for up in (True, False):
                    @pl.when(self.has(d, up))
                    def _():
                        self.to_block(g, s, d, up, True).wait_recv()

    def drain(self, g):
        for d in (0, 1, 2, 3):
            if self.direct and d > 0:
                self.to_role(g, d).wait_send()
            for up in (True, False):
                if d < 3:
                    @pl.when(self.goes(d, up))
                    def _():
                        self.hop(g, d + 1, up, False).wait_send()
                if d > 0 and g not in self.blocks_first:
                    @pl.when(self.has(d, up))
                    def _():
                        for s in range(1, self.spot.blocks):
                            self.to_block(g, s, d, up).wait_send()
        for s in range(1, self.spot.blocks):
            self.to_block(g, s, 0, True).wait_send()


class Exchange:
    def __init__(self, spot, sent, core_in, chip, side_in, full, core_sems, side_sems, back_sems):
        self.spot = spot
        self.sent, self.core_in, self.chip, self.side_in, self.full = sent, core_in, chip, side_in, full
        self.core_sems, self.side_sems, self.back_sems = core_sems, side_sems, back_sems
        self.mine = lanes(spot.core * HALF, HALF)
        self.theirs = lanes((1 - spot.core) * HALF, HALF)

    def core_copy(self, i):
        return send(
            self.sent.at[i], self.core_in.at[i], self.core_sems, (i,),
            self.spot.at(role=flip1(self.spot.role)),
        )

    def side_copy(self, i, slot):
        return send(
            self.chip.at[i], self.side_in.at[i, slot], self.side_sems, (i, slot),
            self.spot.at(role=flip2(self.spot.role)),
        )

    def back_copy(self, i):
        place = self.full.at[i, :, self.mine]
        return send(place, place, self.back_sems, (i,), self.spot.at(role=flip1(self.spot.role)))

    def back_in(self, i):
        place = self.full.at[i, :, self.theirs]
        return send(place, place, self.back_sems, (i,), self.spot.at(role=flip1(self.spot.role)))

    def reduce(self, i, product, kept):
        self.sent[i] = product(self.theirs).astype(bf16)
        self.core_copy(i).start()
        kept[...] = product(self.mine)
        copy = self.core_copy(i)
        copy.wait_recv()
        self.chip[i] = (kept[...] + self.core_in[i].astype(f32)).astype(bf16)
        copy.wait_send()

    def finish(self, i, slot):
        copy = self.side_copy(i, slot)
        copy.wait_recv()
        total = self.chip[i].astype(f32) + self.side_in[i, slot].astype(f32)
        self.full[i, :, self.mine] = total.astype(bf16)
        self.back_copy(i).start()
        copy.wait_send()
        self.back_in(i).wait_recv()
        self.back_copy(i).wait_send()


def each_rows(rows, size, step, unroll=1):
    def one(c, carry):
        step(pl.ds(pl.multiple_of(c * size, size), size))
        return carry

    lax.fori_loop(0, rows // size, one, 0, unroll=unroll)


def unit_picks(held, fsdp, role):
    cols = D // fsdp
    per = HD // fsdp
    bits = fsdp.bit_length() - 1
    for first, count, offset in (
        (0, 256, role * (4 * per)), (256, HD, role * per), (256 + HD, HD, TP * per + role * per)
    ):
        unit = lax.broadcasted_iota(jnp.int32, (count, D), 0)
        place = lax.broadcasted_iota(jnp.int32, (count, D), 1)
        wanted = (unit & (fsdp - 1)) * cols + (unit >> bits) + offset
        held[first : first + count] = jnp.where(place == wanted, 1.0, 0.0).astype(bf16)


def forward_kernel(cfg, *refs):
    fsdp, head, tokens, rows, direct = cfg
    (
        images, image_rest, cotangents, cot_rest, attn_source, in_source, down_source, extras,
        weights_out, vec_out, normed_out, unit_out, inverse_out, qkv_out, att_out, lse_out, hidden_out,
        stream_out, chip_out, cot_out,
        whole, extra, vec, pair, cots, stream, normed, unit, inverse, qkv, att_sum, att,
        values, lse_rows, low_hidden, active, kept,
        sent, core_in, chip, side_in, full,
        role_s, role_r, plane_s, plane_r, block_s, block_r, local_sem,
        core_s, core_r, side_s, side_r, back_s, back_r,
        share_s, share_r, store_sem,
    ) = refs
    spot = Spot(fsdp, head)
    groups = 3 * LAYERS
    greet(spot.partners())
    sems = ((role_s, role_r), (plane_s, plane_r), (block_s, block_r))

    def source(g, role):
        l, k = g // 3, g % 3
        held = (attn_source, in_source, down_source)[k]
        if role is None:
            return held.at[l]
        return held.at[l, :, role] if k == 0 else held.at[l, role]

    small = Gather(spot, lambda g, role: extras, extra, *sems, groups, local_sem, direct)
    large = Gather(spot, source, whole, *sems, 0, local_sem, direct)
    large.blocks_first = (groups - 1,)
    whole_rows = tokens // 16 * 16
    slot = spot.plane // 2
    own_image, own_cot = [
        (main.at[slot, 0:whole_rows], rest.at[slot]) for main, rest in ((images, image_rest), (cotangents, cot_rest))
    ]
    exchange = Exchange(
        spot, sent, core_in, chip, side_in, full, (core_s, core_r), (side_s, side_r), (back_s, back_r)
    )
    owner = spot.core == spot.plane % 2
    x, other_x = spot.image, 1 - spot.image

    small.begin(0)
    large.begin(0)

    def share(source, held, n):
        across = send(
            held.at[x], held.at[x], (share_s, share_r), (n, 0), spot.at(role=flip2(spot.role))
        )
        across_in = send(
            held.at[other_x], held.at[other_x], (share_s, share_r), (n, 0), spot.at(role=flip2(spot.role))
        )
        down = [
            send(held.at[at], held.at[at], (share_s, share_r), (n, 1 + k), spot.at(role=flip1(spot.role)))
            for k, at in enumerate((x, other_x))
        ]
        mine = [
            pltpu.make_async_copy(source[0], held.at[x, 0:whole_rows], store_sem.at[30 + n]),
            pltpu.make_async_copy(source[1], held.at[x, whole_rows:rows], store_sem.at[32 + n]),
        ]
        return across, across_in, down, mine

    def share_begin(source, held, n):
        across, across_in, down, mine = share(source, held, n)

        @pl.when(owner)
        def _():
            for copy in mine:
                copy.start()
            for copy in mine:
                copy.wait()
            across.start()
            down[0].start()

    def share_end(source, held, n):
        across, across_in, down, mine = share(source, held, n)

        @pl.when(owner)
        def _():
            across_in.wait_recv()
            down[1].start()
            across.wait_send()
            down[0].wait_send()
            down[1].wait_send()

        @pl.when(jnp.logical_not(owner))
        def _():
            down[0].wait_recv()
            down[1].wait_recv()

    large.spread(0)
    small.spread(0)
    large.begin(1)
    share_begin(own_image, pair, 0)
    for g in (2, 5, 3, 4):
        large.begin(g)
    small.relay(0, 1)
    large.relay(0, 1)
    large.spread(1)
    small.relay(0, 2)
    large.relay(0, 2)
    small.relay(0, 3)
    large.relay(0, 3)
    large.relay(1, 1)
    large.spread(2)
    large.spread(5)
    share_end(own_image, pair, 0)
    share_begin(own_cot, cots, 1)
    small.complete(0)

    unit_picks(active, fsdp, spot.role)
    for l in range(LAYERS):
        vec[l, 0:6] = extra[0, 0, 0, 16 * l : 16 * l + 16].astype(f32)[0:6]
        for plane in range(4):
            units = dot(extra[0, plane, 0, 16 * l : 16 * l + 16], active[0:384], 1, 1)
            vec[l, 6:7, plane * 256 : plane * 256 + 256] = units[6:7, 0:256]
            if plane % 2 == 0:
                before = units
            else:
                for k in range(2):
                    at = slice(256 + k * HD, 256 + k * HD + HD)
                    to = k * 256 + (plane - 1) * HD
                    vec[l, 7:8, to : to + 128] = jnp.concatenate([before[7:8, at], units[7:8, at]], axis=1)
    store_vec = pltpu.make_async_copy(vec, vec_out, store_sem.at[28])
    store_vec.start()
    large.complete(0)

    lane_pair = lax.broadcasted_iota(jnp.int32, (1, 128), 1) // HD
    valid = lax.broadcasted_iota(jnp.int32, (rows, 1), 0) < tokens

    def stores(l, n, i):
        return [
            pltpu.make_async_copy(normed.at[i], normed_out.at[l, n, i], store_sem.at[0 + i]),
            pltpu.make_async_copy(unit.at[i], unit_out.at[l, n, i], store_sem.at[2 + i]),
            pltpu.make_async_copy(inverse.at[i], inverse_out.at[l, n, i], store_sem.at[4 + i]),
        ]

    def norm(l, n, i, v):
        stream[i] = v
        average = jnp.mean(v, axis=-1, keepdims=True)
        centred = v - average
        scale = lax.rsqrt(jnp.mean(centred * centred, axis=-1, keepdims=True) + epsilon)
        u = centred * scale
        unit[i] = u.astype(bf16)
        inverse[i] = jnp.broadcast_to(scale, (rows, 128))
        normed[i] = (u * vec[l, n : n + 1] + vec[l, 2 + n : 3 + n]).astype(bf16)
        for copy in stores(l, n, i):
            copy.start()

    def attn_stage(l, i):
        g = 3 * l

        @pl.when(l > 0)
        def _():
            exchange.finish(i, 1)
            for copy in stores(l - 1, 1, i):
                copy.wait()
            before = jnp.maximum(l - 1, 0)
            norm(l, 0, i, stream[i] + full[i].astype(f32) + vec[before, 5:6])

        @pl.when(l == 0)
        def _():
            norm(l, 0, i, pair[i].astype(f32))

        store_qkv = pltpu.make_async_copy(qkv, qkv_out.at[l, i], store_sem.at[6])
        store_att = pltpu.make_async_copy(att.at[i], att_out.at[l, i], store_sem.at[8 + i])
        store_lse = pltpu.make_async_copy(lse_rows.at[i], lse_out.at[l, i], store_sem.at[10 + i])

        @pl.when(l + i > 0)
        def _():
            store_qkv.wait()

        @pl.when(l > 0)
        def _():
            store_att.wait()
            store_lse.wait()

        for k in range(3):
            w = whole[g, :, k].reshape(256, D)
            part = dot(normed[i], w, 1, 1)
            if k == 0:
                part = part + vec[l, 7:8, 0:256]
            if k == 2:
                part = part + vec[l, 7:8, 256:512]
                values[...] = jnp.transpose(part).astype(bf16)
            qkv[:, k * 256 : k * 256 + 256] = part.astype(bf16)
        store_qkv.start()
        def one_head(h, carry):
            two = lanes(h // 2 * 128, 128)
            key_two = lanes(256 + h // 2 * 128, 128)
            low_mask = jnp.where(lane_pair == h % 2, HD ** (-0.5), 0.0).astype(bf16)
            s = dot(qkv[:, key_two], qkv[:, two] * low_mask, 1, 1)
            s = jnp.where(valid, s, -1e30)
            largest = jnp.max(s, axis=0, keepdims=True)
            e = jnp.exp(s - largest)
            total = jnp.sum(e, axis=0, keepdims=True)
            lse_rows[i, pl.ds(h, 1)] = largest + jnp.log(total)
            at = pl.ds(pl.multiple_of(h * HD, HD), HD)
            att_sum[at] = dot(values[at], e.astype(bf16), 1, 0) * (1.0 / total)
            return carry

        lax.fori_loop(0, 4, one_head, 0)
        att[i] = jnp.transpose(att_sum[...]).astype(bf16)
        store_att.start()
        store_lse.start()

        @pl.when(jnp.logical_and(l == 0, i == 0))
        def _():
            large.relay(1, 2)

        @pl.when(jnp.logical_and(l == 0, i == 1))
        def _():
            large.relay(1, 3)
            large.relay(2, 2)

        exchange.reduce(
            i, lambda at: dot(att[i], whole[g, :, 3, :, at].reshape(256, HALF), 1, 0), kept
        )
        exchange.side_copy(i, 0).start()

    def mlp_stage(l, i):
        g = 3 * l
        exchange.finish(i, 0)
        for copy in stores(l, 0, i):
            copy.wait()
        norm(l, 1, i, stream[i] + full[i].astype(f32) + vec[l, 4:5])
        store_hidden = pltpu.make_async_copy(low_hidden.at[i], hidden_out.at[l, i], store_sem.at[12 + i])

        @pl.when(l > 0)
        def _():
            store_hidden.wait()

        for k in range(4):
            at = slice(k * 256, k * 256 + 256)
            v = dot(normed[i], whole[g + 1, k].reshape(256, D), 1, 1) + vec[l, 6:7, at]
            low_hidden[i, :, at] = v.astype(bf16)
            active[:, at] = (v * (0.5 + 0.5 * lax.erf(v * (0.5**0.5)))).astype(bf16)
        store_hidden.start()

        @pl.when(jnp.logical_and(l == 0, i == 0))
        def _():
            large.relay(3, 2)

        @pl.when(jnp.logical_and(l == 0, i == 1))
        def _():
            large.relay(5, 1)
            large.relay(4, 2)

        @pl.when(jnp.logical_and(i == 0, l < LAYERS - 1))
        def _():
            large.complete(g + 2)


        exchange.reduce(i, lambda at: dot(active[...], whole[g + 2, :, :, :, at].reshape(D, HALF), 1, 0), kept)

        @pl.when(l < LAYERS - 1)
        def _():
            exchange.side_copy(i, 1).start()

        @pl.when(l == LAYERS - 1)
        def _():
            pltpu.make_async_copy(chip.at[i], chip_out.at[i], store_sem.at[14 + i]).start()
            pltpu.make_async_copy(stream.at[i], stream_out.at[i], store_sem.at[16 + i]).start()

    def store_weights(g):
        return pltpu.make_async_copy(whole.at[g], weights_out.at[g], store_sem.at[18 + g])

    def one_layer(l, carry):
        g = 3 * l

        @pl.when(l > 0)
        def _():
            large.complete(g)

        def attn_image(i, carry):
            attn_stage(l, i)

            @pl.when(jnp.logical_and(l == 0, i == 0))
            def _():
                large.relay(2, 1)
                large.spread(3)

            @pl.when(jnp.logical_and(l > 0, i == 0))
            def _():
                large.relay(5, 3)

            return carry

        lax.fori_loop(0, 2, attn_image, 0)

        @pl.when(l == 0)
        def _():
            large.relay(3, 1)
            large.spread(4)
            large.relay(2, 3)
            large.lift(5)

        large.complete(g + 1)

        def mlp_image(i, carry):
            mlp_stage(l, i)

            @pl.when(jnp.logical_and(l == 0, i == 0))
            def _():
                large.relay(4, 1)
                large.relay(3, 3)

            return carry

        lax.fori_loop(0, 2, mlp_image, 0)

        @pl.when(l == 0)
        def _():
            large.relay(4, 3)
            large.relay(5, 2)

        for k in range(3):
            store_weights(g + k).start()
        return carry

    lax.fori_loop(0, LAYERS, one_layer, 0)
    share_end(own_cot, cots, 1)
    store_cots = pltpu.make_async_copy(cots, cot_out, store_sem.at[29])
    store_cots.start()
    last = LAYERS - 1
    for i in range(2):
        for copy in stores(last, 1, i):
            copy.wait()
        pltpu.make_async_copy(att.at[i], att_out.at[last, i], store_sem.at[8 + i]).wait()
        pltpu.make_async_copy(lse_rows.at[i], lse_out.at[last, i], store_sem.at[10 + i]).wait()
        pltpu.make_async_copy(low_hidden.at[i], hidden_out.at[last, i], store_sem.at[12 + i]).wait()
        pltpu.make_async_copy(chip.at[i], chip_out.at[i], store_sem.at[14 + i]).wait()
        pltpu.make_async_copy(stream.at[i], stream_out.at[i], store_sem.at[16 + i]).wait()
    pltpu.make_async_copy(qkv, qkv_out.at[last, 1], store_sem.at[6]).wait()
    store_vec.wait()
    store_cots.wait()

    for g in range(groups):
        store_weights(g).wait()
        large.drain(g)
    small.drain(0)


def forward_call(fsdp, head, tokens, rows, direct, *operands):
    groups = 3 * LAYERS
    blocks = fsdp // TP
    anyspace = pl.BlockSpec(memory_space=pl.ANY)
    shape = jax.ShapeDtypeStruct
    dma = pltpu.SemaphoreType.DMA
    out_shape = (
        shape((groups, 4, 4, HD, D), bf16),
        shape((LAYERS, 8, D), f32),
        shape((LAYERS, 2, 2, rows, D), bf16),
        shape((LAYERS, 2, 2, rows, D), bf16),
        shape((LAYERS, 2, 2, rows, 128), f32),
        shape((LAYERS, 2, rows, 768), bf16),
        shape((LAYERS, 2, rows, 256), bf16),
        shape((LAYERS, 2, 8, rows), f32),
        shape((LAYERS, 2, rows, D), bf16),
        shape((2, rows, D), f32),
        shape((2, rows, HALF), bf16),
        shape((2, rows, D), bf16),
    )
    scratch = [
        pltpu.VMEM((groups, 4, 4, HD, D), bf16),
        pltpu.VMEM((1, 4, 1, 32, D), bf16),
        pltpu.VMEM((LAYERS, 8, D), f32),
        pltpu.VMEM((2, rows, D), bf16),
        pltpu.VMEM((2, rows, D), bf16),
        pltpu.VMEM((2, rows, D), f32),
        pltpu.VMEM((2, rows, D), bf16),
        pltpu.VMEM((2, rows, D), bf16),
        pltpu.VMEM((2, rows, 128), f32),
        pltpu.VMEM((rows, 768), bf16),
        pltpu.VMEM((256, rows), f32),
        pltpu.VMEM((2, rows, 256), bf16),
        pltpu.VMEM((256, rows), bf16),
        pltpu.VMEM((2, 8, rows), f32),
        pltpu.VMEM((2, rows, D), bf16),
        pltpu.VMEM((rows, D), bf16),
        pltpu.VMEM((rows, HALF), f32),
        pltpu.VMEM((2, rows, HALF), bf16),
        pltpu.VMEM((2, rows, HALF), bf16),
        pltpu.VMEM((2, rows, HALF), bf16),
        pltpu.VMEM((2, 2, rows, HALF), bf16),
        pltpu.VMEM((2, rows, D), bf16),
        dma((groups + 1, 4)), dma((groups + 1, 4)),
        dma((groups + 1, 6)), dma((groups + 1, 6)),
        dma((groups + 1, blocks, 7)), dma((groups + 1, blocks, 7)),
        dma((groups + 1,)),
        dma((2,)), dma((2,)),
        dma((2, 2)), dma((2, 2)),
        dma((2,)), dma((2,)),
        dma((2, 3)), dma((2, 3)),
        dma((34,)),
    ]
    return pl.pallas_call(
        functools.partial(forward_kernel, (fsdp, head, tokens, rows, direct)),
        out_shape=out_shape,
        in_specs=[anyspace] * len(operands),
        out_specs=tuple(anyspace for _ in out_shape),
        scratch_shapes=scratch,
        compiler_params=pltpu.CompilerParams(
            collective_id=0, has_side_effects=True, vmem_limit_bytes=60 << 20
        ),
        name="forward_layers",
    )(*operands)


class Scatter:
    def __init__(self, spot, count, term, block_in, total, plane_in, mine, out, block_sems, plane_sems, role_sems, local_sem, block_free, plane_free, direct):
        self.spot, self.count, self.direct = spot, count, direct
        self.term, self.block_in, self.total = term, block_in, total
        self.plane_in, self.mine, self.out = plane_in, mine, out
        self.block_sems, self.plane_sems, self.role_sems, self.local_sem = block_sems, plane_sems, role_sems, local_sem
        self.block_free, self.plane_free = block_free, plane_free
        self.span = D // spot.blocks
        self.cols = self.span // TP
        self.own = lanes(spot.block * self.span, self.span)

    def slot(self, n):
        return n % self.term.shape[0]

    def third(self, n):
        return n % self.total.shape[0]

    def rows(self, part):
        units = self.term.shape[2]
        return slice(0, units) if part is None else slice(part * units // 2, (part + 1) * units // 2)

    def to_block(self, n, s, part=None):
        block = (self.spot.block + s) % self.spot.blocks
        a, r = self.slot(n), self.rows(part)
        return send(
            self.term.at[a, :, r, lanes(block * self.span, self.span)],
            self.block_in.at[a, s - 1, :, r],
            self.block_sems, (a, s - 1, part or 0), self.spot.at(block=block),
        )

    def along(self, n, plane, up, part=None):
        planes = self.spot.planes
        a, c = self.slot(n), self.third(n)
        first, number = (plane + 1, planes - 1 - plane) if up else (0, plane)
        way, r = 0 if up else 1, self.rows(part)
        return send(
            self.total.at[c, first : first + number, r], self.plane_in.at[a, way, 0:number, r],
            self.plane_sems, (c, way, part or 0), self.spot.at(plane=plane + (1 if up else -1)),
        )

    def to_role(self, n, o, part=None):
        other = flip(self.spot.role, o)
        g, r = self.count - 1 - n, self.rows(part)
        return send(
            self.mine.at[self.slot(n), r, lanes(other * self.cols, self.cols)],
            self.out.at[g, self.spot.role, r],
            self.role_sems, (g, o, part or 0), self.spot.at(role=other),
        )

    def from_role(self, g, o, part=None):
        other = flip(self.spot.role, o)
        place = self.out.at[g, other, self.rows(part)]
        return send(place, place, self.role_sems, (g, o, part or 0), self.spot.at(role=other))

    def keep(self, n, part=None):
        g, r = self.count - 1 - n, self.rows(part)
        if self.direct:
            return pltpu.make_async_copy(
                self.mine.at[self.slot(n), r, lanes(self.spot.role * self.cols, self.cols)],
                self.out.at[g, self.spot.role, r], self.local_sem.at[g, part or 0],
            )
        return pltpu.make_async_copy(
            self.mine.at[self.slot(n), r], self.out.at[g, r], self.local_sem.at[g, part or 0]
        )

    def before_terms(self, n):
        @pl.when(n >= 2)
        def _():
            for s in range(1, self.spot.blocks):
                self.to_block(n - 2, s).wait_send()

    def send_terms(self, n, parts=(None,)):
        for s in range(1, self.spot.blocks):
            @pl.when(n >= 2)
            def _():
                pl.semaphore_wait(self.block_free.at[self.slot(n), s - 1], 1)

            for part in parts:
                self.to_block(n, s, part).start()

    def pass_on(self, n, plane, up, part=None):
        if not part:
            @pl.when(n >= 2)
            def _():
                pl.semaphore_wait(self.plane_free.at[self.slot(n), 0 if up else 1], 1)

        self.along(n, plane, up, part).start()

    def sent_along(self, n, part=None):
        for plane in range(self.spot.planes):
            @pl.when(self.spot.plane == plane)
            def _():
                if plane < self.spot.planes - 1:
                    self.along(n, plane, True, part).wait_send()
                if plane > 0:
                    self.along(n, plane, False, part).wait_send()

    def sum_blocks(self, n, part=None):
        a, c, r = self.slot(n), self.third(n), self.rows(part)
        for s in range(1, self.spot.blocks):
            self.to_block(n, s, part).wait_recv()

        if not part:
            @pl.when(n >= 3)
            def _():
                self.sent_along(n - 3)

        for plane in range(self.spot.planes):
            value = self.term[a, plane, r, self.own].astype(f32)
            for s in range(1, self.spot.blocks):
                value = value + self.block_in[a, s - 1, plane, r].astype(f32)
            self.total[c, plane, r] = value.astype(bf16)

        @pl.when(n + 2 < self.count)
        def _():
            for s in range(1, self.spot.blocks):
                source = (self.spot.block + self.spot.blocks - s) % self.spot.blocks
                pl.semaphore_signal(
                    self.block_free.at[a, s - 1], inc=1, device_id=self.spot.at(block=source), device_id_type=MESH
                )

        last = self.spot.planes - 1

        @pl.when(self.spot.plane == 0)
        def _():
            self.pass_on(n, 0, True, part)

        @pl.when(self.spot.plane == last)
        def _():
            self.pass_on(n, last, False, part)

    def take(self, n, plane, up, part):
        a, c, r = self.slot(n), self.third(n), self.rows(part)
        before = plane - 1 if up else plane + 1
        self.along(n, before, up, part).wait_recv()
        planes = range(plane, self.spot.planes) if up else range(0, plane + 1)
        for at, p in enumerate(planes):
            value = self.total[c, p, r].astype(f32) + self.plane_in[a, 0 if up else 1, at, r].astype(f32)
            self.total[c, p, r] = value.astype(bf16)

        @pl.when(n + 2 < self.count)
        def _():
            pl.semaphore_signal(
                self.plane_free.at[a, 0 if up else 1], inc=1, device_id=self.spot.at(plane=before), device_id_type=MESH
            )

        if (up and plane < self.spot.planes - 1) or (not up and plane > 0):
            self.pass_on(n, plane, up, part)

    def hop(self, n, d, part=None):
        for plane, up in ((d, True), (self.spot.planes - 1 - d, False)):
            @pl.when(self.spot.plane == plane)
            def _():
                self.take(n, plane, up, part)

    def hand_out(self, n, part=None):
        a, r = self.slot(n), self.rows(part)

        if not part:
            @pl.when(n >= 2)
            def _():
                self.keep(n - 2).wait()
                if self.direct:
                    for o in (1, 2, 3):
                        self.to_role(n - 2, o).wait_send()

        self.mine[a, r] = self.total[self.third(n), self.spot.plane, r]
        self.keep(n, part).start()
        if self.direct:
            for o in (1, 2, 3):
                self.to_role(n, o, part).start()

    def finish(self, parts=(None,)):
        last = self.count - 1
        for n in range(max(0, last - 2), last + 1):
            for part in parts if n == last else (None,):
                self.sent_along(n, part)
        for n in range(max(0, last - 1), last + 1):
            for part in parts if n == last else (None,):
                self.keep(n, part).wait()
                for s in range(1, self.spot.blocks):
                    self.to_block(n, s, part).wait_send()
                if self.direct:
                    for o in (1, 2, 3):
                        self.to_role(n, o, part).wait_send()
        if self.direct:
            for g in range(self.count):
                for o in (1, 2, 3):
                    for part in parts if g == 0 else (None,):
                        self.from_role(g, o, part).wait_recv()


def backward_kernel(cfg, *refs):
    fsdp, head, tokens, rows, direct = cfg
    (
        weights_in, vec_in, normed_in, unit_in, inverse_in, qkv_in, att_in, lse_in, hidden_in,
        stream_in, chip_in, cot_in,
        out_pair, in_pair, grads, small_grads,
        weight, vec, up, up_low, hid, gh, normed, unit, inverse, qkv, att, lse, big, grad_rows, flipped, gab, along,
        sent, core_in, chip, side_in, full, last_in, result, sums, unit_sums,
        term, block_in, total, plane_in, mine,
        small_term, small_block_in, small_total, small_plane_in, small_mine,
        core_s, core_r, side_s, side_r, back_s, back_r,
        block_s, block_r, plane_s, plane_r, role_s, role_r, local_sem, block_free, plane_free,
        small_block_s, small_block_r, small_plane_s, small_plane_r, small_role_s, small_role_r, small_local,
        small_block_free, small_plane_free,
        last_s, last_r, out_s, out_r, line_s, line_r, load_sem, weight_sem,
    ) = refs
    kept = big.at[:, 0:HALF]
    spot = Spot(fsdp, head)
    greet(spot.partners())
    exchange = Exchange(
        spot, sent, core_in, chip, side_in, full, (core_s, core_r), (side_s, side_r), (back_s, back_r)
    )
    scatter = Scatter(
        spot, 3 * LAYERS, term, block_in, total, plane_in, mine, grads, (block_s, block_r), (plane_s, plane_r),
        (role_s, role_r), local_sem, block_free, plane_free, direct,
    )
    small = Scatter(
        spot, 1, small_term, small_block_in, small_total, small_plane_in, small_mine, small_grads,
        (small_block_s, small_block_r), (small_plane_s, small_plane_r), (small_role_s, small_role_r),
        small_local, small_block_free, small_plane_free, direct,
    )
    owner = spot.core == spot.plane % 2
    top = LAYERS - 1

    def load(source, target, n):
        return pltpu.make_async_copy(source, target, load_sem.at[n])

    def load_weight(l, k):
        return pltpu.make_async_copy(weights_in.at[3 * l + k], weight.at[k], weight_sem.at[k])

    load_vec = load(vec_in, vec, 0)
    load_cot = load(cot_in, up_low, 1)
    last_chip = qkv.at[:, :, 0:HALF]
    load_chip = load(chip_in, last_chip, 2)

    def load_hidden(l):
        return load(hidden_in.at[l], hid, 4)

    def load_normed(l, n):
        return load(normed_in.at[l, n], normed, 5)

    def load_unit(l, n):
        return [load(unit_in.at[l, n], unit, 6), load(inverse_in.at[l, n], inverse, 7)]

    def load_attn(l):
        return [load(qkv_in.at[l], qkv, 8), load(att_in.at[l], att, 9), load(lse_in.at[l], lse, 10)]

    load_chip.start()
    load_cot.start()
    load_weight(top, 2).start()
    load_hidden(top).start()
    load_vec.start()
    load_weight(top, 1).start()
    load_weight(top, 0).start()
    load_normed(top, 1).start()
    for copy in load_unit(top, 1):
        copy.start()

    last_copy = send(
        last_chip.at[1 - spot.image], last_in, (last_s, last_r), (0,), spot.at(role=flip2(spot.role))
    )
    half_copy = send(
        result.at[:, exchange.mine], result.at[:, exchange.mine], (last_s, last_r), (1,),
        spot.at(role=flip1(spot.role)),
    )
    half_in = send(
        result.at[:, exchange.theirs], result.at[:, exchange.theirs], (last_s, last_r), (1,),
        spot.at(role=flip1(spot.role)),
    )
    load_chip.wait()
    last_copy.start()

    sums[...] = jnp.zeros_like(sums)
    unit_sums[...] = jnp.zeros_like(unit_sums)
    load_cot.wait()

    def eights(v):
        return jnp.sum(v.reshape(v.shape[0] // 8, 8, v.shape[1]), axis=0)

    for i in range(2):
        for start in range(0, rows, 128):
            r = slice(start, min(rows, start + 128))
            v = up_low[i, r].astype(f32)
            up[i, r] = v
            sums[(top + 1) * 6 + 5] += eights(v)
    load_vec.wait()

    def return_copies(pair_out):
        slot = spot.plane // 2
        mine_copy = pltpu.make_async_copy(result, pair_out.at[slot], load_sem.at[12])
        outs = [
            send(result, pair_out.at[slot], (out_s, out_r), (o,), spot.at(plane=flip(spot.plane, o)))
            for o in (1, 2, 3)
        ]
        return mine_copy, outs

    def return_begin(pair_out):
        @pl.when(owner)
        def _():
            mine_copy, outs = return_copies(pair_out)
            mine_copy.start()
            for copy in outs:
                copy.start()

    def return_end(pair_out):
        for o in (1, 2, 3):
            other = flip(spot.plane, o)

            @pl.when(spot.core == other % 2)
            def _():
                place = pair_out.at[other // 2]
                send(place, place, (out_s, out_r), (o,), spot.at(plane=other)).wait_recv()

        @pl.when(owner)
        def _():
            mine_copy, outs = return_copies(pair_out)
            mine_copy.wait()
            for copy in outs:
                copy.wait_send()

    chunk = -(-rows // 4 // 16) * 16
    chunks = [(start, min(chunk, rows - start)) for start in range(0, rows, chunk)]
    last_plane = spot.planes - 1

    def line_copy(s, j, up, first):
        start, size = chunks[j]
        target = in_pair.at[s, start : start + size]
        source = up_low.at[spot.image, start : start + size] if first else target
        return pltpu.make_async_remote_copy(
            src_ref=source, dst_ref=target, send_sem=line_s.at[s, j, 0 if up else 1], recv_sem=line_r.at[s, j],
            device_id=spot.at(plane=spot.plane + (1 if up else -1)), device_id_type=MESH,
        )

    def line_ways(s, act):
        source = 2 * s + spot.core
        for up, edge in ((True, last_plane), (False, 0)):
            beyond = spot.plane > source if up else spot.plane < source

            @pl.when(jnp.logical_and(spot.plane == source, spot.plane != edge))
            def _():
                act(up, True)

            @pl.when(jnp.logical_and(beyond, spot.plane != edge))
            def _():
                act(up, False)

    def line_kept(s):
        return pltpu.make_async_copy(up_low.at[spot.image], in_pair.at[s], load_sem.at[13])

    def line_begin():
        for s in range(2):
            @pl.when(spot.plane == 2 * s + spot.core)
            def _():
                line_kept(s).start()

            for j in range(len(chunks)):
                def act(up, first):
                    if first:
                        line_copy(s, j, up, True).start()

                line_ways(s, act)

    def line_relay(j):
        for s in range(2):
            @pl.when(spot.plane != 2 * s + spot.core)
            def _():
                line_copy(s, j, True, False).wait_recv()

            def act(up, first):
                if not first:
                    line_copy(s, j, up, False).start()

            line_ways(s, act)

    def line_end():
        for s in range(2):
            @pl.when(spot.plane == 2 * s + spot.core)
            def _():
                line_kept(s).wait()

            for j in range(len(chunks)):
                line_ways(s, lambda up, first: line_copy(s, j, up, first).wait_send())

    def norm_back(l, n, i):
        base = (l + 1) * 6
        for start in range(0, rows, 128):
            r = slice(start, min(rows, start + 128))
            g = full[i, r].astype(f32)
            u = unit[i, r].astype(f32)
            scaled = g * vec[l, n : n + 1]
            first = jnp.mean(scaled, axis=-1, keepdims=True)
            second = jnp.mean(scaled * u, axis=-1, keepdims=True)
            v = up[i, r] + inverse[i, r, 0:1] * (scaled - first - u * second)
            up[i, r] = v
            up_low[i, r] = v.astype(bf16)
            sums[base + n] += eights(g * u)
            sums[base + 2 + n] += eights(g)
            sums[base + 4 if n == 1 else base - 1] += eights(v)

    def mlp_stage(l, i, n):
        @pl.when(l < top)
        def _():
            exchange.finish(i, 1)
            norm_back(jnp.minimum(l + 1, top), 0, i)

        @pl.when(i == 0)
        def _():
            load_hidden(l).wait()
            load_weight(l, 2).wait()

        for k in range(4):
            at = slice(k * 256, k * 256 + 256)
            grad_active = dot(up_low[i], weight[2, k].reshape(256, D), 1, 1)
            v = hid[i, :, at].astype(f32)
            below = 0.5 + 0.5 * lax.erf(v * (0.5**0.5))
            slope = below + v * jnp.exp(-0.5 * v * v) * (1.0 / math.sqrt(2.0 * math.pi))
            hid[i, :, at] = (v * below).astype(bf16)
            low_grad = (grad_active * slope).astype(bf16)
            gh[i, :, at] = low_grad
            unit_sums[l, 0, :, at] += eights(low_grad.astype(f32))

        @pl.when(i == 1)
        def _():
            scatter.before_terms(n)
            unit_term(scatter.slot(n), hid, up_low)
            scatter.send_terms(n)

        @pl.when(i == 0)
        def _():
            load_weight(l, 1).wait()

        exchange.reduce(i, lambda at: dot(gh[i], weight[1, :, :, :, at].reshape(D, HALF), 1, 0), kept)
        exchange.side_copy(i, 0).start()

    lane_pair = lax.broadcasted_iota(jnp.int32, (1, 128), 1) // HD
    valid = lax.broadcasted_iota(jnp.int32, (rows, 1), 0) < tokens
    head_rows = jnp.where(
        lax.broadcasted_iota(jnp.int32, (16, 256), 1) // HD == lax.broadcasted_iota(jnp.int32, (16, 256), 0), 1.0, 0.0
    ).astype(bf16)

    def attn_stage(l, i):
        exchange.finish(i, 0)

        @pl.when(i == 0)
        def _():
            for copy in load_unit(l, 1):
                copy.wait()

        norm_back(l, 1, i)

        @pl.when(i == 0)
        def _():
            load_weight(l, 0).wait()
            for copy in load_attn(l):
                copy.wait()

        gab[...] = dot(up_low[i], weight[0, :, 3].reshape(256, D), 1, 1).astype(bf16)
        product = gab[...].astype(f32) * att[i].astype(f32)
        high = product.astype(bf16)
        rest = (product - high.astype(f32)).astype(bf16)
        along[...] = dot(head_rows, high, 1, 1) + dot(head_rows, rest, 1, 1)

        flipped[0:256] = jnp.transpose(qkv[i, :, 256:512])
        flipped[256:512] = jnp.transpose(qkv[i, :, 0:256])
        flipped[512:768] = jnp.transpose(gab[...])
        def one_head(h, carry):
            two, key_two, value_two = [lanes(m * 256 + h // 2 * 128, 128) for m in range(3)]
            low_mask = jnp.where(lane_pair == h % 2, 1.0, 0.0).astype(bf16)
            q = qkv[i, :, two] * (low_mask * HD ** (-0.5))
            p = jnp.exp(dot(qkv[i, :, key_two], q, 1, 1) - lse[i, pl.ds(h, 1)])
            p = jnp.where(valid, p, 0.0)
            grad_p = dot(qkv[i, :, value_two], gab[:, two] * low_mask, 1, 1)
            ds = (p * (grad_p - along[pl.ds(h, 1)])).astype(bf16)
            at = [pl.ds(pl.multiple_of(m * 256 + h * HD, HD), HD) for m in range(3)]
            grad_rows[at[0]] = (dot(flipped[at[0]], ds, 1, 0) * HD ** (-0.5)).astype(bf16)
            grad_rows[at[1]] = (dot(flipped[at[1]], ds, 1, 1) * HD ** (-0.5)).astype(bf16)
            grad_rows[at[2]] = dot(flipped[at[2]], p.astype(bf16), 1, 1).astype(bf16)
            return carry

        lax.fori_loop(0, 4, one_head, 0)
        for m in range(3):
            gh[i, :, m * 256 : m * 256 + 256] = jnp.transpose(grad_rows[m * 256 : m * 256 + 256])
        for m in (0, 2):
            at = slice(m * 256, m * 256 + 256)
            unit_sums[l, 1, :, at] += eights(gh[i, :, at].astype(f32))


        def partial(at):
            terms = [
                dot(gh[i, :, m * 256 : m * 256 + 256], weight[0, :, m, :, at].reshape(256, HALF), 1, 0)
                for m in range(3)
            ]
            return terms[0] + terms[1] + terms[2]

        exchange.reduce(i, partial, kept)
        exchange.side_copy(i, 1).start()

    span = D // spot.blocks

    def unit_term(a, left, right):
        def one(plane, carry):
            at = lanes(plane * 256, 256)
            for b in range(spot.blocks):
                to = slice(b * span, b * span + span)
                part = dot(left[0, :, at], right[0, :, to], 0, 0) + dot(left[1, :, at], right[1, :, to], 0, 0)
                term[a, plane, :, to] = part.astype(bf16)
            return carry

        lax.fori_loop(0, 4, one, 0)

    def attn_term(a):
        for m in range(4):
            left = gh if m < 3 else att
            right = normed if m < 3 else up_low
            at = slice(m * 256, m * 256 + 256) if m < 3 else slice(0, 256)
            for b in range(spot.blocks):
                to = slice(b * span, b * span + span)
                part = dot(left[0, :, at], right[0, :, to], 0, 0) + dot(left[1, :, at], right[1, :, to], 0, 0)
                term[a, :, m * HD : m * HD + HD, to] = part.astype(bf16).reshape(4, HD, span)

    def one_layer(step_index, carry):
        l = top - step_index
        again = l < top
        more = l > 0
        n = 3 * step_index

        def mlp_image(i, carry):
            mlp_stage(l, i, n)

            @pl.when(jnp.logical_and(again, i == 0))
            def _():
                scatter.sum_blocks(n - 2)
                scatter.hop(n - 3, 1)

            return carry

        lax.fori_loop(0, 2, mlp_image, 0)

        @pl.when(l == top)
        def _():
            last_copy.wait_recv()
            load_stream = load(stream_in.at[spot.image], big.at[:, 0:D], 11)
            load_stream.start()

            v = last_chip[spot.image].astype(f32) + last_in[...].astype(f32)
            result[:, exchange.mine] = v.astype(bf16)
            load_stream.wait()

            @pl.when(jnp.logical_not(owner))
            def _():
                half_copy.start()
                half_copy.wait_send()

            @pl.when(owner)
            def _():
                half_in.wait_recv()

                for start in range(0, rows, 128):
                    r = slice(start, min(rows, start + 128))
                    v = big[r, 0:D] + result[r].astype(f32) + vec[top, 5:6]
                    result[r] = v.astype(bf16)

            last_copy.wait_send()
            for copy in load_attn(top):
                copy.start()
            return_begin(out_pair)

        @pl.when(again)
        def _():
            for copy in load_unit(l, 1):
                copy.start()

        load_normed(l, 1).wait()

        @pl.when(again)
        def _():
            scatter.hop(n - 3, 2)
            scatter.sum_blocks(n - 1)
            scatter.hop(n - 2, 1)

        scatter.before_terms(n + 1)
        unit_term(scatter.slot(n + 1), gh, normed)
        scatter.send_terms(n + 1)

        @pl.when(more)
        def _():
            below = jnp.maximum(l - 1, 0)
            load_hidden(below).start()
            load_weight(below, 1).start()
            load_weight(below, 2).start()

        load_normed(l, 0).start()

        @pl.when(again)
        def _():
            scatter.hop(n - 3, 3)
            scatter.hand_out(n - 3)

        def attn_image(i, carry):
            attn_stage(l, i)

            @pl.when(jnp.logical_and(again, i == 0))
            def _():
                scatter.hop(n - 2, 2)
                scatter.hop(n - 1, 1)

            return carry

        lax.fori_loop(0, 2, attn_image, 0)
        for copy in load_unit(l, 0):
            copy.start()
        load_normed(l, 0).wait()

        @pl.when(again)
        def _():
            scatter.hop(n - 2, 3)
            scatter.hand_out(n - 2)
            scatter.hop(n - 1, 2)

        scatter.sum_blocks(n)
        scatter.before_terms(n + 2)
        attn_term(scatter.slot(n + 2))

        @pl.when(more)
        def _():
            scatter.send_terms(n + 2)

        @pl.when(jnp.logical_not(more))
        def _():
            scatter.send_terms(3 * LAYERS - 1, (0, 1))

        @pl.when(more)
        def _():
            below = jnp.maximum(l - 1, 0)
            load_weight(below, 0).start()
            load_normed(below, 1).start()
            for copy in load_attn(below):
                copy.start()

        for copy in load_unit(l, 0):
            copy.wait()
        return carry

    lax.fori_loop(0, LAYERS, one_layer, 0)

    end = 3 * LAYERS
    def last_image(i, carry):
        exchange.finish(i, 1)
        norm_back(0, 0, i)

        @pl.when(i == spot.image)
        def _():
            line_begin()

        return carry

    lax.fori_loop(0, 2, last_image, 0)
    picks = normed.at[0]
    unit_picks(picks, fsdp, spot.role)
    for l in range(LAYERS):
        features = [jnp.sum(sums[(l + 1) * 6 + n], axis=0, keepdims=True) for n in range(6)]
        inner = jnp.sum(unit_sums[l, 0], axis=0, keepdims=True)
        qkv_sums = jnp.sum(unit_sums[l, 1], axis=0, keepdims=True)
        for plane in range(4):
            parts = [
                inner[:, plane * 256 : plane * 256 + 256],
                qkv_sums[:, plane * HD : plane * HD + HD],
                qkv_sums[:, 512 + plane * HD : 512 + plane * HD + HD],
            ]
            values = jnp.broadcast_to(jnp.concatenate(parts, axis=1), (16, 384)).astype(bf16)
            row = dot(values[:, 0:256], picks[0:256], 1, 0)[0:1]
            other_row = dot(values[:, 256:384], picks[256:384], 1, 0)[0:1]
            block = jnp.concatenate(features + [row, other_row, jnp.zeros((8, D), f32)], axis=0)
            small_term[0, plane, 16 * l : 16 * l + 16] = block.astype(bf16)
    small.send_terms(0)
    scatter.hop(end - 3, 1)
    scatter.hop(end - 4, 3)
    scatter.hand_out(end - 4)
    scatter.sum_blocks(end - 2)
    line_relay(0)
    scatter.hop(end - 3, 2)
    scatter.sum_blocks(end - 1, 0)
    line_relay(1)
    small.sum_blocks(0)
    scatter.hop(end - 2, 1)
    scatter.sum_blocks(end - 1, 1)
    scatter.hop(end - 1, 1, 0)
    line_relay(2)
    small.hop(0, 1)
    scatter.hop(end - 3, 3)
    scatter.hand_out(end - 3)
    scatter.hop(end - 1, 1, 1)
    scatter.hop(end - 2, 2)
    scatter.hop(end - 1, 2, 0)
    line_relay(3)
    small.hop(0, 2)
    scatter.hop(end - 1, 2, 1)
    scatter.hop(end - 2, 3)
    scatter.hand_out(end - 2)
    scatter.hop(end - 1, 3, 0)
    scatter.hand_out(end - 1, 0)
    small.hop(0, 3)
    small.hand_out(0)
    scatter.hop(end - 1, 3, 1)
    scatter.hand_out(end - 1, 1)
    scatter.finish((0, 1))
    small.finish()
    return_end(out_pair)
    line_end()


def backward_call(fsdp, head, tokens, rows, direct, kept):
    groups = 3 * LAYERS
    blocks = fsdp // TP
    span = D // blocks
    cols = span // TP
    anyspace = pl.BlockSpec(memory_space=pl.ANY)
    shape = jax.ShapeDtypeStruct
    dma, plain = pltpu.SemaphoreType.DMA, pltpu.SemaphoreType.REGULAR
    out_shape = (
        shape((2, rows, D), bf16),
        shape((2, rows, D), bf16),
        shape((groups, TP, 256, cols) if direct else (groups, 256, span), bf16),
        shape((1, TP, 32, cols) if direct else (1, 32, span), bf16),
    )
    scratch = [
        pltpu.VMEM((3, 4, 4, HD, D), bf16),
        pltpu.VMEM((LAYERS, 8, D), f32),
        pltpu.VMEM((2, rows, D), f32),
        pltpu.VMEM((2, rows, D), bf16),
        pltpu.VMEM((2, rows, D), bf16),
        pltpu.VMEM((2, rows, D), bf16),
        pltpu.VMEM((2, rows, D), bf16),
        pltpu.VMEM((2, rows, D), bf16),
        pltpu.VMEM((2, rows, 128), f32),
        pltpu.VMEM((2, rows, 768), bf16),
        pltpu.VMEM((2, rows, 256), bf16),
        pltpu.VMEM((2, 8, rows), f32),
        pltpu.VMEM((rows, D), f32),
        pltpu.VMEM((768, rows), bf16),
        pltpu.VMEM((768, rows), bf16),
        pltpu.VMEM((rows, 256), bf16),
        pltpu.VMEM((16, rows), f32),
        pltpu.VMEM((2, rows, HALF), bf16),
        pltpu.VMEM((2, rows, HALF), bf16),
        pltpu.VMEM((2, rows, HALF), bf16),
        pltpu.VMEM((2, 2, rows, HALF), bf16),
        pltpu.VMEM((2, rows, D), bf16),
        pltpu.VMEM((rows, HALF), bf16),
        pltpu.VMEM((rows, D), bf16),
        pltpu.VMEM((6 * (LAYERS + 1), 8, D), f32),
        pltpu.VMEM((LAYERS, 2, 8, D), f32),
    ]
    for slots, thirds, units in ((2, 3, 256), (1, 1, 32)):
        scratch += [
            pltpu.VMEM((slots, 4, units, D), bf16),
            pltpu.VMEM((slots, blocks - 1, 4, units, span), bf16),
            pltpu.VMEM((thirds, 4, units, span), bf16),
            pltpu.VMEM((slots, 2, 3, units, span), bf16),
            pltpu.VMEM((slots, units, span), bf16),
        ]
    scratch += [dma((2,)), dma((2,)), dma((2, 2)), dma((2, 2)), dma((2,)), dma((2,))]
    for slots, thirds, count in ((2, 3, groups), (1, 1, 1)):
        scratch += [
            dma((slots, blocks - 1, 2)), dma((slots, blocks - 1, 2)),
            dma((thirds, 2, 2)), dma((thirds, 2, 2)),
            dma((count, 4, 2)), dma((count, 4, 2)),
            dma((count, 2)),
            plain((slots, blocks - 1)), plain((slots, 2)),
        ]
    scratch += [dma((2,)), dma((2,)), dma((4,)), dma((4,)), dma((2, 4, 2)), dma((2, 4)), dma((16,)), dma((3,))]
    return pl.pallas_call(
        functools.partial(backward_kernel, (fsdp, head, tokens, rows, direct)),
        out_shape=out_shape,
        in_specs=[anyspace] * len(kept),
        out_specs=tuple(anyspace for _ in out_shape),
        scratch_shapes=scratch,
        compiler_params=pltpu.CompilerParams(
            collective_id=1, has_side_effects=True, vmem_limit_bytes=63 << 20
        ),
        name="backward_layers",
    )(*kept)


class Places:
    def __init__(self, fsdp, head):
        self.fsdp, self.head = fsdp, head
        self.blocks = fsdp // TP
        index, plane = lax.axis_index("fsdp"), lax.axis_index("head")
        self.block, self.role, self.plane = index // TP, index % TP, plane

    def pairs(self, move, sends=None):
        found = []
        for block in range(self.blocks):
            for role in range(TP):
                for plane in range(self.head):
                    if sends is not None and not sends(block, role, plane):
                        continue
                    to_block, to_role, to_plane = move(block, role, plane)
                    found.append(
                        (
                            (block * TP + role) * self.head + plane,
                            (to_block * TP + to_role) * self.head + to_plane,
                        )
                    )
        return found

    def role_xor(self, v, bits, sends=None):
        return lax.ppermute(v, AXES, self.pairs(lambda b, r, p: (b, r ^ bits, p), sends))


def by_xor(parts, index):
    a, b, c, d = parts
    odd = (index & 1) == 1
    a, b = jnp.where(odd, b, a), jnp.where(odd, a, b)
    c, d = jnp.where(odd, d, c), jnp.where(odd, c, d)
    top = (index & 2) == 2
    return [jnp.where(top, c, a), jnp.where(top, d, b), jnp.where(top, a, c), jnp.where(top, b, d)]


def pack_inputs(pl, w_qkv, w_out, w_in, w_down, qv_bias, in_bias, gains, shifts):
    cols = w_qkv.shape[2]
    attn = jnp.concatenate([w_qkv.transpose(0, 1, 3, 2), w_out[:, None]], axis=1).reshape(LAYERS, 4, TP, HD, cols)
    inner = w_in.transpose(0, 2, 1).reshape(LAYERS, TP, 4, HD, cols)
    down = w_down.reshape(LAYERS, TP, 4, HD, cols)
    qv = qv_bias.reshape(LAYERS, 1, -1)
    small = jnp.concatenate(
        [
            gains, shifts, in_bias.reshape(LAYERS, 1, cols),
            jnp.pad(qv, ((0, 0), (0, 0), (0, cols - qv.shape[2]))),
            jnp.zeros((LAYERS, 8, cols), bf16),
        ],
        axis=1,
    ).reshape(1, 16 * LAYERS, cols)
    if cols % 128 == 0:
        return attn, inner, down, small, True
    attn = gather_roles(pl, attn.transpose(0, 2, 1, 3, 4).reshape(LAYERS, TP, 256, cols))
    inner, down = [gather_roles(pl, v.reshape(LAYERS, TP, 256, cols)) for v in (inner, down)]
    small = gather_roles(pl, jnp.broadcast_to(small[:, None], (1, TP) + small.shape[1:]))
    attn, inner, down = [v.reshape(LAYERS, 4, HD, TP * cols) for v in (attn, inner, down)]
    return attn, inner, down, small, False


def gather_roles(pl, pack):
    exchanged = [lax.dynamic_index_in_dim(pack, pl.role, 1, False)]
    for bits in (1, 2, 3):
        exchanged.append(pl.role_xor(lax.dynamic_index_in_dim(pack, pl.role ^ bits, 1, False), bits))
    return jnp.concatenate(by_xor(exchanged, pl.role), axis=-1)


def scatter_roles(pl, mine):
    groups, units, width = mine.shape
    mine = mine.reshape(groups, units, TP, width // TP)
    exchanged = [lax.dynamic_index_in_dim(mine, pl.role, 2, False)]
    for bits in (1, 2, 3):
        exchanged.append(pl.role_xor(lax.dynamic_index_in_dim(mine, pl.role ^ bits, 2, False), bits))
    return jnp.stack(by_xor(exchanged, pl.role), axis=1)


def body(images, cotangent, w_qkv, w_out, w_in, w_down, qv_bias, in_bias, gains, shifts):
    fsdp, head = lax.axis_size("fsdp"), lax.axis_size("head")
    places = Places(fsdp, head)
    cols = w_qkv.shape[2]
    per = HD // fsdp
    tokens = images.shape[1]
    rows = -(-tokens // 16) * 16
    attn, inner, down, extras, direct = pack_inputs(
        places, w_qkv, w_out, w_in, w_down, qv_bias, in_bias, gains, shifts
    )
    edge = tokens // 16 * 16
    pad = ((0, 0), (0, rows - tokens), (0, 0))
    image_rest, cot_rest = [jnp.pad(v[:, edge:], pad) for v in (images, cotangent)]
    kept = forward_call(
        fsdp, head, tokens, rows, direct,
        images, image_rest, cotangent, cot_rest, attn, inner, down, extras,
    )
    block_out, input_grad, grads, small = backward_call(fsdp, head, tokens, rows, direct, kept)
    if not direct:
        grads, small = scatter_roles(places, grads), scatter_roles(places, small)
    grads = grads.astype(f32).reshape(LAYERS, 3, TP, 256, cols)
    attn = grads[:, 0].reshape(LAYERS, TP, 4, HD, cols).transpose(0, 2, 1, 3, 4).reshape(LAYERS, 4, TP * HD, cols)
    small = small.astype(f32).reshape(TP, LAYERS, 16, cols)
    features = small[0, :, 0:6]
    units = jnp.sum(small[:, :, 6:8], axis=0)
    qv = units[:, 1, 0 : 2 * TP * per].reshape(LAYERS, 2, TP * per, 1)
    inner = units[:, 0].reshape(LAYERS, cols, 1)
    return (
        lax.optimization_barrier(block_out[:, :tokens]).astype(f32),
        lax.optimization_barrier(input_grad[:, :tokens]).astype(f32),
        attn[:, :3].transpose(0, 1, 3, 2),
        attn[:, 3],
        grads[:, 1].reshape(LAYERS, TP * 256, cols).transpose(0, 2, 1),
        grads[:, 2].reshape(LAYERS, TP * 256, cols),
        qv,
        inner,
        features[:, 0:2],
        features[:, 2:6],
    )


def solution(mesh):
    placed = (
        P("fsdp", None, None),
        P("fsdp", None, None),
        P(None, None, "fsdp", "head"),
        P(None, "head", "fsdp"),
        P(None, "fsdp", "head"),
        P(None, "head", "fsdp"),
        P(None, None, "head", "fsdp"),
        P(None, "head", "fsdp"),
        P(None, None, "fsdp"),
        P(None, None, "fsdp"),
    )
    return jax.shard_map(
        body, mesh=mesh, in_specs=placed, out_specs=placed, check_vma=False
    )
```
